512 devices in a mesh: beam: 128 (over x, y, z_lo), slab: 4 (over z_hi, core).
Axes of the slice: x: 4, y: 8, z: 8 (z_hi: 2, z_lo: 4; z = z_hi * 4 + z_lo), core: 2. Of those that a mesh axis runs over, the one named last changes fastest.
Arguments:
- potential: float32 [4, 3, 65536], P('slab', None, 'beam'), may hold values from 0 to 3
- tilts: int32 [128, 2], replicated, may hold values from -32 to 31
- aperture: int32 [128], replicated, may hold values 0 or 1
- positions: int32 [512, 2], replicated, may hold values from 0 to 127
Outputs:
- intensity: float32 [512, 16384], P('slab', 'beam')
The draws below stay inside these ranges and needn't reach their ends.
All inputs are finite; a program needn't handle non-finite values.
Results may differ from the reference program's by a relative error of at most 0.00016.
Values sent between devices are 32-bit elements; how exact they have to be, the bound alone decides.
No kernel may reach another device: no remote copies, remote signals or barrier semaphores. Data moves between devices by JAX's collectives and lax.ppermute only.
A program may use at most 64 MiB of HBM per device.

```python
import math
import jax
import jax.numpy as jnp
from jax import lax

G = 256
K = 128
SLICES = 3
PROBES = 512
BEAMS = 128
CONFIGS = 4


def plant(array, own_key, low, top_value):
    dims = array.shape
    place = [jax.random.randint(jax.random.fold_in(own_key, axis), (), 0, dims[axis]) for axis in range(len(dims))]
    array = array.at[tuple(place)].set(low)
    longest = dims.index(max(dims))
    place[longest] = (place[longest] + 1) % dims[longest]
    return array.at[tuple(place)].set(top_value)


def shard_levels(stream_key, extent, split, low, high):
    gain = 1.0
    for axis_at, parts in split:
        heights = jax.random.uniform(jax.random.fold_in(jax.random.fold_in(stream_key, 6), axis_at), (parts,), jnp.float32, low / len(split), high / len(split))
        gain = gain * jnp.repeat(jnp.exp(heights), extent[axis_at] // parts).reshape((-1,) + (1,) * (len(extent) - 1 - axis_at))
    return gain


def setup_inputs(seed: int = 0) -> dict:
    key_list = jax.random.split(jax.random.key(seed), 5)
    potential = jnp.clip(3.0 * jax.random.uniform(key_list[0], (CONFIGS, SLICES, G * G), jnp.float32) ** shard_levels(key_list[0], (CONFIGS, SLICES, G * G), ((0, 4), (2, 128)), -0.2, 0.2), 0.0, 3.0)
    tilts = plant(jax.random.randint(key_list[1], (BEAMS, 2), 0 - K // 4, K // 4), jax.random.fold_in(key_list[1], 1), 0 - K // 4, (K // 4) - 1).astype(jnp.int32)
    aperture = plant((jax.random.randint(key_list[2], (BEAMS,), 0, 4) < 3).astype(jnp.int32), jax.random.fold_in(key_list[2], 1), 0, 1)
    positions = plant(jax.random.randint(key_list[3], (PROBES, 2), 0, K), jax.random.fold_in(key_list[3], 1), 0, K - 1).astype(jnp.int32)
    return dict(potential=potential, tilts=tilts, aperture=aperture, positions=positions)


def reference(potential, tilts, aperture, positions):
    points = jnp.arange(G, dtype=jnp.int32)
    tilt_x = tilts[:, 0]
    tilt_y = tilts[:, 1]
    index = (tilt_x[:, None, None] * points[None, :, None] + tilt_y[:, None, None] * points[None, None, :]) % G
    angle = 2.0 * math.pi / G * index.astype(jnp.float32)
    start_wave = lax.complex(jnp.cos(angle), jnp.sin(angle))
    freqs = jnp.where(points < G // 2, points, points - G)
    square = freqs[:, None] ** 2 + freqs[None, :] ** 2
    keep = (square <= (G // 3) ** 2).astype(jnp.float32)
    kernel_angle = -0.00019 * square.astype(jnp.float32)
    kernel = lax.complex(jnp.cos(kernel_angle) * keep, jnp.sin(kernel_angle) * keep)
    band = jnp.arange(K, dtype=jnp.int32)
    picks = jnp.where(band < K // 2, band, band - K + G)
    probe_index = (positions[:, 0:1] * tilt_x[None, :] + positions[:, 1:2] * tilt_y[None, :]) % K
    beam_square = tilt_x ** 2 + tilt_y ** 2
    probe_angle = -(2.0 * math.pi / K) * probe_index.astype(jnp.float32) - 0.01 * beam_square.astype(jnp.float32)[None, :]
    weight = aperture.astype(jnp.float32)[None, :] / math.sqrt(BEAMS)
    coef = lax.complex(jnp.cos(probe_angle) * weight, jnp.sin(probe_angle) * weight)
    total = jnp.zeros((PROBES, K * K), jnp.float32)
    for config in range(CONFIGS):
        wave = start_wave
        spectrum = start_wave
        for layer in range(SLICES):
            phase = potential[config, layer].reshape(G, G)
            wave = wave * lax.complex(jnp.cos(phase), jnp.sin(phase))
            spectrum = jnp.fft.fft2(wave) * kernel
            if layer < SLICES - 1:
                wave = jnp.fft.ifft2(spectrum)
        cropped = spectrum[:, picks][:, :, picks]
        smatrix = (jnp.fft.ifft2(cropped) * (K * K / (G * G))).reshape(BEAMS, K * K)
        waves = jnp.dot(coef, smatrix, precision=lax.Precision.HIGHEST)
        total = total + jnp.real(waves) ** 2 + jnp.imag(waves) ** 2
    return total / CONFIGS
```

```python
import math

import jax
import jax.numpy as jnp
import ml_dtypes
import numpy as np
from jax import lax
from jax.experimental import pallas as pl
from jax.experimental.pallas import tpu as pltpu
from jax.sharding import PartitionSpec as P

G = 256
K = 128
SLICES = 3
LIMIT = (G // 3) ** 2
REACH = G // 3
ROWS = 176

FRESNEL_RATE = 0.00019
DEFOCUS_RATE = 0.01

F32 = jnp.float32
BF16 = jnp.bfloat16


def split_table(table):
    high = table.astype(ml_dtypes.bfloat16)
    low = (table - high.astype(np.float64)).astype(ml_dtypes.bfloat16)
    return high, low


def waves_of(freqs, points, length, sign):
    return np.exp(sign * 2j * math.pi / length * ((freqs[:, None] * points[None, :]) % length))


def left_form(table):
    return np.block([[table.real, -table.imag], [table.imag, table.real]])


def right_form(table):
    return np.concatenate([table.real, table.imag], axis=1)


def tables():
    xs = np.concatenate([np.arange(0, G, 2), np.arange(1, G, 2)])
    ys = np.arange(G)
    us = np.arange(-REACH, REACH + 1)
    vs = np.where(ys < G // 2, ys, ys - G)
    chirp_u = np.exp(-1j * FRESNEL_RATE * us.astype(np.float64) ** 2)
    chirp_v = np.exp(-1j * FRESNEL_RATE * vs.astype(np.float64) ** 2)
    inside = np.abs(vs) <= REACH
    ahead_left = np.zeros((ROWS, G), np.complex128)
    ahead_left[: len(us)] = chirp_u[:, None] * waves_of(us, xs, G, -1) / G
    ahead_right = waves_of(ys, vs, G, -1) * (chirp_v * inside)[None, :] / G
    back_right = waves_of(vs, ys, G, 1) * inside[:, None]
    back_left = np.zeros((G, ROWS), np.complex128)
    back_left[:, : len(us)] = waves_of(xs, us, G, 1)
    band = np.arange(K)
    band_freq = np.where(band < K // 2, band, band - K)
    chirp_b = np.exp(-1j * FRESNEL_RATE * band_freq.astype(np.float64) ** 2)
    crop_left = chirp_b[:, None] * waves_of(band_freq, xs, G, -1) / G
    crop_right = waves_of(ys, band_freq, G, -1) * chirp_b[None, :] / G
    image = waves_of(band, band, K, 1)
    last = left_form(image).reshape(2, K, 2 * K).transpose(1, 0, 2).reshape(2 * K, 2 * K)
    out = []
    for table in (
        left_form(ahead_left),
        right_form(ahead_right),
        right_form(back_right),
        left_form(back_left),
        left_form(crop_left),
        right_form(crop_right),
        right_form(image),
        last,
    ):
        out.extend(split_table(table))
    return out


def split(value):
    high = value.astype(BF16)
    return high, (value - high.astype(F32)).astype(BF16)


def from_left(high_ref, low_ref, field):
    high, low = split(field)
    table = high_ref[...]
    return jnp.dot(
        jnp.concatenate([table, table, low_ref[...]], axis=1),
        jnp.concatenate([high, low, high], axis=0),
        preferred_element_type=F32,
    )


def from_right(field, high_ref, low_ref):
    high, low = split(field)
    table = high_ref[...]
    product = jnp.dot(
        jnp.concatenate([high, low, high], axis=1),
        jnp.concatenate([table, table, low_ref[...]], axis=0),
        preferred_element_type=F32,
    )
    m, n = product.shape[0] // 2, product.shape[1] // 2
    return product[:m, :n] - product[m:, n:], product[:m, n:] + product[m:, :n]


def sine_cosine(t):
    s = t * t
    sine = jnp.full_like(t, -2.5052108e-8)
    for term in (2.7557319e-6, -1.9841270e-4, 8.3333333e-3, -1.6666667e-1, 1.0):
        sine = sine * s + term
    cosine = jnp.full_like(t, 2.0876757e-9)
    for term in (-2.7557319e-7, 2.4801587e-5, -1.3888889e-3, 4.1666667e-2, -0.5, 1.0):
        cosine = cosine * s + term
    return sine * t, cosine


def circle(steps, length):
    near = ((steps + length // 2) & (length - 1)) - length // 2
    sine, cosine = sine_cosine(near.astype(F32) * (math.pi / length))
    return 2.0 * sine * cosine, 1.0 - 2.0 * sine * sine


def prepare_kernel(tilt_ref, places_ref, tilts_ref, weight_ref, start_ref, high_ref, low_ref):
    rows = lax.broadcasted_iota(jnp.int32, (G, G), 0)
    x = jnp.where(rows < G // 2, 2 * rows, 2 * rows - (G - 1))
    y = lax.broadcasted_iota(jnp.int32, (G, G), 1)
    sine, cosine = circle(tilt_ref[0] * x + tilt_ref[1] * y, G)
    start_ref[:G, :] = cosine
    start_ref[G:, :] = sine
    probes = places_ref.shape[0]
    beams = tilts_ref.shape[1]
    steps = places_ref[:, 0:1] * tilts_ref[0:1, :] + places_ref[:, 1:2] * tilts_ref[1:2, :]
    sine, cosine = circle(-steps, K)
    weight_re, weight_im = weight_ref[0:1, :], weight_ref[1:2, :]
    real = cosine * weight_re - sine * weight_im
    imag = cosine * weight_im + sine * weight_re
    for rows, columns, part in (
        (0, 0, real),
        (0, beams, -imag),
        (probes, 0, imag),
        (probes, beams, real),
    ):
        high, low = split(part)
        high_ref[rows : rows + probes, columns : columns + beams] = high
        low_ref[rows : rows + probes, columns : columns + beams] = low


def transmission(potential_ref, layer):
    stride = 4 * SLICES
    count = G // 2

    def rows(parity):
        return jnp.concatenate(
            [
                potential_ref[pl.ds(4 * layer + 2 * parity + half, count, stride), :]
                for half in range(2)
            ],
            axis=1,
        )

    sine, cosine = sine_cosine(jnp.concatenate([rows(0), rows(1)], axis=0) - 1.5)
    cos_mid, sin_mid = math.cos(1.5), math.sin(1.5)
    return cosine * cos_mid - sine * sin_mid, sine * cos_mid + cosine * sin_mid


def propagate_kernel(potential_ref, start_ref, *refs):
    ahead_left, ahead_right, back_right, back_left = (refs[2 * i : 2 * i + 2] for i in range(4))
    crop_left, crop_right, image_right, image_left = (refs[2 * i : 2 * i + 2] for i in range(4, 8))
    out_ref = refs[16]
    u = lax.broadcasted_iota(jnp.int32, (ROWS, G), 0) - REACH
    v = lax.broadcasted_iota(jnp.int32, (ROWS, G), 1)
    v = jnp.where(v < G // 2, v, v - G)
    keep = u * u + v * v <= LIMIT
    real, imag = start_ref[:G, :], start_ref[G:, :]
    for layer in range(SLICES):
        cosine, sine = transmission(potential_ref, layer)
        real, imag = real * cosine - imag * sine, real * sine + imag * cosine
        field = jnp.concatenate([real, imag], axis=0)
        if layer < SLICES - 1:
            real, imag = from_right(from_left(*ahead_left, field), *ahead_right)
            field = jnp.concatenate([jnp.where(keep, real, 0.0), jnp.where(keep, imag, 0.0)], axis=0)
            real, imag = from_right(field, *back_right)
            field = from_left(*back_left, jnp.concatenate([real, imag], axis=0))
            real, imag = field[:G], field[G:]
        else:
            real, imag = from_right(from_left(*crop_left, field), *crop_right)
            u = lax.broadcasted_iota(jnp.int32, (K, K), 0)
            v = lax.broadcasted_iota(jnp.int32, (K, K), 1)
            u = jnp.where(u < K // 2, u, u - K)
            v = jnp.where(v < K // 2, v, v - K)
            keep = u * u + v * v <= LIMIT
            field = jnp.concatenate([jnp.where(keep, real, 0.0), jnp.where(keep, imag, 0.0)], axis=0)
            real, imag = from_right(field, *image_right)
            out_ref[...] = from_left(*image_left, jnp.concatenate([real, imag], axis=0))


def probe_kernel(block_ref, high_ref, low_ref, *out_refs):
    beams = block_ref.shape[0] // 2
    field = jnp.concatenate(
        [block_ref[pl.ds(part, beams, 2), :] for part in range(2)], axis=0
    )
    waves = from_left(high_ref, low_ref, field)
    probes = waves.shape[0] // 2
    real, imag = waves[:probes], waves[probes:]
    total = (real * real + imag * imag) * (1.0 / len(out_refs))
    quarter = probes // len(out_refs)
    for i, out_ref in enumerate(out_refs):
        out_ref[...] = total[i * quarter : (i + 1) * quarter]


VMEM = pl.BlockSpec(memory_space=pltpu.VMEM)
SMEM = pl.BlockSpec(memory_space=pltpu.SMEM)
PARAMS = pltpu.CompilerParams(vmem_limit_bytes=24 * 1024 * 1024)


def per_device(sizes, potential, tilts, aperture, positions):
    nx, ny, nz = sizes
    devices = lax.axis_size("beam")
    configs = lax.axis_size("slab")
    beams = tilts.shape[0]
    probes = positions.shape[0]
    quarter = probes // configs
    own = lax.axis_index("beam")
    slab = lax.axis_index("slab")

    piece = potential.reshape(SLICES * G * G // devices // K, K)
    near = [[x * ny * nz + i for i in range(ny * nz)] for x in range(nx)]
    far = [[x * ny * nz + i for x in range(nx)] for i in range(ny * nz)]
    part = lax.all_to_all(
        jnp.broadcast_to(piece[None], (ny * nz, *piece.shape)), "beam", 0, 0, axis_index_groups=near
    )
    part = part.reshape(ny * nz * piece.shape[0], K)
    whole = lax.all_to_all(
        jnp.broadcast_to(part[None], (nx, *part.shape)), "beam", 0, 0, axis_index_groups=far
    ).reshape(devices * piece.shape[0], K)

    order = jnp.bitwise_xor(slab, jnp.arange(configs, dtype=jnp.int32))
    places = positions.reshape(configs, quarter, 2)[order].reshape(probes, 2)
    square = (tilts[:, 0] ** 2 + tilts[:, 1] ** 2).astype(F32)
    amount = aperture.astype(F32) * (1.0 / math.sqrt(beams))
    weight = jnp.stack([jnp.cos(DEFOCUS_RATE * square) * amount, -jnp.sin(DEFOCUS_RATE * square) * amount])
    tilt = lax.dynamic_index_in_dim(tilts, own, 0, keepdims=False)
    start, coef_high, coef_low = pl.pallas_call(
        prepare_kernel,
        out_shape=(
            jax.ShapeDtypeStruct((2 * G, G), F32),
            jax.ShapeDtypeStruct((2 * probes, 2 * beams), BF16),
            jax.ShapeDtypeStruct((2 * probes, 2 * beams), BF16),
        ),
        in_specs=[SMEM, VMEM, VMEM, VMEM],
        out_specs=(VMEM, VMEM, VMEM),
        compiler_params=PARAMS,
        name="prepare",
    )(tilt, places, tilts.T, weight)

    constants = [jnp.asarray(table) for table in tables()]
    image = pl.pallas_call(
        propagate_kernel,
        out_shape=jax.ShapeDtypeStruct((2 * K, K), F32),
        in_specs=[VMEM] * (2 + len(constants)),
        out_specs=VMEM,
        compiler_params=PARAMS,
        name="propagate",
    )(whole, start, *constants)

    block = lax.all_to_all(image.reshape(K, 2, K), "beam", 0, 0).reshape(2 * beams, K)
    parts = pl.pallas_call(
        probe_kernel,
        out_shape=[jax.ShapeDtypeStruct((quarter, K), F32)] * configs,
        in_specs=[VMEM] * 3,
        out_specs=[VMEM] * configs,
        compiler_params=PARAMS,
        name="probe",
    )(block, coef_high, coef_low)

    def swap(value, bit):
        return lax.ppermute(value, "slab", [(i, i ^ bit) for i in range(configs)])

    got = swap(jnp.concatenate([parts[1], parts[3]], axis=0), 1)
    other = parts[2] + got[quarter:]
    return parts[0] + got[:quarter] + swap(other, 2)


def solution(mesh):
    def step(*args):
        return per_device((4, 8, 4), *args)

    return jax.shard_map(
        step,
        mesh=mesh,
        in_specs=(P("slab", None, "beam"), P(), P(), P()),
        out_specs=P("slab", "beam"),
        check_vma=False,
    )
```

```python
import functools
import math

import jax
import jax.numpy as jnp
import ml_dtypes
import numpy as np
from jax import lax
from jax.experimental import pallas as pl
from jax.experimental.pallas import tpu as pltpu
from jax.sharding import PartitionSpec as P

G = 256
K = 128
SLICES = 3
LIMIT = (G // 3) ** 2
REACH = G // 3
ROWS = 176

WIDTH = 2 * G
TABLES = (
    (2 * ROWS, 2 * G),
    (G, 2 * G),
    (G, 2 * G),
    (2 * G, 2 * ROWS),
    (2 * K, 2 * G),
    (G, 2 * K),
    (K, 2 * K),
    (2 * K, 2 * K),
)

FRESNEL_RATE = 0.00019
DEFOCUS_RATE = 0.01

F32 = jnp.float32
BF16 = jnp.bfloat16


def split_table(table):
    high = table.astype(ml_dtypes.bfloat16)
    low = (table - high.astype(np.float64)).astype(ml_dtypes.bfloat16)
    return high, low


def waves_of(freqs, points, length, sign):
    return np.exp(sign * 2j * math.pi / length * ((freqs[:, None] * points[None, :]) % length))


def left_form(table):
    return np.block([[table.real, -table.imag], [table.imag, table.real]])


def right_form(table):
    return np.concatenate([table.real, table.imag], axis=1)


def tables():
    xs = np.concatenate([np.arange(0, G, 2), np.arange(1, G, 2)])
    ys = np.arange(G)
    us = np.arange(-REACH, REACH + 1)
    vs = np.where(ys < G // 2, ys, ys - G)
    chirp_u = np.exp(-1j * FRESNEL_RATE * us.astype(np.float64) ** 2)
    chirp_v = np.exp(-1j * FRESNEL_RATE * vs.astype(np.float64) ** 2)
    inside = np.abs(vs) <= REACH
    ahead_left = np.zeros((ROWS, G), np.complex128)
    ahead_left[: len(us)] = chirp_u[:, None] * waves_of(us, xs, G, -1) / G
    ahead_right = waves_of(ys, vs, G, -1) * (chirp_v * inside)[None, :] / G
    back_right = waves_of(vs, ys, G, 1) * inside[:, None]
    back_left = np.zeros((G, ROWS), np.complex128)
    back_left[:, : len(us)] = waves_of(xs, us, G, 1)
    band = np.arange(K)
    band_freq = np.where(band < K // 2, band, band - K)
    chirp_b = np.exp(-1j * FRESNEL_RATE * band_freq.astype(np.float64) ** 2)
    crop_left = chirp_b[:, None] * waves_of(band_freq, xs, G, -1) / G
    crop_right = waves_of(ys, band_freq, G, -1) * chirp_b[None, :] / G
    image = waves_of(band, band, K, 1)
    last = left_form(image).reshape(2, K, 2 * K).transpose(1, 0, 2).reshape(2 * K, 2 * K)
    out = []
    for table in (
        left_form(ahead_left),
        right_form(ahead_right),
        right_form(back_right),
        left_form(back_left),
        left_form(crop_left),
        right_form(crop_right),
        right_form(image),
        last,
    ):
        high, low = split_table(table)
        if table.shape[1] <= WIDTH // 2:
            rows = [np.concatenate([high, low], axis=1)]
        else:
            rows = [np.pad(term, ((0, 0), (0, WIDTH - table.shape[1]))) for term in (high, low)]
        out.append(np.concatenate(rows, axis=0))
    return np.concatenate(out, axis=0)


def table_of(ref, which):
    shapes = TABLES[:which]
    m, n = TABLES[which]
    at = sum(rows * (1 if columns <= WIDTH // 2 else 2) for rows, columns in shapes)
    if n <= WIDTH // 2:
        return ref[at : at + m, :n], ref[at : at + m, n : 2 * n]
    return ref[at : at + m, :n], ref[at + m : at + 2 * m, :n]


def split(value):
    high = value.astype(BF16)
    return high, (value - high.astype(F32)).astype(BF16)


def from_left(table, field):
    high, low = split(field)
    return jnp.dot(
        jnp.concatenate([table[0], table[0], table[1]], axis=1),
        jnp.concatenate([high, low, high], axis=0),
        preferred_element_type=F32,
    )


def from_right(field, table):
    high, low = split(field)
    product = jnp.dot(
        jnp.concatenate([high, low, high], axis=1),
        jnp.concatenate([table[0], table[0], table[1]], axis=0),
        preferred_element_type=F32,
    )
    m, n = product.shape[0] // 2, product.shape[1] // 2
    return product[:m, :n] - product[m:, n:], product[:m, n:] + product[m:, :n]


def sine_cosine(t):
    s = t * t
    sine = jnp.full_like(t, -2.5052108e-8)
    for term in (2.7557319e-6, -1.9841270e-4, 8.3333333e-3, -1.6666667e-1, 1.0):
        sine = sine * s + term
    cosine = jnp.full_like(t, 2.0876757e-9)
    for term in (-2.7557319e-7, 2.4801587e-5, -1.3888889e-3, 4.1666667e-2, -0.5, 1.0):
        cosine = cosine * s + term
    return sine * t, cosine


def circle(steps, length):
    near = ((steps + length // 2) & (length - 1)) - length // 2
    sine, cosine = sine_cosine(near.astype(F32) * (math.pi / length))
    return 2.0 * sine * cosine, 1.0 - 2.0 * sine * sine


def prepare_kernel(tilt_ref, places_ref, tilts_ref, weight_ref, start_ref, high_ref, low_ref):
    rows = lax.broadcasted_iota(jnp.int32, (G, G), 0)
    x = jnp.where(rows < G // 2, 2 * rows, 2 * rows - (G - 1))
    y = lax.broadcasted_iota(jnp.int32, (G, G), 1)
    sine, cosine = circle(tilt_ref[0] * (x + tilt_ref[2]) + tilt_ref[1] * y, G)
    start_ref[:G, :] = cosine
    start_ref[G:, :] = sine
    probes = places_ref.shape[0]
    beams = tilts_ref.shape[1]
    steps = places_ref[:, 0:1] * tilts_ref[0:1, :] + places_ref[:, 1:2] * tilts_ref[1:2, :]
    sine, cosine = circle(-steps, K)
    weight_re, weight_im = weight_ref[0:1, :], weight_ref[1:2, :]
    real = cosine * weight_re - sine * weight_im
    imag = cosine * weight_im + sine * weight_re
    for rows, columns, part in (
        (0, 0, real),
        (0, beams, -imag),
        (probes, 0, imag),
        (probes, beams, real),
    ):
        high, low = split(part)
        high_ref[rows : rows + probes, columns : columns + beams] = high
        low_ref[rows : rows + probes, columns : columns + beams] = low


def transmission(potential_refs, layer):
    stride = 4 * SLICES

    def rows(parity):
        return jnp.concatenate(
            [
                jnp.concatenate(
                    [
                        ref[pl.ds(4 * layer + 2 * parity + half, ref.shape[0] // stride, stride), :]
                        for half in range(2)
                    ],
                    axis=1,
                )
                for ref in potential_refs
            ],
            axis=0,
        )

    sine, cosine = sine_cosine(jnp.concatenate([rows(0), rows(1)], axis=0) - 1.5)
    cos_mid, sin_mid = math.cos(1.5), math.sin(1.5)
    return cosine * cos_mid - sine * sin_mid, sine * cos_mid + cosine * sin_mid


def masked(real, imag, first, limit_of):
    u = lax.broadcasted_iota(jnp.int32, real.shape, 0)
    v = lax.broadcasted_iota(jnp.int32, real.shape, 1)
    half = real.shape[1] // 2
    u = u - first if first else jnp.where(u < half, u, u - 2 * half)
    v = jnp.where(v < half, v, v - 2 * half)
    keep = u * u + v * v <= limit_of
    return jnp.concatenate([jnp.where(keep, real, 0.0), jnp.where(keep, imag, 0.0)], axis=0)


def propagate_kernel(turn_ref, table_ref, start_ref, *refs):
    potential_refs, out_ref = refs[:-1], refs[-1]
    blocks = len(potential_refs)
    table = functools.partial(table_of, table_ref)
    real, imag = start_ref[:G, :], start_ref[G:, :]
    for layer in range(SLICES):
        cosine, sine = transmission(potential_refs, layer)
        real, imag = real * cosine - imag * sine, real * sine + imag * cosine
        field = jnp.concatenate([real, imag], axis=0)
        if layer < SLICES - 1:
            field = from_left(table(0), field)
            field = masked(*from_right(field, table(1)), REACH, LIMIT)
            real, imag = from_right(field, table(2))
            field = from_left(table(3), jnp.concatenate([real, imag], axis=0))
            real, imag = field[:G], field[G:]
        else:
            field = from_left(table(4), field)
            field = masked(*from_right(field, table(5)), 0, LIMIT)
            real, imag = from_right(field, table(6))
            image = from_left(table(7), jnp.concatenate([real, imag], axis=0))
    rows = image.shape[0] // blocks
    for k in range(blocks):
        place = lax.rem(turn_ref[0] + k, blocks) * rows
        out_ref[pl.ds(pl.multiple_of(place, rows), rows), :] = image[k * rows : (k + 1) * rows]


def probe_kernel(block_ref, high_ref, low_ref, *out_refs):
    beams = block_ref.shape[0] // 2
    field = jnp.concatenate(
        [block_ref[pl.ds(part, beams, 2), :] for part in range(2)], axis=0
    )
    waves = from_left((high_ref[...], low_ref[...]), field)
    probes = waves.shape[0] // 2
    real, imag = waves[:probes], waves[probes:]
    total = (real * real + imag * imag) * (1.0 / len(out_refs))
    quarter = probes // len(out_refs)
    for i, out_ref in enumerate(out_refs):
        out_ref[...] = total[i * quarter : (i + 1) * quarter]


VMEM = pl.BlockSpec(memory_space=pltpu.VMEM)
SMEM = pl.BlockSpec(memory_space=pltpu.SMEM)
PARAMS = pltpu.CompilerParams(vmem_limit_bytes=24 * 1024 * 1024)


def per_device(sizes, potential, tilts, aperture, positions):
    nx, ny, nz = sizes
    devices = lax.axis_size("beam")
    configs = lax.axis_size("slab")
    beams = tilts.shape[0]
    probes = positions.shape[0]
    quarter = probes // configs
    own = lax.axis_index("beam")
    slab = lax.axis_index("slab")

    piece = potential.reshape(SLICES * G * G // devices // K, K)
    run = ny * nz
    near = [[x * run + i for i in range(run)] for x in range(nx)]
    part = lax.all_to_all(
        jnp.broadcast_to(piece[None], (run, *piece.shape)), "beam", 0, 0, axis_index_groups=near
    ).reshape(run * piece.shape[0], K)

    def fetch(k):
        return lax.ppermute(
            part, "beam", [((x + k) % nx * run + i, x * run + i) for x in range(nx) for i in range(run)]
        )

    blocks = [part] + [fetch(k) for k in range(1, nx)]

    order = jnp.bitwise_xor(slab, jnp.arange(configs, dtype=jnp.int32))
    places = positions.reshape(configs, quarter, 2)[order].reshape(probes, 2)
    square = (tilts[:, 0] ** 2 + tilts[:, 1] ** 2).astype(F32)
    amount = aperture.astype(F32) * (1.0 / math.sqrt(beams))
    weight = jnp.stack([jnp.cos(DEFOCUS_RATE * square) * amount, -jnp.sin(DEFOCUS_RATE * square) * amount])
    place = own // run
    turn = place.reshape(1)
    tilt = jnp.concatenate([lax.dynamic_index_in_dim(tilts, own, 0, keepdims=False), turn * (G // nx)])
    start, coef_high, coef_low = pl.pallas_call(
        prepare_kernel,
        out_shape=(
            jax.ShapeDtypeStruct((2 * G, G), F32),
            jax.ShapeDtypeStruct((2 * probes, 2 * beams), BF16),
            jax.ShapeDtypeStruct((2 * probes, 2 * beams), BF16),
        ),
        in_specs=[SMEM, VMEM, VMEM, VMEM],
        out_specs=(VMEM, VMEM, VMEM),
        compiler_params=PARAMS,
        name="prepare",
    )(tilt, places, tilts.T, weight)

    image = pl.pallas_call(
        propagate_kernel,
        out_shape=jax.ShapeDtypeStruct((2 * K, K), F32),
        in_specs=[SMEM] + [VMEM] * (2 + nx),
        out_specs=VMEM,
        compiler_params=PARAMS,
        name="propagate",
    )(turn, jnp.asarray(tables()), start, *blocks)

    block = lax.all_to_all(image.reshape(K, 2, K), "beam", 0, 0).reshape(2 * beams, K)
    parts = pl.pallas_call(
        probe_kernel,
        out_shape=[jax.ShapeDtypeStruct((quarter, K), F32)] * configs,
        in_specs=[VMEM] * 3,
        out_specs=[VMEM] * configs,
        compiler_params=PARAMS,
        name="probe",
    )(block, coef_high, coef_low)

    total = parts[0]
    for bit in (2, 3, 1):
        total = total + lax.ppermute(parts[bit], "slab", [(i, i ^ bit) for i in range(configs)])
    return total


def solution(mesh):
    def step(*args):
        return per_device((4, 8, 4), *args)

    return jax.shard_map(
        step,
        mesh=mesh,
        in_specs=(P("slab", None, "beam"), P(), P(), P()),
        out_specs=P("slab", "beam"),
        check_vma=False,
    )
```

```python
import functools
import math

import jax
import jax.numpy as jnp
import ml_dtypes
import numpy as np
from jax import lax
from jax.experimental import pallas as pl
from jax.experimental.pallas import tpu as pltpu
from jax.sharding import PartitionSpec as P

G = 256
K = 128
SLICES = 3
LIMIT = (G // 3) ** 2
REACH = G // 3
ROWS = 176

WIDTH = 2 * G
TABLES = (
    (2 * ROWS, 2 * G),
    (G, 2 * G),
    (G, 2 * G),
    (2 * G, 2 * ROWS),
    (2 * K, 2 * G),
    (G, 2 * K),
    (K, 2 * K),
    (2 * K, 2 * K),
)

FRESNEL_RATE = 0.00019
DEFOCUS_RATE = 0.01

F32 = jnp.float32
BF16 = jnp.bfloat16


def split_table(table):
    high = table.astype(ml_dtypes.bfloat16)
    low = (table - high.astype(np.float64)).astype(ml_dtypes.bfloat16)
    return high, low


def waves_of(freqs, points, length, sign):
    return np.exp(sign * 2j * math.pi / length * ((freqs[:, None] * points[None, :]) % length))


def left_form(table):
    return np.block([[table.real, -table.imag], [table.imag, table.real]])


def right_form(table):
    return np.concatenate([table.real, table.imag], axis=1)


def tables():
    xs = np.concatenate([np.arange(0, G, 2), np.arange(1, G, 2)])
    ys = np.arange(G)
    us = np.arange(-REACH, REACH + 1)
    vs = np.where(ys < G // 2, ys, ys - G)
    chirp_u = np.exp(-1j * FRESNEL_RATE * us.astype(np.float64) ** 2)
    chirp_v = np.exp(-1j * FRESNEL_RATE * vs.astype(np.float64) ** 2)
    inside = np.abs(vs) <= REACH
    ahead_left = np.zeros((ROWS, G), np.complex128)
    ahead_left[: len(us)] = chirp_u[:, None] * waves_of(us, xs, G, -1) / G
    ahead_right = waves_of(ys, vs, G, -1) * (chirp_v * inside)[None, :] / G
    back_right = waves_of(vs, ys, G, 1) * inside[:, None]
    back_left = np.zeros((G, ROWS), np.complex128)
    back_left[:, : len(us)] = waves_of(xs, us, G, 1)
    band = np.arange(K)
    band_freq = np.where(band < K // 2, band, band - K)
    chirp_b = np.exp(-1j * FRESNEL_RATE * band_freq.astype(np.float64) ** 2)
    crop_left = chirp_b[:, None] * waves_of(band_freq, xs, G, -1) / G
    crop_right = waves_of(ys, band_freq, G, -1) * chirp_b[None, :] / G
    image = waves_of(band, band, K, 1)
    last = left_form(image).reshape(2, K, 2 * K).transpose(1, 0, 2).reshape(2 * K, 2 * K)
    out = []
    for table in (
        left_form(ahead_left),
        right_form(ahead_right),
        right_form(back_right),
        left_form(back_left),
        left_form(crop_left),
        right_form(crop_right),
        right_form(image),
        last,
    ):
        high, low = split_table(table)
        if table.shape[1] <= WIDTH // 2:
            rows = [np.concatenate([high, low], axis=1)]
        else:
            rows = [np.pad(term, ((0, 0), (0, WIDTH - table.shape[1]))) for term in (high, low)]
        out.append(np.concatenate(rows, axis=0))
    return np.concatenate(out, axis=0)


def table_of(ref, which):
    shapes = TABLES[:which]
    m, n = TABLES[which]
    at = sum(rows * (1 if columns <= WIDTH // 2 else 2) for rows, columns in shapes)
    if n <= WIDTH // 2:
        return ref[at : at + m, :n], ref[at : at + m, n : 2 * n]
    return ref[at : at + m, :n], ref[at + m : at + 2 * m, :n]


def split(value):
    high = value.astype(BF16)
    return high, (value - high.astype(F32)).astype(BF16)


def from_left(table, field):
    high, low = split(field)
    return jnp.dot(
        jnp.concatenate([table[0], table[0], table[1]], axis=1),
        jnp.concatenate([high, low, high], axis=0),
        preferred_element_type=F32,
    )


def from_right(field, table):
    high, low = split(field)
    product = jnp.dot(
        jnp.concatenate([high, low, high], axis=1),
        jnp.concatenate([table[0], table[0], table[1]], axis=0),
        preferred_element_type=F32,
    )
    m, n = product.shape[0] // 2, product.shape[1] // 2
    return product[:m, :n] - product[m:, n:], product[:m, n:] + product[m:, :n]


def sine_cosine(t):
    s = t * t
    sine = jnp.full_like(t, -2.5052108e-8)
    for term in (2.7557319e-6, -1.9841270e-4, 8.3333333e-3, -1.6666667e-1, 1.0):
        sine = sine * s + term
    cosine = jnp.full_like(t, 2.0876757e-9)
    for term in (-2.7557319e-7, 2.4801587e-5, -1.3888889e-3, 4.1666667e-2, -0.5, 1.0):
        cosine = cosine * s + term
    return sine * t, cosine


def circle(steps, length):
    near = ((steps + length // 2) & (length - 1)) - length // 2
    sine, cosine = sine_cosine(near.astype(F32) * (math.pi / length))
    return 2.0 * sine * cosine, 1.0 - 2.0 * sine * sine


def prepare_kernel(tilt_ref, places_ref, tilts_ref, weight_ref, start_ref, high_ref, low_ref):
    rows = lax.broadcasted_iota(jnp.int32, (G, G), 0)
    x = jnp.where(rows < G // 2, 2 * rows, 2 * rows - (G - 1))
    y = lax.broadcasted_iota(jnp.int32, (G, G), 1)
    sine, cosine = circle(tilt_ref[0] * x + tilt_ref[1] * y, G)
    start_ref[:G, :] = cosine
    start_ref[G:, :] = sine
    probes = places_ref.shape[0]
    beams = tilts_ref.shape[1]
    steps = places_ref[:, 0:1] * tilts_ref[0:1, :] + places_ref[:, 1:2] * tilts_ref[1:2, :]
    sine, cosine = circle(-steps, K)
    weight_re, weight_im = weight_ref[0:1, :], weight_ref[1:2, :]
    real = cosine * weight_re - sine * weight_im
    imag = cosine * weight_im + sine * weight_re
    for rows, columns, part in (
        (0, 0, real),
        (0, beams, -imag),
        (probes, 0, imag),
        (probes, beams, real),
    ):
        high, low = split(part)
        high_ref[rows : rows + probes, columns : columns + beams] = high
        low_ref[rows : rows + probes, columns : columns + beams] = low


def screened(wave, potential_ref, layer):
    count = G // 2
    stride = potential_ref.shape[0] // count
    potential = jnp.concatenate(
        [
            jnp.concatenate(
                [potential_ref[pl.ds(4 * layer + 2 * parity + half, count, stride), :] for half in range(2)],
                axis=1,
            )
            for parity in range(2)
        ],
        axis=0,
    )
    sine, cosine = sine_cosine(potential - 1.5)
    cos_mid, sin_mid = math.cos(1.5), math.sin(1.5)
    cosine, sine = cosine * cos_mid - sine * sin_mid, sine * cos_mid + cosine * sin_mid
    real, imag = wave[:G], wave[G:]
    return jnp.concatenate([real * cosine - imag * sine, real * sine + imag * cosine], axis=0)


def masked(real, imag, first, limit_of):
    u = lax.broadcasted_iota(jnp.int32, real.shape, 0)
    v = lax.broadcasted_iota(jnp.int32, real.shape, 1)
    half = real.shape[1] // 2
    u = u - first if first else jnp.where(u < half, u, u - 2 * half)
    v = jnp.where(v < half, v, v - 2 * half)
    keep = u * u + v * v <= limit_of
    return jnp.concatenate([jnp.where(keep, real, 0.0), jnp.where(keep, imag, 0.0)], axis=0)


def step(field, table):
    field = from_left(table(0), field)
    field = masked(*from_right(field, table(1)), REACH, LIMIT)
    real, imag = from_right(field, table(2))
    return from_left(table(3), jnp.concatenate([real, imag], axis=0))


def propagate_kernel(table_ref, wave_ref, potential_ref, out_ref):
    table = functools.partial(table_of, table_ref)
    wave = wave_ref[...]
    for layer in range(SLICES - 1):
        wave = step(screened(wave, potential_ref, layer), table)
    field = from_left(table(4), screened(wave, potential_ref, SLICES - 1))
    field = masked(*from_right(field, table(5)), 0, LIMIT)
    real, imag = from_right(field, table(6))
    out_ref[...] = from_left(table(7), jnp.concatenate([real, imag], axis=0))


def probe_kernel(configs, block_ref, high_ref, low_ref, mine_ref, other_ref):
    here = block_ref.shape[0] // (2 * K)
    field = jnp.concatenate(
        [
            jnp.concatenate(
                [block_ref[pl.ds(2 * K * config + part, K, 2), :] for part in range(2)], axis=0
            )
            for config in range(here)
        ],
        axis=1,
    )
    waves = from_left((high_ref[...], low_ref[...]), field)
    probes = waves.shape[0] // 2
    real, imag = waves[:probes], waves[probes:]
    power = real * real + imag * imag
    total = sum(power[:, K * config : K * config + K] for config in range(here)) * (1.0 / configs)
    mine_ref[...] = total[: probes // 2]
    other_ref[...] = total[probes // 2 :]


VMEM = pl.BlockSpec(memory_space=pltpu.VMEM)
SMEM = pl.BlockSpec(memory_space=pltpu.SMEM)
PARAMS = pltpu.CompilerParams(vmem_limit_bytes=24 * 1024 * 1024)


def per_device(potential, tilts, aperture, positions):
    nx, near = lax.axis_size("x"), lax.axis_size("y") * lax.axis_size("z")
    pairs, cores = lax.axis_size("far"), lax.axis_size("core")
    configs = pairs * cores
    beams = tilts.shape[0]
    probes = positions.shape[0]
    quarter = probes // configs
    own = lax.axis_index(("x", "y", "z"))
    slab = lax.axis_index(("far", "core"))

    def gather(piece, count, axes):
        copies = jnp.broadcast_to(piece[None], (count, *piece.shape))
        return lax.all_to_all(copies, axes, 0, 0, tiled=True).reshape(count * piece.shape[0], K)

    whole = potential.reshape(potential.size // K, K)
    whole = gather(gather(whole, near, ("y", "z")), nx, "x")

    places = positions.reshape(configs, quarter, 2)
    places = jnp.concatenate([places[slab], places[slab ^ 1]], axis=0)
    square = (tilts[:, 0] ** 2 + tilts[:, 1] ** 2).astype(F32)
    amount = aperture.astype(F32) * (1.0 / math.sqrt(beams))
    weight = jnp.stack([jnp.cos(DEFOCUS_RATE * square) * amount, -jnp.sin(DEFOCUS_RATE * square) * amount])
    tilt = lax.dynamic_index_in_dim(tilts, own, 0, keepdims=False)
    start, coef_high, coef_low = pl.pallas_call(
        prepare_kernel,
        out_shape=(
            jax.ShapeDtypeStruct((2 * G, G), F32),
            jax.ShapeDtypeStruct((4 * quarter, 2 * beams), BF16),
            jax.ShapeDtypeStruct((4 * quarter, 2 * beams), BF16),
        ),
        in_specs=[SMEM] + [VMEM] * 3,
        out_specs=(VMEM,) * 3,
        compiler_params=PARAMS,
        name="prepare",
    )(tilt, places, tilts.T, weight)

    image = pl.pallas_call(
        propagate_kernel,
        out_shape=jax.ShapeDtypeStruct((2 * K, K), F32),
        in_specs=[VMEM] * 3,
        out_specs=VMEM,
        compiler_params=PARAMS,
        name="propagate",
    )(jnp.asarray(tables()), start, whole)

    rows = jnp.broadcast_to(image.reshape(1, K, 2, K), (pairs, K, 2, K)).reshape(pairs * K, 2, K)
    block = lax.all_to_all(rows, ("far", "x", "y", "z"), 0, 0, tiled=True).reshape(2 * pairs * beams, K)
    mine, other = pl.pallas_call(
        functools.partial(probe_kernel, configs),
        out_shape=[jax.ShapeDtypeStruct((quarter, K), F32)] * cores,
        in_specs=[VMEM] * 3,
        out_specs=[VMEM] * cores,
        compiler_params=PARAMS,
        name="probe",
    )(block, coef_high, coef_low)
    return mine + lax.ppermute(other, "core", [(0, 1), (1, 0)])


def solution(mesh):
    fine = jax.sharding.Mesh(mesh.devices.reshape(4, 8, 4, 2, 2), ("x", "y", "z", "far", "core"))
    beam, slab = ("x", "y", "z"), ("far", "core")
    return jax.shard_map(
        per_device,
        mesh=fine,
        in_specs=(P(slab, None, beam), P(), P(), P()),
        out_specs=P(slab, beam),
        check_vma=False,
    )
```

```python
import functools
import math

import jax
import jax.numpy as jnp
from jax import lax
from jax.experimental import pallas as pl
from jax.experimental.pallas import tpu as pltpu
from jax.sharding import PartitionSpec as P

G = 256
K = 128
SLICES = 3
LIMIT = (G // 3) ** 2
REACH = G // 3
ROWS = 176
PIECE = SLICES * 4

FRESNEL_RATE = 0.00019
DEFOCUS_RATE = 0.01

F32 = jnp.float32
BF16 = jnp.bfloat16


def split(value):
    high = value.astype(BF16)
    return high, (value - high.astype(F32)).astype(BF16)


def sine_of(t):
    s = t * t
    sine = jnp.full_like(t, -2.5052108e-8)
    for term in (2.7557319e-6, -1.9841270e-4, 8.3333333e-3, -1.6666667e-1, 1.0):
        sine = sine * s + term
    return sine * t


def cosine_of(t):
    s = t * t
    cosine = jnp.full_like(t, 2.0876757e-9)
    for term in (-2.7557319e-7, 2.4801587e-5, -1.3888889e-3, 4.1666667e-2, -0.5, 1.0):
        cosine = cosine * s + term
    return cosine


def half_angle(steps, length):
    near = ((steps + length // 2) & (length - 1)) - length // 2
    return near.astype(F32) * (math.pi / length)


def cosine_step(steps, length):
    sine = sine_of(half_angle(steps, length))
    return 1.0 - 2.0 * sine * sine


def circle(steps, length):
    half = half_angle(steps, length)
    sine = sine_of(half)
    return 2.0 * sine * cosine_of(half), 1.0 - 2.0 * sine * sine


def iota(shape, axis):
    return lax.broadcasted_iota(jnp.int32, shape, axis)


def natural(place):
    return place & (G // 2 - 1)


def mixed(place):
    n = 2 * natural(place)
    return jnp.where(n < G // 2, n, n - (G // 2 - 1))


def folded(place, order):
    factor = jnp.where(place == G // 2, G // 2, order(place))
    return factor, jnp.where(place > G // 2, -(G // 4), 0)


def position(place, order):
    n = order(place)
    return jnp.where(place < G // 2, n, jnp.where(place == G // 2, G // 2, -n))


def signed(index, length):
    return jnp.where(index < length // 2, index, index - length)


def forward_table(shape, frequency, order, axis):
    factor, offset = folded(iota(shape, axis), order)
    return cosine_step(frequency(iota(shape, 1 - axis)) * factor + offset, G)


def fresnel(shape, frequency_u, frequency_v):
    u, v = frequency_u(iota(shape, 0)), frequency_v(iota(shape, 1))
    square = u * u + v * v
    angle = jnp.minimum(square, LIMIT).astype(F32) * FRESNEL_RATE
    keep = jnp.where(square <= LIMIT, 1.0 / (G * G), 0.0)
    return cosine_of(angle) * keep, -sine_of(angle) * keep


def copies_kernel(potential_ref, out_ref):
    values = potential_ref[0]
    pick = ((iota((K, K), 0) + iota((K, K), 1)) & (K - 1)) == 0
    mirror = jnp.where(pick, 1.0, 0.0)
    quarters = [values[:, K * i : K * (i + 1)] for i in range(4)]
    for i in (1, 3):
        quarters[i] = jnp.dot(
            quarters[i], mirror, precision=lax.Precision.HIGHEST, preferred_element_type=F32
        )
    piece = jnp.concatenate(quarters, axis=0)
    out_ref[...] = jnp.broadcast_to(piece[None], out_ref.shape)


AHEAD_LEFT = (0, ROWS, G)
AHEAD_RIGHT = (AHEAD_LEFT[0] + AHEAD_LEFT[1], G, G)
BACK_RIGHT = (AHEAD_RIGHT[0] + G, G, G)
BACK_LEFT = (BACK_RIGHT[0] + G, G, G)
CROP_LEFT = (BACK_LEFT[0] + G, K, G)
CROP_RIGHT = (CROP_LEFT[0] + K, G, K)
IMAGE_RIGHT = (CROP_RIGHT[0] + G, K, 2 * K)
IMAGE_LEFT = (IMAGE_RIGHT[0] + K, 2 * K, 2 * K)
TABLE_ROWS = IMAGE_LEFT[0] + IMAGE_LEFT[1]

def terms(ref, where):
    row, rows, columns = where
    return ref[row : row + rows, :columns], ref[row : row + rows, G : G + columns]


def near(index):
    return index - REACH


def whole(index):
    return index


def band(index):
    return signed(index, K)


def plane_wave(tilt_x, tilt_y):
    sine_x, cosine_x = circle(tilt_x * position(iota((G, K), 0), mixed), G)
    sine_y, cosine_y = circle(tilt_y * position(iota((8, G), 1), natural), G)
    sine_x, cosine_x = (jnp.concatenate([value] * (G // K), axis=1) for value in (sine_x, cosine_x))
    sine_y, cosine_y = (jnp.concatenate([value] * (G // 8), axis=0) for value in (sine_y, cosine_y))
    return cosine_x * cosine_y - sine_x * sine_y, sine_x * cosine_y + cosine_x * sine_y


def prepare_kernel(places_ref, tilts_ref, weight_ref, high_ref, low_ref, table_ref):
    probes = places_ref.shape[0]
    beams = tilts_ref.shape[1]
    steps = places_ref[:, 0:1] * tilts_ref[0:1, :] + places_ref[:, 1:2] * tilts_ref[1:2, :]
    sine, cosine = circle(-steps, K)
    weight_re, weight_im = weight_ref[0:1, :], weight_ref[1:2, :]
    real = cosine * weight_re - sine * weight_im
    imag = cosine * weight_im + sine * weight_re
    for row, column, part in (
        (0, 0, real),
        (0, beams, -imag),
        (probes, 0, imag),
        (probes, beams, real),
    ):
        high, low = split(part)
        high_ref[row : row + probes, column : column + beams] = high
        low_ref[row : row + probes, column : column + beams] = low

    m, other = iota((2 * K, 2 * K), 0), iota((2 * K, 2 * K), 1)
    turn = 2 * (m >> 1) * (other & (K - 1)) + (G // 4) * ((other >> 7) - (m & 1))
    left, right = iota((K, 2 * K), 0), iota((K, 2 * K), 1)
    for (row, rows, columns), table in (
        (AHEAD_LEFT, forward_table((ROWS, G), near, mixed, 1)),
        (AHEAD_RIGHT, forward_table((G, G), whole, natural, 0)),
        (BACK_RIGHT, forward_table((G, G), whole, natural, 1)),
        (BACK_LEFT, forward_table((G, G), near, mixed, 0)),
        (CROP_LEFT, forward_table((K, G), band, mixed, 1)),
        (CROP_RIGHT, forward_table((G, K), band, natural, 0)),
        (IMAGE_RIGHT, cosine_step(2 * left * (right & (K - 1)) - (G // 4) * (right >> 7), G)),
        (IMAGE_LEFT, cosine_step(turn, G)),
    ):
        high, low = split(table)
        table_ref[row : row + rows, :columns] = high
        table_ref[row : row + rows, G : G + columns] = low


def from_left(table, field):
    high, low = split(field)
    short = table[0].shape[1] - field.shape[0]
    if short:
        none = jnp.zeros((short, field.shape[1]), BF16)
        high, low = jnp.concatenate([high, none], axis=0), jnp.concatenate([low, none], axis=0)
    return jnp.dot(
        jnp.concatenate([table[0], table[0], table[1]], axis=1),
        jnp.concatenate([high, low, high], axis=0),
        preferred_element_type=F32,
    )


def from_right(field, table):
    high, low = split(field)
    return jnp.dot(
        jnp.concatenate([high, low, high], axis=1),
        jnp.concatenate([table[0], table[0], table[1]], axis=0),
        preferred_element_type=F32,
    )


def halves(value, axis):
    half = value.shape[axis] // 2
    return lax.slice_in_dim(value, 0, half, axis=axis), lax.slice_in_dim(value, half, 2 * half, axis=axis)


def fold(real, imag, axis):
    real_ahead, real_back = halves(real, axis)
    imag_ahead, imag_back = halves(imag, axis)
    alone = iota(real_ahead.shape, axis) == 0
    return (
        jnp.concatenate(
            [
                jnp.where(alone, real_ahead, real_ahead + real_back),
                jnp.where(alone, real_back, imag_ahead - imag_back),
            ],
            axis=axis,
        ),
        jnp.concatenate(
            [
                jnp.where(alone, imag_ahead, imag_ahead + imag_back),
                jnp.where(alone, imag_back, real_back - real_ahead),
            ],
            axis=axis,
        ),
    )


def unfold(real, imag, axis):
    real_even, real_odd = halves(real, axis)
    imag_even, imag_odd = halves(imag, axis)
    alone = iota(real_even.shape, axis) == 0
    return (
        jnp.concatenate(
            [
                jnp.where(alone, real_even, real_even - imag_odd),
                jnp.where(alone, real_odd, real_even + imag_odd),
            ],
            axis=axis,
        ),
        jnp.concatenate(
            [
                jnp.where(alone, imag_even, imag_even + real_odd),
                jnp.where(alone, imag_odd, imag_even - real_odd),
            ],
            axis=axis,
        ),
    )


def spectrum(real, imag, left, right, factor):
    field = from_left(left, jnp.concatenate(fold(real, imag, 0), axis=1))
    field = jnp.concatenate(fold(*halves(field, 1), 1), axis=0)
    real, imag = halves(from_right(field, right), 0)
    return (
        real * factor[0] - imag * factor[1],
        real * factor[1] + imag * factor[0],
    )


def screened(real, imag, potential_ref, layer):
    count = G // 4

    def rows(half, parity, side):
        at = PIECE * count * half + SLICES * (2 * parity + side) + layer
        return potential_ref[pl.ds(at, count, PIECE), :]

    def block(half, parity):
        values = jnp.concatenate([rows(half, parity, side) for side in range(2)], axis=1)
        return pltpu.roll(values, 1, 0) if half and not parity else values

    potential = jnp.concatenate([block(half, parity) for half in range(2) for parity in range(2)], axis=0)
    sine, cosine = sine_of(potential - 1.5), cosine_of(potential - 1.5)
    cos_mid, sin_mid = math.cos(1.5), math.sin(1.5)
    cosine, sine = cosine * cos_mid - sine * sin_mid, sine * cos_mid + cosine * sin_mid
    return real * cosine - imag * sine, real * sine + imag * cosine


def propagate_kernel(tilt_ref, potential_ref, table_ref, out_ref, factor_ref):
    table = functools.partial(terms, table_ref)
    real, imag = fresnel((ROWS, G), near, lambda index: signed(index, G))
    factor_ref[0], factor_ref[1] = real, imag
    real, imag = plane_wave(tilt_ref[0], tilt_ref[1])
    for layer in range(SLICES - 1):
        real, imag = screened(real, imag, potential_ref, layer)
        real, imag = spectrum(real, imag, table(AHEAD_LEFT), table(AHEAD_RIGHT), factor_ref)
        field = from_right(jnp.concatenate([real, imag], axis=0), table(BACK_RIGHT))
        field = jnp.concatenate(unfold(*halves(field, 0), 1), axis=1)
        real, imag = unfold(*halves(from_left(table(BACK_LEFT), field), 1), 0)
    real, imag = screened(real, imag, potential_ref, SLICES - 1)
    real, imag = spectrum(real, imag, table(CROP_LEFT), table(CROP_RIGHT), fresnel((K, K), band, band))
    product = from_right(jnp.concatenate([real, imag], axis=0), table(IMAGE_RIGHT))
    real = product[:K, :K] - product[K:, K:]
    imag = product[:K, K:] + product[K:, :K]
    out_ref[...] = from_left(table(IMAGE_LEFT), jnp.concatenate([real, imag], axis=0))


def probe_kernel(configs, block_ref, high_ref, low_ref, mine_ref, other_ref):
    here = block_ref.shape[0] // (2 * K)
    field = jnp.concatenate(
        [
            jnp.concatenate(
                [block_ref[pl.ds(2 * K * config + part, K, 2), :] for part in range(2)], axis=0
            )
            for config in range(here)
        ],
        axis=1,
    )
    waves = from_left((high_ref[...], low_ref[...]), field)
    probes = waves.shape[0] // 2
    real, imag = waves[:probes], waves[probes:]
    power = real * real + imag * imag
    total = sum(power[:, K * config : K * config + K] for config in range(here)) * (1.0 / configs)
    mine_ref[...] = total[: probes // 2]
    other_ref[...] = total[probes // 2 :]


VMEM = pl.BlockSpec(memory_space=pltpu.VMEM)
SMEM = pl.BlockSpec(memory_space=pltpu.SMEM)
PARAMS = pltpu.CompilerParams(vmem_limit_bytes=24 * 1024 * 1024)


def shape_of(dtype, *shape):
    return jax.ShapeDtypeStruct(shape, dtype)


def prepare(places, tilts, weight):
    probes, beams = places.shape[0], tilts.shape[1]
    out = [
        shape_of(BF16, 2 * probes, 2 * beams),
        shape_of(BF16, 2 * probes, 2 * beams),
        shape_of(BF16, TABLE_ROWS, 2 * G),
    ]
    return pl.pallas_call(
        prepare_kernel,
        out_shape=out,
        in_specs=[VMEM] * 3,
        out_specs=[VMEM] * len(out),
        compiler_params=PARAMS,
        name="prepare",
    )(places, tilts, weight)


def propagate(tilt, potential, table):
    return pl.pallas_call(
        propagate_kernel,
        out_shape=shape_of(F32, 2 * K, K),
        in_specs=[SMEM, VMEM, VMEM],
        out_specs=VMEM,
        scratch_shapes=[pltpu.VMEM((2, ROWS, G), F32)],
        compiler_params=PARAMS,
        name="propagate",
    )(tilt, potential, table)


def probe(block, high, low, configs):
    quarter = high.shape[0] // 4
    return pl.pallas_call(
        functools.partial(probe_kernel, configs),
        out_shape=[shape_of(F32, quarter, K)] * 2,
        in_specs=[VMEM] * 3,
        out_specs=[VMEM] * 2,
        compiler_params=PARAMS,
        name="probe",
    )(block, high, low)


def copies_of(potential, count):
    return pl.pallas_call(
        copies_kernel,
        out_shape=shape_of(F32, count, PIECE, K),
        in_specs=[VMEM],
        out_specs=VMEM,
        compiler_params=PARAMS,
        name="copies",
    )(potential)


def per_device(groups, potential, tilts, aperture, positions):
    near, far = groups
    devices = lax.axis_size("beam")
    pairs, cores = lax.axis_size("pair"), lax.axis_size("core")
    configs = pairs * cores
    beams = tilts.shape[0]
    quarter = positions.shape[0] // configs
    own = lax.axis_index("beam")
    slab = lax.axis_index(("pair", "core"))

    part = lax.all_to_all(copies_of(potential, len(near[0])), "beam", 0, 0, axis_index_groups=near)
    part, tilts, aperture, positions = lax.optimization_barrier((part, tilts, aperture, positions))
    part = part.reshape(len(near[0]) * PIECE, K)
    whole = lax.all_to_all(
        jnp.broadcast_to(part[None], (len(far[0]), *part.shape)), "beam", 0, 0, axis_index_groups=far
    ).reshape(devices * PIECE, K)

    places = positions.reshape(configs, quarter, 2)
    places = jnp.concatenate([places[slab], places[slab ^ 1]], axis=0)
    square = (tilts[:, 0] ** 2 + tilts[:, 1] ** 2).astype(F32)
    amount = aperture.astype(F32) * (1.0 / math.sqrt(beams))
    weight = jnp.stack([jnp.cos(DEFOCUS_RATE * square) * amount, -jnp.sin(DEFOCUS_RATE * square) * amount])
    tilt = lax.dynamic_index_in_dim(tilts, own, 0, keepdims=False)
    coef_high, coef_low, table = prepare(places, tilts.T, weight)
    image = propagate(tilt, whole, table)

    rows = jnp.broadcast_to(image.reshape(1, K, 2, K), (pairs, K, 2, K)).reshape(pairs * K, 2, K)
    block = lax.all_to_all(rows, ("pair", "beam"), 0, 0, tiled=True).reshape(2 * pairs * beams, K)
    mine, other = probe(block, coef_high, coef_low, configs)
    return mine + lax.ppermute(other, "core", [(0, 1), (1, 0)])


def solution(mesh):
    fine = jax.sharding.Mesh(mesh.devices.reshape(-1, 2, 2), ("beam", "pair", "core"))
    nx, run = 4, mesh.devices.shape[0] // 4
    near = [[x * run + i for i in (range(run) if 2 * x < nx else reversed(range(run)))] for x in range(nx)]
    order = [*range(nx // 2), *reversed(range(nx // 2, nx))]
    far = [[x * run + i for x in order] for i in range(run)]
    return jax.shard_map(
        functools.partial(per_device, (near, far)),
        mesh=fine,
        in_specs=(P(("pair", "core"), None, "beam"), P(), P(), P()),
        out_specs=P(("pair", "core"), "beam"),
        check_vma=False,
    )
```

```python
import functools
import math

import jax
import jax.numpy as jnp
from jax import lax
from jax.experimental import pallas as pl
from jax.experimental.pallas import tpu as pltpu
from jax.sharding import PartitionSpec as P

G = 256
K = 128
SLICES = 3
LIMIT = (G // 3) ** 2
REACH = G // 3
ROWS = 176
PIECE = SLICES * 4

FRESNEL_RATE = 0.00019
DEFOCUS_RATE = 0.01

F32 = jnp.float32
BF16 = jnp.bfloat16


def split(value):
    high = value.astype(BF16)
    return high, (value - high.astype(F32)).astype(BF16)


def sine_of(t):
    s = t * t
    sine = jnp.full_like(t, 2.60501958e-6)
    for term in (-1.9808983e-4, 8.33304978e-3, -1.66666579e-1, 0.999999996):
        sine = sine * s + term
    return sine * t


def cosine_of(t):
    s = t * t
    cosine = jnp.full_like(t, 2.31515759e-5)
    for term in (-1.38535979e-3, 4.16635698e-2, -0.499999047, 0.999999953):
        cosine = cosine * s + term
    return cosine


def half_angle(steps, length):
    near = ((steps + length // 2) & (length - 1)) - length // 2
    return near.astype(F32) * (math.pi / length)


def cosine_step(steps, length):
    sine = sine_of(half_angle(steps, length))
    return 1.0 - 2.0 * sine * sine


def circle(steps, length):
    half = half_angle(steps, length)
    sine = sine_of(half)
    return 2.0 * sine * cosine_of(half), 1.0 - 2.0 * sine * sine


def iota(shape, axis):
    return lax.broadcasted_iota(jnp.int32, shape, axis)


def natural(place):
    return place & (G // 2 - 1)


def mixed(place):
    n = 2 * natural(place)
    return jnp.where(n < G // 2, n, n - (G // 2 - 1))


def folded(place, order):
    factor = jnp.where(place == G // 2, G // 2, order(place))
    return factor, jnp.where(place > G // 2, -(G // 4), 0)


def position(place, order):
    n = order(place)
    return jnp.where(place < G // 2, n, jnp.where(place == G // 2, G // 2, -n))


def signed(index, length):
    return jnp.where(index < length // 2, index, index - length)


def forward_table(shape, frequency, order, axis):
    factor, offset = folded(iota(shape, axis), order)
    return cosine_step(frequency(iota(shape, 1 - axis)) * factor + offset, G)


def fresnel(shape, frequency_u, frequency_v):
    u, v = frequency_u(iota(shape, 0)), frequency_v(iota(shape, 1))
    square = u * u + v * v
    angle = jnp.minimum(square, LIMIT).astype(F32) * FRESNEL_RATE
    keep = jnp.where(square <= LIMIT, 1.0 / (G * G), 0.0)
    return cosine_of(angle) * keep, -sine_of(angle) * keep


def copies_kernel(potential_ref, out_ref):
    values = potential_ref[0]
    pick = ((iota((K, K), 0) + iota((K, K), 1)) & (K - 1)) == 0
    mirror = jnp.where(pick, 1.0, 0.0)
    quarters = [values[:, K * i : K * (i + 1)] for i in range(4)]
    for i in (1, 3):
        quarters[i] = jnp.dot(
            quarters[i], mirror, precision=lax.Precision.HIGHEST, preferred_element_type=F32
        )
    pieces = [
        jnp.concatenate([quarter[layer : layer + 1] for quarter in quarters], axis=0)[None]
        for layer in range(SLICES)
    ]
    out_ref[...] = jnp.concatenate(pieces * (out_ref.shape[0] // SLICES), axis=0)


AHEAD_LEFT = (0, ROWS, G)
AHEAD_RIGHT = (AHEAD_LEFT[0] + AHEAD_LEFT[1], G, G)
BACK_RIGHT = (AHEAD_RIGHT[0] + G, G, G)
BACK_LEFT = (BACK_RIGHT[0] + G, G, G)
CROP_LEFT = (BACK_LEFT[0] + G, K, G)
IMAGE_RIGHT = (CROP_LEFT[0] + K, K, 2 * K)
IMAGE_LEFT = (IMAGE_RIGHT[0] + K, 2 * K, 2 * K)
TABLE_ROWS = IMAGE_LEFT[0] + IMAGE_LEFT[1]

def terms(ref, where):
    row, rows, columns = where
    return ref[row : row + rows, :columns], ref[row : row + rows, G : G + columns]


def near(index):
    return index - ROWS // 2


def whole(index):
    return index


def centred(index):
    return index - K // 2


def prepare_kernel(
    tilt_ref, places_ref, tilts_ref, weight_ref, coef_ref, table_ref, factor_ref, across_ref
):
    across_ref[0], across_ref[1] = circle(tilt_ref[0] * position(iota((G, K), 0), mixed), G)
    factor_ref[0], factor_ref[1] = fresnel((ROWS, G), near, lambda index: signed(index, G))

    probes = places_ref.shape[0]
    beams = tilts_ref.shape[1]
    steps = places_ref[:, 0:1] * tilts_ref[0:1, :] + places_ref[:, 1:2] * tilts_ref[1:2, :]
    sine, cosine = circle(-steps, K)
    weight_re, weight_im = weight_ref[0:1, :], weight_ref[1:2, :]
    coef_ref[0] = cosine * weight_re - sine * weight_im
    coef_ref[1] = cosine * weight_im + sine * weight_re

    m, other = iota((2 * K, 2 * K), 0), iota((2 * K, 2 * K), 1)
    turn = 2 * (m >> 1) * centred(other & (K - 1)) + (G // 4) * ((other >> 7) - (m & 1))
    left, right = iota((K, 2 * K), 0), iota((K, 2 * K), 1)
    for (row, rows, columns), table in (
        (AHEAD_LEFT, forward_table((ROWS, G), near, mixed, 1)),
        (AHEAD_RIGHT, forward_table((G, G), whole, natural, 0)),
        (BACK_RIGHT, forward_table((G, G), whole, natural, 1)),
        (BACK_LEFT, forward_table((G, G), near, mixed, 0)),
        (CROP_LEFT, forward_table((K, G), centred, mixed, 1)),
        (IMAGE_RIGHT, cosine_step(2 * left * (right & (K - 1)) - (G // 4) * (right >> 7), G)),
        (IMAGE_LEFT, cosine_step(turn, G)),
    ):
        high, low = split(table)
        table_ref[row : row + rows, :columns] = high
        table_ref[row : row + rows, G : G + columns] = low


def from_left(table, field):
    high, low = split(field)
    short = table[0].shape[1] - field.shape[0]
    if short:
        none = jnp.zeros((short, field.shape[1]), BF16)
        high, low = jnp.concatenate([high, none], axis=0), jnp.concatenate([low, none], axis=0)
    return jnp.dot(
        jnp.concatenate([table[0], table[0], table[1]], axis=1),
        jnp.concatenate([high, low, high], axis=0),
        preferred_element_type=F32,
    )


def from_right(field, table):
    high, low = split(field)
    return jnp.dot(
        jnp.concatenate([high, low, high], axis=1),
        jnp.concatenate([table[0], table[0], table[1]], axis=0),
        preferred_element_type=F32,
    )


def halves(value, axis):
    half = value.shape[axis] // 2
    return lax.slice_in_dim(value, 0, half, axis=axis), lax.slice_in_dim(value, half, 2 * half, axis=axis)


def alone(first, others, axis):
    if axis:
        return jnp.where(iota(others.shape, 1) == 0, first, others)
    head = jnp.where(iota((8, others.shape[1]), 0) == 0, first[:8], others[:8])
    return jnp.concatenate([head, others[8:]], axis=0)


def fold(real, imag, axis):
    real_ahead, real_back = halves(real, axis)
    imag_ahead, imag_back = halves(imag, axis)
    real_odd, imag_odd = real_back - real_ahead, imag_ahead - imag_back
    return (
        jnp.concatenate(
            [alone(real_ahead, real_ahead + real_back, axis), alone(real_back, imag_odd, axis)], axis=axis
        ),
        jnp.concatenate(
            [alone(imag_ahead, imag_ahead + imag_back, axis), alone(imag_back, real_odd, axis)], axis=axis
        ),
    )


def unfold(real, imag, axis):
    real_even, real_odd = halves(real, axis)
    imag_even, imag_odd = halves(imag, axis)
    return (
        jnp.concatenate(
            [alone(real_even, real_even - imag_odd, axis), alone(real_odd, real_even + imag_odd, axis)],
            axis=axis,
        ),
        jnp.concatenate(
            [alone(imag_even, imag_even + real_odd, axis), alone(imag_odd, imag_even - real_odd, axis)],
            axis=axis,
        ),
    )


def spectrum(real, imag, left, right, factor):
    field = from_left(left, jnp.concatenate(fold(real, imag, 0), axis=1))
    field = jnp.concatenate(fold(*halves(field, 1), 1), axis=0)
    real, imag = halves(from_right(field, right), 0)
    return (
        real * factor[0] - imag * factor[1],
        real * factor[1] + imag * factor[0],
    )


def screened(real, imag, potential_ref, layer):
    count = G // 4

    def rows(half, parity, side):
        at = PIECE * count * half + 4 * layer + 2 * parity + side
        return potential_ref[pl.ds(at, count, PIECE), :]

    def block(half, parity):
        values = jnp.concatenate([rows(half, parity, side) for side in range(2)], axis=1)
        return pltpu.roll(values, 1, 0) if half and not parity else values

    potential = jnp.concatenate([block(half, parity) for half in range(2) for parity in range(2)], axis=0)
    turned = potential - math.pi / 2
    sine, cosine = cosine_of(turned), sine_of(turned)
    return -(real * cosine + imag * sine), real * sine - imag * cosine


def plane_wave(across_ref, tilt_y):
    sine_x, cosine_x = (jnp.concatenate([across_ref[i]] * (G // K), axis=1) for i in range(2))
    sine_y, cosine_y = circle(tilt_y * position(iota((8, G), 1), natural), G)
    sine_y, cosine_y = (jnp.concatenate([value] * (G // 8), axis=0) for value in (sine_y, cosine_y))
    return cosine_x * cosine_y - sine_x * sine_y, sine_x * cosine_y + cosine_x * sine_y


def band_of(value):
    return jnp.where(iota((value.shape[0], K), 1) < K // 2, value[:, :K], value[:, K:])


def propagate_kernel(tilt_ref, potential_ref, table_ref, factor_ref, across_ref, out_ref):
    table = functools.partial(terms, table_ref)
    real, imag = plane_wave(across_ref, tilt_ref[1])
    for layer in range(SLICES - 1):
        real, imag = screened(real, imag, potential_ref, layer)
        real, imag = spectrum(real, imag, table(AHEAD_LEFT), table(AHEAD_RIGHT), factor_ref)
        field = from_right(jnp.concatenate([real, imag], axis=0), table(BACK_RIGHT))
        field = jnp.concatenate(unfold(*halves(field, 0), 1), axis=1)
        real, imag = unfold(*halves(from_left(table(BACK_LEFT), field), 1), 0)
    crop_right = [band_of(term) for term in table(AHEAD_RIGHT)]
    first = (ROWS - K) // 2
    crop_factor = [band_of(factor_ref[i, first : first + K, :]) for i in range(2)]
    real, imag = screened(real, imag, potential_ref, SLICES - 1)
    real, imag = spectrum(real, imag, table(CROP_LEFT), crop_right, crop_factor)
    product = from_right(jnp.concatenate([real, imag], axis=0), table(IMAGE_RIGHT))
    real = product[:K, :K] - product[K:, K:]
    imag = product[:K, K:] + product[K:, :K]
    out_ref[...] = from_left(table(IMAGE_LEFT), jnp.concatenate([real, imag], axis=0))


def probe_kernel(configs, block_ref, coef_ref, mine_ref, other_ref):
    here = block_ref.shape[0] // (2 * K)
    field = jnp.concatenate(
        [
            jnp.concatenate(
                [block_ref[pl.ds(2 * K * config + part, K, 2), :] for part in range(2)], axis=0
            )
            for config in range(here)
        ],
        axis=1,
    )
    real, imag = coef_ref[0], coef_ref[1]
    table = jnp.concatenate(
        [jnp.concatenate([real, -imag], axis=1), jnp.concatenate([imag, real], axis=1)], axis=0
    )
    waves = from_left(split(table), field)
    probes = waves.shape[0] // 2
    real, imag = waves[:probes], waves[probes:]
    power = real * real + imag * imag
    total = sum(power[:, K * config : K * config + K] for config in range(here)) * (1.0 / configs)
    mine_ref[...] = total[: probes // 2]
    other_ref[...] = total[probes // 2 :]


VMEM = pl.BlockSpec(memory_space=pltpu.VMEM)
SMEM = pl.BlockSpec(memory_space=pltpu.SMEM)
PARAMS = pltpu.CompilerParams(vmem_limit_bytes=24 * 1024 * 1024)


def shape_of(dtype, *shape):
    return jax.ShapeDtypeStruct(shape, dtype)


def prepare(tilt, places, tilts, weight):
    out = [
        shape_of(F32, 2, places.shape[0], tilts.shape[1]),
        shape_of(BF16, TABLE_ROWS, 2 * G),
        shape_of(F32, 2, ROWS, G),
        shape_of(F32, 2, G, K),
    ]
    return pl.pallas_call(
        prepare_kernel,
        out_shape=out,
        in_specs=[SMEM] + [VMEM] * 3,
        out_specs=[VMEM] * len(out),
        compiler_params=PARAMS,
        name="prepare",
    )(tilt, places, tilts, weight)


def propagate(*operands):
    return pl.pallas_call(
        propagate_kernel,
        out_shape=shape_of(F32, 2 * K, K),
        in_specs=[SMEM] + [VMEM] * (len(operands) - 1),
        out_specs=VMEM,
        compiler_params=PARAMS,
        name="propagate",
    )(*operands)


def probe(block, coef, configs):
    quarter = coef.shape[1] // 2
    return pl.pallas_call(
        functools.partial(probe_kernel, configs),
        out_shape=[shape_of(F32, quarter, K)] * 2,
        in_specs=[VMEM] * 2,
        out_specs=[VMEM] * 2,
        compiler_params=PARAMS,
        name="probe",
    )(block, coef)


def copies_of(potential, count):
    return pl.pallas_call(
        copies_kernel,
        out_shape=shape_of(F32, count * SLICES, 4, K),
        in_specs=[VMEM],
        out_specs=VMEM,
        compiler_params=PARAMS,
        name="copies",
    )(potential)


def per_device(groups, potential, tilts, aperture, positions):
    near, far = groups
    devices = lax.axis_size("beam")
    pairs, cores = lax.axis_size("pair"), lax.axis_size("core")
    configs = pairs * cores
    beams = tilts.shape[0]
    quarter = positions.shape[0] // configs
    own = lax.axis_index("beam")
    slab = lax.axis_index(("pair", "core"))

    copies = copies_of(potential, len(near[0]))
    part = lax.all_to_all(copies, "beam", 0, 0, axis_index_groups=near, tiled=True)
    part, tilts, aperture, positions = lax.optimization_barrier((part, tilts, aperture, positions))
    part = part.reshape(len(near[0]) * PIECE, K)
    whole = lax.all_to_all(
        jnp.broadcast_to(part[None], (len(far[0]), *part.shape)), "beam", 0, 0, axis_index_groups=far
    ).reshape(devices * PIECE, K)

    places = positions.reshape(configs, quarter, 2)
    places = jnp.concatenate([places[slab], places[slab ^ 1]], axis=0)
    square = (tilts[:, 0] ** 2 + tilts[:, 1] ** 2).astype(F32)
    amount = aperture.astype(F32) * (1.0 / math.sqrt(beams))
    weight = jnp.stack([jnp.cos(DEFOCUS_RATE * square) * amount, -jnp.sin(DEFOCUS_RATE * square) * amount])
    tilt = lax.dynamic_index_in_dim(tilts, own, 0, keepdims=False)
    coef, *tables = prepare(tilt, places, tilts.T, weight)
    image = propagate(tilt, whole, *tables)

    rows = jnp.broadcast_to(image.reshape(1, K, 2, K), (pairs, K, 2, K)).reshape(pairs * K, 2, K)
    block = lax.all_to_all(rows, ("pair", "beam"), 0, 0, tiled=True).reshape(2 * pairs * beams, K)
    mine, other = probe(block, coef, configs)
    return mine + lax.ppermute(other, "core", [(0, 1), (1, 0)])


def solution(mesh):
    fine = jax.sharding.Mesh(mesh.devices.reshape(-1, 2, 2), ("beam", "pair", "core"))
    nx, run = 4, mesh.devices.shape[0] // 4
    near = [[x * run + i for i in (range(run) if 2 * x < nx else reversed(range(run)))] for x in range(nx)]
    order = [*range(nx // 2), *reversed(range(nx // 2, nx))]
    far = [[x * run + i for x in order] for i in range(run)]
    return jax.shard_map(
        functools.partial(per_device, (near, far)),
        mesh=fine,
        in_specs=(P(("pair", "core"), None, "beam"), P(), P(), P()),
        out_specs=P(("pair", "core"), "beam"),
        check_vma=False,
    )
```

```python
import functools
import math

import jax
import jax.numpy as jnp
from jax import lax
from jax.experimental import pallas as pl
from jax.experimental.pallas import tpu as pltpu
from jax.sharding import PartitionSpec as P

G = 256
K = 128
SLICES = 3
LIMIT = (G // 3) ** 2
REACH = G // 3
ROWS = 176
CUBE, REST = 8, 16
PIECE = SLICES * 4

FRESNEL_RATE = 0.00019
DEFOCUS_RATE = 0.01

F32 = jnp.float32
BF16 = jnp.bfloat16


def split(value):
    high = value.astype(BF16)
    return high, (value - high.astype(F32)).astype(BF16)


def sine_of(t):
    s = t * t
    sine = jnp.full_like(t, 2.60501958e-6)
    for term in (-1.9808983e-4, 8.33304978e-3, -1.66666579e-1, 0.999999996):
        sine = sine * s + term
    return sine * t


def cosine_of(t):
    s = t * t
    cosine = jnp.full_like(t, 2.31515759e-5)
    for term in (-1.38535979e-3, 4.16635698e-2, -0.499999047, 0.999999953):
        cosine = cosine * s + term
    return cosine


def half_angle(steps, length):
    near = ((steps + length // 2) & (length - 1)) - length // 2
    return near.astype(F32) * (math.pi / length)


def cosine_step(steps, length):
    sine = sine_of(half_angle(steps, length))
    return 1.0 - 2.0 * sine * sine


def circle(steps, length):
    half = half_angle(steps, length)
    sine = sine_of(half)
    return 2.0 * sine * cosine_of(half), 1.0 - 2.0 * sine * sine


def iota(shape, axis):
    return lax.broadcasted_iota(jnp.int32, shape, axis)


def natural(place):
    return place


def mixed(place):
    n = place >> 6
    for source, target in ((5, 5), (4, 2), (3, 0), (2, 4), (1, 3), (0, 1)):
        n = n + (((place >> source) & 1) << (target + 1))
    return n


def position(place, order):
    n = order(place & (G // 2 - 1))
    return jnp.where(place < G // 2, n, G - 1 - n)


def folded(order, axis):
    place = iota((8, G) if axis else (G, K), axis)
    factor = 2 * order(place & (G // 2 - 1)) + 1
    return factor, jnp.where(place < G // 2, 0, -(G // 2))


def spread(value, shape):
    for axis in range(2):
        times = shape[axis] // value.shape[axis]
        if times > 1:
            value = jnp.concatenate([value] * times, axis=axis)
    return value


def signed(index, length):
    return jnp.where(index < length // 2, index, index - length)


def forward_table(shape, frequency, order, axis):
    factor, offset = (spread(value, shape) for value in folded(order, axis))
    return cosine_step(frequency(iota(shape, 1 - axis)) * factor + offset, 2 * G)


def fresnel(shape, frequency_u, frequency_v):
    u, v = frequency_u(iota(shape, 0)), frequency_v(iota(shape, 1))
    square = u * u + v * v
    angle = jnp.minimum(square, LIMIT).astype(F32) * FRESNEL_RATE
    keep = jnp.where(square <= LIMIT, 1.0 / (G * G), 0.0)
    return cosine_of(angle) * keep, -sine_of(angle) * keep


def copies_kernel(potential_ref, out_ref):
    values = potential_ref[0]
    pick = iota((K, K), 0) + iota((K, K), 1) == K - 1
    mirror = jnp.where(pick, 1.0, 0.0)
    quarters = [values[:, K * i : K * (i + 1)] for i in range(4)]
    for i in (1, 3):
        quarters[i] = jnp.dot(
            quarters[i], mirror, precision=lax.Precision.HIGHEST, preferred_element_type=F32
        )
    pieces = [
        jnp.concatenate([quarter[layer : layer + 1] for quarter in quarters], axis=0)[None]
        for layer in range(SLICES)
    ]
    out_ref[...] = jnp.concatenate(pieces * (out_ref.shape[0] // SLICES), axis=0)


AHEAD_LEFT = (0, ROWS, G)
AHEAD_RIGHT = (AHEAD_LEFT[0] + AHEAD_LEFT[1], G, G)
BACK_RIGHT = (AHEAD_RIGHT[0] + G, G, G)
BACK_LEFT = (BACK_RIGHT[0] + G, G, G)
CROP_LEFT = (BACK_LEFT[0] + G, K, G)
IMAGE_RIGHT = (CROP_LEFT[0] + K, K, 2 * K)
IMAGE_LEFT = (IMAGE_RIGHT[0] + K, 2 * K, 2 * K)
TABLE_ROWS = IMAGE_LEFT[0] + IMAGE_LEFT[1]

def terms(ref, where):
    row, rows, columns = where
    return ref[row : row + rows, :columns], ref[row : row + rows, G : G + columns]


def near(index):
    return index - ROWS // 2


def whole(index):
    return signed(index, G)


def centred(index):
    return index - K // 2


def prepare_kernel(
    tilt_ref, places_ref, tilts_ref, weight_ref, coef_ref, table_ref, factor_ref, across_ref
):
    across_ref[0], across_ref[1] = circle(tilt_ref[0] * position(iota((G, K), 0), mixed), G)
    factor_ref[0], factor_ref[1] = fresnel((ROWS, G), near, whole)

    probes = places_ref.shape[0]
    beams = tilts_ref.shape[1]
    steps = places_ref[:, 0:1] * tilts_ref[0:1, :] + places_ref[:, 1:2] * tilts_ref[1:2, :]
    sine, cosine = circle(-steps, K)
    weight_re, weight_im = weight_ref[0:1, :], weight_ref[1:2, :]
    coef_ref[0] = cosine * weight_re - sine * weight_im
    coef_ref[1] = cosine * weight_im + sine * weight_re

    m, other = iota((2 * K, 2 * K), 0), iota((2 * K, 2 * K), 1)
    turn = (4 * (m >> 1) + 1) * centred(other & (K - 1)) + K * ((other >> 7) - (m & 1))
    left, right = iota((K, 2 * K), 0), iota((K, 2 * K), 1)
    for (row, rows, columns), table in (
        (AHEAD_LEFT, forward_table((ROWS, G), near, mixed, 1)),
        (AHEAD_RIGHT, forward_table((G, G), whole, natural, 0)),
        (BACK_RIGHT, forward_table((G, G), whole, natural, 1)),
        (BACK_LEFT, forward_table((G, G), near, mixed, 0)),
        (CROP_LEFT, forward_table((K, G), centred, mixed, 1)),
        (IMAGE_RIGHT, cosine_step(signed(left, K) * (4 * (right & (K - 1)) + 1) - K * (right >> 7), 2 * G)),
        (IMAGE_LEFT, cosine_step(turn, 2 * G)),
    ):
        high, low = split(table)
        table_ref[row : row + rows, :columns] = high
        table_ref[row : row + rows, G : G + columns] = low


def from_left(table, field):
    high, low = split(field)
    short = table[0].shape[1] - field.shape[0]
    if short:
        none = jnp.zeros((short, field.shape[1]), BF16)
        high, low = jnp.concatenate([high, none], axis=0), jnp.concatenate([low, none], axis=0)
    return jnp.dot(
        jnp.concatenate([table[0], table[0], table[1]], axis=1),
        jnp.concatenate([high, low, high], axis=0),
        preferred_element_type=F32,
    )


def from_right(field, table):
    high, low = split(field)
    return jnp.dot(
        jnp.concatenate([high, low, high], axis=1),
        jnp.concatenate([table[0], table[0], table[1]], axis=0),
        preferred_element_type=F32,
    )


def halves(value, axis):
    half = value.shape[axis] // 2
    return lax.slice_in_dim(value, 0, half, axis=axis), lax.slice_in_dim(value, half, 2 * half, axis=axis)


def fold(real, imag, axis):
    real_ahead, real_back = halves(real, axis)
    imag_ahead, imag_back = halves(imag, axis)
    return (
        jnp.concatenate([real_ahead + real_back, imag_ahead - imag_back], axis=axis),
        jnp.concatenate([imag_ahead + imag_back, real_back - real_ahead], axis=axis),
    )


def unfold(real, imag, axis):
    real_even, real_odd = halves(real, axis)
    imag_even, imag_odd = halves(imag, axis)
    return (
        jnp.concatenate([real_even - imag_odd, real_even + imag_odd], axis=axis),
        jnp.concatenate([imag_even + real_odd, imag_even - real_odd], axis=axis),
    )


def spectrum(real, imag, left, right, factor):
    field = from_left(left, jnp.concatenate(fold(real, imag, 0), axis=1))
    field = jnp.concatenate(fold(*halves(field, 1), 1), axis=0)
    real, imag = halves(from_right(field, right), 0)
    return (
        real * factor[0] - imag * factor[1],
        real * factor[1] + imag * factor[0],
    )


def screened(real, imag, potential_ref, layer):
    def rows(half, parity, side):
        places = [
            (CUBE - 1 - k if half else k) * REST + (REST // 2 if half else 0) for k in range(CUBE)
        ]
        own = 4 * layer + 2 * (1 - parity if half else parity) + side
        return jnp.concatenate(
            [potential_ref[pl.ds(PIECE * place + own, REST // 2, PIECE), :] for place in places], axis=0
        )

    potential = jnp.concatenate(
        [
            jnp.concatenate([rows(half, parity, side) for side in range(2)], axis=1)
            for half in range(2)
            for parity in range(2)
        ],
        axis=0,
    )
    turned = potential - math.pi / 2
    sine, cosine = cosine_of(turned), sine_of(turned)
    return -(real * cosine + imag * sine), real * sine - imag * cosine


def plane_wave(across_ref, tilt_y):
    sine_x, cosine_x = (jnp.concatenate([across_ref[i]] * (G // K), axis=1) for i in range(2))
    sine_y, cosine_y = circle(tilt_y * position(iota((8, G), 1), natural), G)
    sine_y, cosine_y = (jnp.concatenate([value] * (G // 8), axis=0) for value in (sine_y, cosine_y))
    return cosine_x * cosine_y - sine_x * sine_y, sine_x * cosine_y + cosine_x * sine_y


def band_of(value):
    return jnp.where(iota((value.shape[0], K), 1) < K // 2, value[:, :K], value[:, K:])


def propagate_kernel(tilt_ref, potential_ref, table_ref, factor_ref, across_ref, out_ref):
    table = functools.partial(terms, table_ref)
    real, imag = plane_wave(across_ref, tilt_ref[1])
    for layer in range(SLICES - 1):
        real, imag = screened(real, imag, potential_ref, layer)
        real, imag = spectrum(real, imag, table(AHEAD_LEFT), table(AHEAD_RIGHT), factor_ref)
        field = from_right(jnp.concatenate([real, imag], axis=0), table(BACK_RIGHT))
        field = jnp.concatenate(unfold(*halves(field, 0), 1), axis=1)
        real, imag = unfold(*halves(from_left(table(BACK_LEFT), field), 1), 0)
    crop_right = [band_of(term) for term in table(AHEAD_RIGHT)]
    first = (ROWS - K) // 2
    crop_factor = [band_of(factor_ref[i, first : first + K, :]) for i in range(2)]
    real, imag = screened(real, imag, potential_ref, SLICES - 1)
    real, imag = spectrum(real, imag, table(CROP_LEFT), crop_right, crop_factor)
    product = from_right(jnp.concatenate([real, imag], axis=0), table(IMAGE_RIGHT))
    real = product[:K, :K] - product[K:, K:]
    imag = product[:K, K:] + product[K:, :K]
    out_ref[...] = from_left(table(IMAGE_LEFT), jnp.concatenate([real, imag], axis=0))


def probe_kernel(configs, block_ref, coef_ref, mine_ref, other_ref):
    here = block_ref.shape[0] // (2 * K)
    field = jnp.concatenate(
        [
            jnp.concatenate(
                [block_ref[pl.ds(2 * K * config + part, K, 2), :] for part in range(2)], axis=0
            )
            for config in range(here)
        ],
        axis=1,
    )
    real, imag = coef_ref[0], coef_ref[1]
    table = jnp.concatenate(
        [jnp.concatenate([real, -imag], axis=1), jnp.concatenate([imag, real], axis=1)], axis=0
    )
    waves = from_left(split(table), field)
    probes = waves.shape[0] // 2
    real, imag = waves[:probes], waves[probes:]
    power = real * real + imag * imag
    total = sum(power[:, K * config : K * config + K] for config in range(here)) * (1.0 / configs)
    mine_ref[...] = total[: probes // 2]
    other_ref[...] = total[probes // 2 :]


VMEM = pl.BlockSpec(memory_space=pltpu.VMEM)
SMEM = pl.BlockSpec(memory_space=pltpu.SMEM)
PARAMS = pltpu.CompilerParams(vmem_limit_bytes=24 * 1024 * 1024)


def shape_of(dtype, *shape):
    return jax.ShapeDtypeStruct(shape, dtype)


def prepare(tilt, places, tilts, weight):
    out = [
        shape_of(F32, 2, places.shape[0], tilts.shape[1]),
        shape_of(BF16, TABLE_ROWS, 2 * G),
        shape_of(F32, 2, ROWS, G),
        shape_of(F32, 2, G, K),
    ]
    return pl.pallas_call(
        prepare_kernel,
        out_shape=out,
        in_specs=[SMEM] + [VMEM] * 3,
        out_specs=[VMEM] * len(out),
        compiler_params=PARAMS,
        name="prepare",
    )(tilt, places, tilts, weight)


def propagate(*operands):
    return pl.pallas_call(
        propagate_kernel,
        out_shape=shape_of(F32, 2 * K, K),
        in_specs=[SMEM] + [VMEM] * (len(operands) - 1),
        out_specs=VMEM,
        compiler_params=PARAMS,
        name="propagate",
    )(*operands)


def probe(block, coef, configs):
    quarter = coef.shape[1] // 2
    return pl.pallas_call(
        functools.partial(probe_kernel, configs),
        out_shape=[shape_of(F32, quarter, K)] * 2,
        in_specs=[VMEM] * 2,
        out_specs=[VMEM] * 2,
        compiler_params=PARAMS,
        name="probe",
    )(block, coef)


def copies_of(potential, count):
    return pl.pallas_call(
        copies_kernel,
        out_shape=shape_of(F32, count * SLICES, 4, K),
        in_specs=[VMEM],
        out_specs=VMEM,
        compiler_params=PARAMS,
        name="copies",
    )(potential)


def per_device(groups, potential, tilts, aperture, positions):
    far, near = groups
    devices = lax.axis_size("beam")
    pairs, cores = lax.axis_size("pair"), lax.axis_size("core")
    configs = pairs * cores
    beams = tilts.shape[0]
    quarter = positions.shape[0] // configs
    own = lax.axis_index("beam")
    slab = lax.axis_index(("pair", "core"))

    part = lax.all_to_all(copies_of(potential, REST), "beam", 0, 0, axis_index_groups=far, tiled=True)
    part, tilts, aperture, positions = lax.optimization_barrier((part, tilts, aperture, positions))
    part = part.reshape(REST * PIECE, K)
    whole = lax.all_to_all(
        jnp.broadcast_to(part[None], (CUBE, *part.shape)), "beam", 0, 0, axis_index_groups=near
    ).reshape(devices * PIECE, K)

    places = positions.reshape(configs, quarter, 2)
    places = jnp.concatenate([places[slab], places[slab ^ 1]], axis=0)
    square = (tilts[:, 0] ** 2 + tilts[:, 1] ** 2).astype(F32)
    amount = aperture.astype(F32) * (1.0 / math.sqrt(beams))
    weight = jnp.stack([jnp.cos(DEFOCUS_RATE * square) * amount, -jnp.sin(DEFOCUS_RATE * square) * amount])
    tilt = lax.dynamic_index_in_dim(tilts, own, 0, keepdims=False)
    coef, *tables = prepare(tilt, places, tilts.T, weight)
    image = propagate(tilt, whole, *tables)

    rows = jnp.broadcast_to(image.reshape(1, K, 2, K), (pairs, K, 2, K)).reshape(pairs * K, 2, K)
    block = lax.all_to_all(rows, ("pair", "beam"), 0, 0, tiled=True).reshape(2 * pairs * beams, K)
    mine, other = probe(block, coef, configs)
    return mine + lax.ppermute(other, "core", [(0, 1), (1, 0)])


def spread_bits(value, targets):
    return sum(((value >> source) & 1) << target for source, target in enumerate(reversed(targets)))


def exchange_groups():
    low, high = (5, 2, 0), (4, 3, 1)
    half = range(REST // 2)
    far = [
        [spread_bits(k, low) + spread_bits(j, high) for j in half]
        + [64 + spread_bits(k, low) + spread_bits(j, high) for j in reversed(half)]
        for k in range(CUBE)
    ]
    near = [
        [top + spread_bits(k, low) + spread_bits(j, high) for k in range(CUBE)]
        for top in (0, 64)
        for j in half
    ]
    return far, near


def solution(mesh):
    fine = jax.sharding.Mesh(mesh.devices.reshape(-1, 2, 2), ("beam", "pair", "core"))
    return jax.shard_map(
        functools.partial(per_device, exchange_groups()),
        mesh=fine,
        in_specs=(P(("pair", "core"), None, "beam"), P(), P(), P()),
        out_specs=P(("pair", "core"), "beam"),
        check_vma=False,
    )
```

```python
import functools
import math

import jax
import jax.numpy as jnp
from jax import lax
from jax.experimental import pallas as pl
from jax.experimental.pallas import tpu as pltpu
from jax.sharding import PartitionSpec as P

G = 256
K = 128
SLICES = 3
LIMIT = (G // 3) ** 2
REACH = G // 3
ROWS = 176
CUBE, REST = 8, 16
PIECE = SLICES * 4

FRESNEL_RATE = 0.00019
DEFOCUS_RATE = 0.01

F32 = jnp.float32
BF16 = jnp.bfloat16


def split(value):
    high = value.astype(BF16)
    return high, (value - high.astype(F32)).astype(BF16)


def sine_of(t):
    s = t * t
    sine = jnp.full_like(t, 2.60501958e-6)
    for term in (-1.9808983e-4, 8.33304978e-3, -1.66666579e-1, 0.999999996):
        sine = sine * s + term
    return sine * t


def cosine_of(t):
    s = t * t
    cosine = jnp.full_like(t, 2.31515759e-5)
    for term in (-1.38535979e-3, 4.16635698e-2, -0.499999047, 0.999999953):
        cosine = cosine * s + term
    return cosine


def half_angle(steps, length):
    near = ((steps + length // 2) & (length - 1)) - length // 2
    return near.astype(F32) * (math.pi / length)


def cosine_step(steps, length):
    sine = sine_of(half_angle(steps, length))
    return 1.0 - 2.0 * sine * sine


def circle(steps, length):
    half = half_angle(steps, length)
    sine = sine_of(half)
    return 2.0 * sine * cosine_of(half), 1.0 - 2.0 * sine * sine


def iota(shape, axis):
    return lax.broadcasted_iota(jnp.int32, shape, axis)


def natural(place):
    return place


def mixed(place):
    n = place >> 6
    for source, target in ((5, 5), (4, 2), (3, 0), (2, 4), (1, 3), (0, 1)):
        n = n + (((place >> source) & 1) << (target + 1))
    return n


def position(place, order):
    n = order(place & (G // 2 - 1))
    return jnp.where(place < G // 2, n, G - 1 - n)


def folded(order, axis):
    place = iota((8, G) if axis else (G, K), axis)
    factor = 2 * order(place & (G // 2 - 1)) + 1
    return factor, jnp.where(place < G // 2, 0, -(G // 2))


def spread(value, shape):
    for axis in range(2):
        times = shape[axis] // value.shape[axis]
        if times > 1:
            value = jnp.concatenate([value] * times, axis=axis)
    return value


def signed(index, length):
    return jnp.where(index < length // 2, index, index - length)


def forward_table(shape, frequency, order, axis):
    factor, offset = (spread(value, shape) for value in folded(order, axis))
    return cosine_step(frequency(iota(shape, 1 - axis)) * factor + offset, 2 * G)


def fresnel(shape, frequency_u, frequency_v):
    u, v = frequency_u(iota(shape, 0)), frequency_v(iota(shape, 1))
    square = u * u + v * v
    angle = jnp.minimum(square, LIMIT).astype(F32) * FRESNEL_RATE
    keep = jnp.where(square <= LIMIT, 1.0 / (G * G), 0.0)
    return cosine_of(angle) * keep, -sine_of(angle) * keep


def copies_kernel(potential_ref, out_ref):
    values = potential_ref[0]
    pick = iota((K, K), 0) + iota((K, K), 1) == K - 1
    mirror = jnp.where(pick, 1.0, 0.0)
    quarters = [values[:, K * i : K * (i + 1)] for i in range(4)]
    for i in (1, 3):
        quarters[i] = jnp.dot(
            quarters[i], mirror, precision=lax.Precision.HIGHEST, preferred_element_type=F32
        )
    pieces = [
        jnp.concatenate([quarter[layer : layer + 1] for quarter in quarters], axis=0)[None]
        for layer in range(SLICES)
    ]
    out_ref[...] = jnp.concatenate(pieces * (out_ref.shape[0] // SLICES), axis=0)


AHEAD_LEFT = (0, ROWS, G)
AHEAD_RIGHT = (AHEAD_LEFT[0] + AHEAD_LEFT[1], G, G)
BACK_RIGHT = (AHEAD_RIGHT[0] + G, G, G)
BACK_LEFT = (BACK_RIGHT[0] + G, G, G)
CROP_LEFT = (BACK_LEFT[0] + G, K, G)
IMAGE_RIGHT = (CROP_LEFT[0] + K, K, 2 * K)
IMAGE_LEFT = (IMAGE_RIGHT[0] + K, 2 * K, 2 * K)
TABLE_ROWS = IMAGE_LEFT[0] + IMAGE_LEFT[1]

def terms(ref, where):
    row, rows, columns = where
    return ref[row : row + rows, :columns], ref[row : row + rows, G : G + columns]


def near(index):
    return index - ROWS // 2


def whole(index):
    return signed(index, G)


def centred(index):
    return index - K // 2


def prepare_kernel(
    tilt_ref, places_ref, tilts_ref, weight_ref, coef_ref, table_ref, factor_ref, across_ref
):
    across_ref[0], across_ref[1] = circle(tilt_ref[0] * position(iota((G, K), 0), mixed), G)
    factor_ref[0], factor_ref[1] = fresnel((ROWS, G), near, whole)

    probes = places_ref.shape[0]
    beams = tilts_ref.shape[1]
    steps = places_ref[:, 0:1] * tilts_ref[0:1, :] + places_ref[:, 1:2] * tilts_ref[1:2, :]
    sine, cosine = circle(-steps, K)
    weight_re, weight_im = weight_ref[0:1, :], weight_ref[1:2, :]
    coef_ref[0] = cosine * weight_re - sine * weight_im
    coef_ref[1] = cosine * weight_im + sine * weight_re

    m, other = iota((2 * K, 2 * K), 0), iota((2 * K, 2 * K), 1)
    turn = (4 * (m >> 1) + 1) * centred(other & (K - 1)) + K * ((other >> 7) - (m & 1))
    left, right = iota((K, 2 * K), 0), iota((K, 2 * K), 1)
    for (row, rows, columns), table in (
        (AHEAD_LEFT, forward_table((ROWS, G), near, mixed, 1)),
        (AHEAD_RIGHT, forward_table((G, G), whole, natural, 0)),
        (BACK_RIGHT, forward_table((G, G), whole, natural, 1)),
        (BACK_LEFT, forward_table((G, G), near, mixed, 0)),
        (CROP_LEFT, forward_table((K, G), centred, mixed, 1)),
        (IMAGE_RIGHT, cosine_step(signed(left, K) * (4 * (right & (K - 1)) + 1) - K * (right >> 7), 2 * G)),
        (IMAGE_LEFT, cosine_step(turn, 2 * G)),
    ):
        high, low = split(table)
        table_ref[row : row + rows, :columns] = high
        table_ref[row : row + rows, G : G + columns] = low


def from_left(table, field):
    high, low = split(field)
    short = table[0].shape[1] - field.shape[0]
    if short:
        none = jnp.zeros((short, field.shape[1]), BF16)
        high, low = jnp.concatenate([high, none], axis=0), jnp.concatenate([low, none], axis=0)
    return jnp.dot(
        jnp.concatenate([table[0], table[0], table[1]], axis=1),
        jnp.concatenate([high, low, high], axis=0),
        preferred_element_type=F32,
    )


def from_right(field, table):
    high, low = split(field)
    return jnp.dot(
        jnp.concatenate([high, low, high], axis=1),
        jnp.concatenate([table[0], table[0], table[1]], axis=0),
        preferred_element_type=F32,
    )


def halves(value, axis):
    half = value.shape[axis] // 2
    return lax.slice_in_dim(value, 0, half, axis=axis), lax.slice_in_dim(value, half, 2 * half, axis=axis)


def fold(real, imag, axis):
    real_ahead, real_back = halves(real, axis)
    imag_ahead, imag_back = halves(imag, axis)
    return (
        jnp.concatenate([real_ahead + real_back, imag_ahead - imag_back], axis=axis),
        jnp.concatenate([imag_ahead + imag_back, real_back - real_ahead], axis=axis),
    )


def unfold(real, imag, axis):
    real_even, real_odd = halves(real, axis)
    imag_even, imag_odd = halves(imag, axis)
    return (
        jnp.concatenate([real_even - imag_odd, real_even + imag_odd], axis=axis),
        jnp.concatenate([imag_even + real_odd, imag_even - real_odd], axis=axis),
    )


def spectrum(real, imag, left, right, factor):
    field = from_left(left, jnp.concatenate(fold(real, imag, 0), axis=1))
    field = jnp.concatenate(fold(*halves(field, 1), 1), axis=0)
    real, imag = halves(from_right(field, right), 0)
    return (
        real * factor[0] - imag * factor[1],
        real * factor[1] + imag * factor[0],
    )


def screened(real, imag, potential_ref, layer):
    def rows(half, parity, side):
        places = [
            (CUBE - 1 - k if half else k) * REST + (REST // 2 if half else 0) for k in range(CUBE)
        ]
        own = 4 * layer + 2 * (1 - parity if half else parity) + side
        return jnp.concatenate(
            [potential_ref[pl.ds(PIECE * place + own, REST // 2, PIECE), :] for place in places], axis=0
        )

    potential = jnp.concatenate(
        [
            jnp.concatenate([rows(half, parity, side) for side in range(2)], axis=1)
            for half in range(2)
            for parity in range(2)
        ],
        axis=0,
    )
    turned = potential - math.pi / 2
    sine, cosine = cosine_of(turned), sine_of(turned)
    return -(real * cosine + imag * sine), real * sine - imag * cosine


def plane_wave(across_ref, tilt_y):
    sine_x, cosine_x = (jnp.concatenate([across_ref[i]] * (G // K), axis=1) for i in range(2))
    sine_y, cosine_y = circle(tilt_y * position(iota((8, G), 1), natural), G)
    sine_y, cosine_y = (jnp.concatenate([value] * (G // 8), axis=0) for value in (sine_y, cosine_y))
    return cosine_x * cosine_y - sine_x * sine_y, sine_x * cosine_y + cosine_x * sine_y


def band_of(value):
    return jnp.where(iota((value.shape[0], K), 1) < K // 2, value[:, :K], value[:, K:])


def propagate_kernel(tilt_ref, potential_ref, table_ref, factor_ref, across_ref, out_ref):
    table = functools.partial(terms, table_ref)
    real, imag = plane_wave(across_ref, tilt_ref[1])
    for layer in range(SLICES - 1):
        real, imag = screened(real, imag, potential_ref, layer)
        real, imag = spectrum(real, imag, table(AHEAD_LEFT), table(AHEAD_RIGHT), factor_ref)
        field = from_right(jnp.concatenate([real, imag], axis=0), table(BACK_RIGHT))
        field = jnp.concatenate(unfold(*halves(field, 0), 1), axis=1)
        real, imag = unfold(*halves(from_left(table(BACK_LEFT), field), 1), 0)
    crop_right = [band_of(term) for term in table(AHEAD_RIGHT)]
    first = (ROWS - K) // 2
    crop_factor = [band_of(factor_ref[i, first : first + K, :]) for i in range(2)]
    real, imag = screened(real, imag, potential_ref, SLICES - 1)
    real, imag = spectrum(real, imag, table(CROP_LEFT), crop_right, crop_factor)
    product = from_right(jnp.concatenate([real, imag], axis=0), table(IMAGE_RIGHT))
    real = product[:K, :K] - product[K:, K:]
    imag = product[:K, K:] + product[K:, :K]
    out_ref[...] = from_left(table(IMAGE_LEFT), jnp.concatenate([real, imag], axis=0))


def probe_kernel(configs, block_ref, coef_ref, mine_ref, other_ref):
    here = block_ref.shape[0] // (2 * K)
    field = jnp.concatenate(
        [
            jnp.concatenate(
                [block_ref[pl.ds(2 * K * config + part, K, 2), :] for part in range(2)], axis=0
            )
            for config in range(here)
        ],
        axis=1,
    )
    real, imag = coef_ref[0], coef_ref[1]
    table = jnp.concatenate(
        [jnp.concatenate([real, -imag], axis=1), jnp.concatenate([imag, real], axis=1)], axis=0
    )
    waves = from_left(split(table), field)
    probes = waves.shape[0] // 2
    real, imag = waves[:probes], waves[probes:]
    power = real * real + imag * imag
    total = sum(power[:, K * config : K * config + K] for config in range(here)) * (1.0 / configs)
    mine_ref[...] = total[: probes // 2]
    other_ref[...] = total[probes // 2 :]


VMEM = pl.BlockSpec(memory_space=pltpu.VMEM)
SMEM = pl.BlockSpec(memory_space=pltpu.SMEM)
PARAMS = pltpu.CompilerParams(vmem_limit_bytes=24 * 1024 * 1024)


def shape_of(dtype, *shape):
    return jax.ShapeDtypeStruct(shape, dtype)


def prepare(tilt, places, tilts, weight):
    out = [
        shape_of(F32, 2, places.shape[0], tilts.shape[1]),
        shape_of(BF16, TABLE_ROWS, 2 * G),
        shape_of(F32, 2, ROWS, G),
        shape_of(F32, 2, G, K),
    ]
    return pl.pallas_call(
        prepare_kernel,
        out_shape=out,
        in_specs=[SMEM] + [VMEM] * 3,
        out_specs=[VMEM] * len(out),
        compiler_params=PARAMS,
        name="prepare",
    )(tilt, places, tilts, weight)


def propagate(*operands):
    return pl.pallas_call(
        propagate_kernel,
        out_shape=shape_of(F32, 2 * K, K),
        in_specs=[SMEM] + [VMEM] * (len(operands) - 1),
        out_specs=VMEM,
        compiler_params=PARAMS,
        name="propagate",
    )(*operands)


def probe(block, coef, configs):
    quarter = coef.shape[1] // 2
    return pl.pallas_call(
        functools.partial(probe_kernel, configs),
        out_shape=[shape_of(F32, quarter, K)] * 2,
        in_specs=[VMEM] * 2,
        out_specs=[VMEM] * 2,
        compiler_params=PARAMS,
        name="probe",
    )(block, coef)


def copies_of(potential, count):
    return pl.pallas_call(
        copies_kernel,
        out_shape=shape_of(F32, count * SLICES, 4, K),
        in_specs=[VMEM],
        out_specs=VMEM,
        compiler_params=PARAMS,
        name="copies",
    )(potential)


def per_device(groups, potential, tilts, aperture, positions):
    devices = lax.axis_size("beam")
    pairs, cores = lax.axis_size("pair"), lax.axis_size("core")
    configs = pairs * cores
    beams = tilts.shape[0]
    quarter = positions.shape[0] // configs
    own = lax.axis_index("beam")
    slab = lax.axis_index(("pair", "core"))

    pieces = lax.all_to_all(
        copies_of(potential, devices), "beam", 0, 0, axis_index_groups=groups, tiled=True
    )
    whole = pieces.reshape(devices * PIECE, K)

    places = positions.reshape(configs, quarter, 2)
    places = jnp.concatenate([places[slab], places[slab ^ 1]], axis=0)
    square = (tilts[:, 0] ** 2 + tilts[:, 1] ** 2).astype(F32)
    amount = aperture.astype(F32) * (1.0 / math.sqrt(beams))
    weight = jnp.stack([jnp.cos(DEFOCUS_RATE * square) * amount, -jnp.sin(DEFOCUS_RATE * square) * amount])
    tilt = lax.dynamic_index_in_dim(tilts, own, 0, keepdims=False)
    coef, *tables = prepare(tilt, places, tilts.T, weight)
    image = propagate(tilt, whole, *tables)

    rows = jnp.broadcast_to(image.reshape(1, K, 2, K), (pairs, K, 2, K)).reshape(pairs * K, 2, K)
    block = lax.all_to_all(rows, ("pair", "beam"), 0, 0, tiled=True).reshape(2 * pairs * beams, K)
    mine, other = probe(block, coef, configs)
    return mine + lax.ppermute(other, "core", [(0, 1), (1, 0)])


def spread_bits(value, targets):
    return sum(((value >> source) & 1) << target for source, target in enumerate(reversed(targets)))


def exchange_groups():
    low, high = (5, 2, 0), (4, 3, 1)
    half = range(REST // 2)
    far = [
        [spread_bits(k, low) + spread_bits(j, high) for j in half]
        + [64 + spread_bits(k, low) + spread_bits(j, high) for j in reversed(half)]
        for k in range(CUBE)
    ]
    return [sum(far, [])]


def solution(mesh):
    fine = jax.sharding.Mesh(mesh.devices.reshape(-1, 2, 2), ("beam", "pair", "core"))
    return jax.shard_map(
        functools.partial(per_device, exchange_groups()),
        mesh=fine,
        in_specs=(P(("pair", "core"), None, "beam"), P(), P(), P()),
        out_specs=P(("pair", "core"), "beam"),
        check_vma=False,
    )
```

```python
import functools
import math

import jax
import jax.numpy as jnp
from jax import lax
from jax.experimental import pallas as pl
from jax.experimental.pallas import tpu as pltpu
from jax.sharding import PartitionSpec as P

G = 256
K = 128
SLICES = 3
LIMIT = (G // 3) ** 2
REACH = G // 3
ROWS = 176
CUBE, REST = 8, 16
PIECE = SLICES * 4

FRESNEL_RATE = 0.00019
DEFOCUS_RATE = 0.01

F32 = jnp.float32
BF16 = jnp.bfloat16


def split(value):
    high = value.astype(BF16)
    return high, (value - high.astype(F32)).astype(BF16)


def sine_of(t):
    s = t * t
    sine = jnp.full_like(t, 2.60501958e-6)
    for term in (-1.9808983e-4, 8.33304978e-3, -1.66666579e-1, 0.999999996):
        sine = sine * s + term
    return sine * t


def cosine_of(t):
    s = t * t
    cosine = jnp.full_like(t, 2.31515759e-5)
    for term in (-1.38535979e-3, 4.16635698e-2, -0.499999047, 0.999999953):
        cosine = cosine * s + term
    return cosine


def half_angle(steps, length):
    near = ((steps + length // 2) & (length - 1)) - length // 2
    return near.astype(F32) * (math.pi / length)


def cosine_step(steps, length):
    sine = sine_of(half_angle(steps, length))
    return 1.0 - 2.0 * sine * sine


def circle(steps, length):
    half = half_angle(steps, length)
    sine = sine_of(half)
    return 2.0 * sine * cosine_of(half), 1.0 - 2.0 * sine * sine


def iota(shape, axis):
    return lax.broadcasted_iota(jnp.int32, shape, axis)


def natural(place):
    return place


def mixed(place):
    n = place >> 6
    for source, target in ((5, 5), (4, 2), (3, 0), (2, 4), (1, 3), (0, 1)):
        n = n + (((place >> source) & 1) << (target + 1))
    return n


def position(place, order):
    n = order(place & (G // 2 - 1))
    return jnp.where(place < G // 2, n, G - 1 - n)


def folded(order, axis):
    place = iota((8, G) if axis else (G, K), axis)
    factor = 2 * order(place & (G // 2 - 1)) + 1
    return factor, jnp.where(place < G // 2, 0, -(G // 2))


def spread(value, shape):
    for axis in range(2):
        times = shape[axis] // value.shape[axis]
        if times > 1:
            value = jnp.concatenate([value] * times, axis=axis)
    return value


def signed(index, length):
    return jnp.where(index < length // 2, index, index - length)


def forward_table(shape, frequency, order, axis):
    factor, offset = (spread(value, shape) for value in folded(order, axis))
    return cosine_step(frequency(iota(shape, 1 - axis)) * factor + offset, 2 * G)


def fresnel(shape, frequency_u, frequency_v):
    u, v = frequency_u(iota(shape, 0)), frequency_v(iota(shape, 1))
    square = u * u + v * v
    angle = jnp.minimum(square, LIMIT).astype(F32) * FRESNEL_RATE
    keep = jnp.where(square <= LIMIT, 1.0 / (G * G), 0.0)
    return cosine_of(angle) * keep, -sine_of(angle) * keep


def copies_kernel(potential_ref, out_ref):
    values = potential_ref[0]
    pick = iota((K, K), 0) + iota((K, K), 1) == K - 1
    mirror = jnp.where(pick, 1.0, 0.0)
    quarters = [values[:, K * i : K * (i + 1)] for i in range(4)]
    for i in (1, 3):
        quarters[i] = jnp.dot(
            quarters[i], mirror, precision=lax.Precision.HIGHEST, preferred_element_type=F32
        )
    pieces = [
        jnp.concatenate([quarter[layer : layer + 1] for quarter in quarters], axis=0)[None]
        for layer in range(SLICES)
    ]
    out_ref[...] = jnp.concatenate(pieces * (out_ref.shape[0] // SLICES), axis=0)


AHEAD_LEFT = (0, ROWS, G)
AHEAD_RIGHT = (AHEAD_LEFT[0] + AHEAD_LEFT[1], G, G)
BACK_RIGHT = (AHEAD_RIGHT[0] + G, G, G)
BACK_LEFT = (BACK_RIGHT[0] + G, G, G)
CROP_LEFT = (BACK_LEFT[0] + G, K, G)
IMAGE_RIGHT = (CROP_LEFT[0] + K, K, 2 * K)
IMAGE_LEFT = (IMAGE_RIGHT[0] + K, 2 * K, 2 * K)
TABLE_ROWS = IMAGE_LEFT[0] + IMAGE_LEFT[1]

def terms(ref, where):
    row, rows, columns = where
    return ref[row : row + rows, :columns], ref[row : row + rows, G : G + columns]


def near(index):
    return index - ROWS // 2


def whole(index):
    return signed(index, G)


def centred(index):
    return index - K // 2


def prepare_kernel(
    tilt_ref, places_ref, tilts_ref, weight_ref, coef_ref, table_ref, factor_ref, across_ref
):
    across_ref[0], across_ref[1] = circle(tilt_ref[0] * position(iota((G, K), 0), mixed), G)
    factor_ref[0], factor_ref[1] = fresnel((ROWS, G), near, whole)

    probes = places_ref.shape[0]
    beams = tilts_ref.shape[1]
    steps = places_ref[:, 0:1] * tilts_ref[0:1, :] + places_ref[:, 1:2] * tilts_ref[1:2, :]
    sine, cosine = circle(-steps, K)
    weight_re, weight_im = weight_ref[0:1, :], weight_ref[1:2, :]
    coef_ref[0] = cosine * weight_re - sine * weight_im
    coef_ref[1] = cosine * weight_im + sine * weight_re

    m, other = iota((2 * K, 2 * K), 0), iota((2 * K, 2 * K), 1)
    turn = (4 * (m >> 1) + 1) * centred(other & (K - 1)) + K * ((other >> 7) - (m & 1))
    left, right = iota((K, 2 * K), 0), iota((K, 2 * K), 1)
    for (row, rows, columns), table in (
        (AHEAD_LEFT, forward_table((ROWS, G), near, mixed, 1)),
        (AHEAD_RIGHT, forward_table((G, G), whole, natural, 0)),
        (BACK_RIGHT, forward_table((G, G), whole, natural, 1)),
        (BACK_LEFT, forward_table((G, G), near, mixed, 0)),
        (CROP_LEFT, forward_table((K, G), centred, mixed, 1)),
        (IMAGE_RIGHT, cosine_step(signed(left, K) * (4 * (right & (K - 1)) + 1) - K * (right >> 7), 2 * G)),
        (IMAGE_LEFT, cosine_step(turn, 2 * G)),
    ):
        high, low = split(table)
        table_ref[row : row + rows, :columns] = high
        table_ref[row : row + rows, G : G + columns] = low


def from_left(table, field):
    high, low = split(field)
    short = table[0].shape[1] - field.shape[0]
    if short:
        none = jnp.zeros((short, field.shape[1]), BF16)
        high, low = jnp.concatenate([high, none], axis=0), jnp.concatenate([low, none], axis=0)
    return jnp.dot(
        jnp.concatenate([table[0], table[0], table[1]], axis=1),
        jnp.concatenate([high, low, high], axis=0),
        preferred_element_type=F32,
    )


def from_right(field, table):
    high, low = split(field)
    return jnp.dot(
        jnp.concatenate([high, low, high], axis=1),
        jnp.concatenate([table[0], table[0], table[1]], axis=0),
        preferred_element_type=F32,
    )


def halves(value, axis):
    half = value.shape[axis] // 2
    return lax.slice_in_dim(value, 0, half, axis=axis), lax.slice_in_dim(value, half, 2 * half, axis=axis)


def fold(real, imag, axis):
    real_ahead, real_back = halves(real, axis)
    imag_ahead, imag_back = halves(imag, axis)
    return (
        jnp.concatenate([real_ahead + real_back, imag_ahead - imag_back], axis=axis),
        jnp.concatenate([imag_ahead + imag_back, real_back - real_ahead], axis=axis),
    )


def unfold(real, imag, axis):
    real_even, real_odd = halves(real, axis)
    imag_even, imag_odd = halves(imag, axis)
    return (
        jnp.concatenate([real_even - imag_odd, real_even + imag_odd], axis=axis),
        jnp.concatenate([imag_even + real_odd, imag_even - real_odd], axis=axis),
    )


def spectrum(real, imag, left, right, factor):
    field = from_left(left, jnp.concatenate(fold(real, imag, 0), axis=1))
    field = jnp.concatenate(fold(*halves(field, 1), 1), axis=0)
    real, imag = halves(from_right(field, right), 0)
    return (
        real * factor[0] - imag * factor[1],
        real * factor[1] + imag * factor[0],
    )


def screened(real, imag, potential_ref, layer):
    def rows(half, parity, side):
        places = [
            (CUBE - 1 - k if half else k) * REST + (REST // 2 if half else 0) for k in range(CUBE)
        ]
        own = 4 * layer + 2 * (1 - parity if half else parity) + side
        return jnp.concatenate(
            [potential_ref[pl.ds(PIECE * place + own, REST // 2, PIECE), :] for place in places], axis=0
        )

    potential = jnp.concatenate(
        [
            jnp.concatenate([rows(half, parity, side) for side in range(2)], axis=1)
            for half in range(2)
            for parity in range(2)
        ],
        axis=0,
    )
    turned = potential - math.pi / 2
    sine, cosine = cosine_of(turned), sine_of(turned)
    return -(real * cosine + imag * sine), real * sine - imag * cosine


def plane_wave(across_ref, tilt_y):
    sine_x, cosine_x = (jnp.concatenate([across_ref[i]] * (G // K), axis=1) for i in range(2))
    sine_y, cosine_y = circle(tilt_y * position(iota((8, G), 1), natural), G)
    sine_y, cosine_y = (jnp.concatenate([value] * (G // 8), axis=0) for value in (sine_y, cosine_y))
    return cosine_x * cosine_y - sine_x * sine_y, sine_x * cosine_y + cosine_x * sine_y


def band_of(value):
    return jnp.where(iota((value.shape[0], K), 1) < K // 2, value[:, :K], value[:, K:])


def propagate_kernel(tilt_ref, potential_ref, table_ref, factor_ref, across_ref, out_ref):
    table = functools.partial(terms, table_ref)
    real, imag = plane_wave(across_ref, tilt_ref[1])
    for layer in range(SLICES - 1):
        real, imag = screened(real, imag, potential_ref, layer)
        real, imag = spectrum(real, imag, table(AHEAD_LEFT), table(AHEAD_RIGHT), factor_ref)
        field = from_right(jnp.concatenate([real, imag], axis=0), table(BACK_RIGHT))
        field = jnp.concatenate(unfold(*halves(field, 0), 1), axis=1)
        real, imag = unfold(*halves(from_left(table(BACK_LEFT), field), 1), 0)
    crop_right = [band_of(term) for term in table(AHEAD_RIGHT)]
    first = (ROWS - K) // 2
    crop_factor = [band_of(factor_ref[i, first : first + K, :]) for i in range(2)]
    real, imag = screened(real, imag, potential_ref, SLICES - 1)
    real, imag = spectrum(real, imag, table(CROP_LEFT), crop_right, crop_factor)
    product = from_right(jnp.concatenate([real, imag], axis=0), table(IMAGE_RIGHT))
    real = product[:K, :K] - product[K:, K:]
    imag = product[:K, K:] + product[K:, :K]
    out_ref[...] = from_left(table(IMAGE_LEFT), jnp.concatenate([real, imag], axis=0))


def probe_kernel(configs, block_ref, coef_ref, mine_ref, other_ref):
    here = block_ref.shape[0] // (2 * K)
    field = jnp.concatenate(
        [
            jnp.concatenate(
                [block_ref[pl.ds(2 * K * config + part, K, 2), :] for part in range(2)], axis=0
            )
            for config in range(here)
        ],
        axis=1,
    )
    real, imag = coef_ref[0], coef_ref[1]
    table = jnp.concatenate(
        [jnp.concatenate([real, -imag], axis=1), jnp.concatenate([imag, real], axis=1)], axis=0
    )
    waves = from_left(split(table), field)
    probes = waves.shape[0] // 2
    real, imag = waves[:probes], waves[probes:]
    power = real * real + imag * imag
    total = sum(power[:, K * config : K * config + K] for config in range(here)) * (1.0 / configs)
    mine_ref[...] = total[: probes // 2]
    other_ref[...] = total[probes // 2 :]


VMEM = pl.BlockSpec(memory_space=pltpu.VMEM)
SMEM = pl.BlockSpec(memory_space=pltpu.SMEM)
PARAMS = pltpu.CompilerParams(vmem_limit_bytes=24 * 1024 * 1024)


def shape_of(dtype, *shape):
    return jax.ShapeDtypeStruct(shape, dtype)


def prepare(tilt, places, tilts, weight):
    out = [
        shape_of(F32, 2, places.shape[0], tilts.shape[1]),
        shape_of(BF16, TABLE_ROWS, 2 * G),
        shape_of(F32, 2, ROWS, G),
        shape_of(F32, 2, G, K),
    ]
    return pl.pallas_call(
        prepare_kernel,
        out_shape=out,
        in_specs=[SMEM] + [VMEM] * 3,
        out_specs=[VMEM] * len(out),
        compiler_params=PARAMS,
        name="prepare",
    )(tilt, places, tilts, weight)


def propagate(*operands):
    return pl.pallas_call(
        propagate_kernel,
        out_shape=shape_of(F32, 2 * K, K),
        in_specs=[SMEM] + [VMEM] * (len(operands) - 1),
        out_specs=VMEM,
        compiler_params=PARAMS,
        name="propagate",
    )(*operands)


def probe(block, coef, configs):
    quarter = coef.shape[1] // 2
    return pl.pallas_call(
        functools.partial(probe_kernel, configs),
        out_shape=[shape_of(F32, quarter, K)] * 2,
        in_specs=[VMEM] * 2,
        out_specs=[VMEM] * 2,
        compiler_params=PARAMS,
        name="probe",
    )(block, coef)


def copies_of(potential, count):
    return pl.pallas_call(
        copies_kernel,
        out_shape=shape_of(F32, count * SLICES, 4, K),
        in_specs=[VMEM],
        out_specs=VMEM,
        compiler_params=PARAMS,
        name="copies",
    )(potential)


def per_device(groups, potential, tilts, aperture, positions):
    far, near = groups
    devices = lax.axis_size("beam")
    pairs, cores = lax.axis_size("pair"), lax.axis_size("core")
    configs = pairs * cores
    beams = tilts.shape[0]
    quarter = positions.shape[0] // configs
    own = lax.axis_index("beam")
    slab = lax.axis_index(("pair", "core"))

    part = lax.all_to_all(copies_of(potential, REST), "beam", 0, 0, axis_index_groups=far, tiled=True)

    places = positions.reshape(configs, quarter, 2)
    places = jnp.concatenate([places[slab], places[slab ^ 1]], axis=0)
    square = (tilts[:, 0] ** 2 + tilts[:, 1] ** 2).astype(F32)
    amount = aperture.astype(F32) * (1.0 / math.sqrt(beams))
    weight = jnp.stack([jnp.cos(DEFOCUS_RATE * square) * amount, -jnp.sin(DEFOCUS_RATE * square) * amount])
    tilt = lax.dynamic_index_in_dim(tilts, own, 0, keepdims=False)
    coef, *tables = prepare(tilt, places, tilts.T, weight)
    part, coef, *tables = lax.optimization_barrier((part, coef, *tables))
    part = part.reshape(REST * PIECE, K)
    whole = lax.all_to_all(
        jnp.broadcast_to(part[None], (CUBE, *part.shape)), "beam", 0, 0, axis_index_groups=near
    ).reshape(devices * PIECE, K)
    image = propagate(tilt, whole, *tables)

    rows = jnp.broadcast_to(image.reshape(1, K, 2, K), (pairs, K, 2, K)).reshape(pairs * K, 2, K)
    block = lax.all_to_all(rows, ("pair", "beam"), 0, 0, tiled=True).reshape(2 * pairs * beams, K)
    mine, other = probe(block, coef, configs)
    return mine + lax.ppermute(other, "core", [(0, 1), (1, 0)])


def spread_bits(value, targets):
    return sum(((value >> source) & 1) << target for source, target in enumerate(reversed(targets)))


def exchange_groups():
    low, high = (5, 2, 0), (4, 3, 1)
    half = range(REST // 2)
    far = [
        [spread_bits(k, low) + spread_bits(j, high) for j in half]
        + [64 + spread_bits(k, low) + spread_bits(j, high) for j in reversed(half)]
        for k in range(CUBE)
    ]
    near = [
        [top + spread_bits(k, low) + spread_bits(j, high) for k in range(CUBE)]
        for top in (0, 64)
        for j in half
    ]
    return far, near


def solution(mesh):
    fine = jax.sharding.Mesh(mesh.devices.reshape(-1, 2, 2), ("beam", "pair", "core"))
    return jax.shard_map(
        functools.partial(per_device, exchange_groups()),
        mesh=fine,
        in_specs=(P(("pair", "core"), None, "beam"), P(), P(), P()),
        out_specs=P(("pair", "core"), "beam"),
        check_vma=False,
    )
```

```python
import functools
import math

import jax
import jax.numpy as jnp
from jax import lax
from jax.experimental import pallas as pl
from jax.experimental.pallas import tpu as pltpu
from jax.sharding import PartitionSpec as P

G = 256
K = 128
SLICES = 3
LIMIT = (G // 3) ** 2
REACH = G // 3
ROWS = 176
CUBE, REST = 8, 16
PIECE = SLICES * 4

FRESNEL_RATE = 0.00019
DEFOCUS_RATE = 0.01

F32 = jnp.float32
BF16 = jnp.bfloat16


def split(value):
    high = value.astype(BF16)
    return high, (value - high.astype(F32)).astype(BF16)


def sine_of(t):
    s = t * t
    sine = jnp.full_like(t, 2.60501958e-6)
    for term in (-1.9808983e-4, 8.33304978e-3, -1.66666579e-1, 0.999999996):
        sine = sine * s + term
    return sine * t


def cosine_of(t):
    s = t * t
    cosine = jnp.full_like(t, 2.31515759e-5)
    for term in (-1.38535979e-3, 4.16635698e-2, -0.499999047, 0.999999953):
        cosine = cosine * s + term
    return cosine


def half_angle(steps, length):
    near = ((steps + length // 2) & (length - 1)) - length // 2
    return near.astype(F32) * (math.pi / length)


def cosine_step(steps, length):
    sine = sine_of(half_angle(steps, length))
    return 1.0 - 2.0 * sine * sine


def circle(steps, length):
    half = half_angle(steps, length)
    sine = sine_of(half)
    return 2.0 * sine * cosine_of(half), 1.0 - 2.0 * sine * sine


def iota(shape, axis):
    return lax.broadcasted_iota(jnp.int32, shape, axis)


def natural(place):
    return place


def mixed(place):
    n = place >> 6
    for source, target in ((5, 5), (4, 2), (3, 0), (2, 4), (1, 3), (0, 1)):
        n = n + (((place >> source) & 1) << (target + 1))
    return n


def position(place, order):
    n = order(place & (G // 2 - 1))
    return jnp.where(place < G // 2, n, G - 1 - n)


def folded(order, axis):
    place = iota((8, G) if axis else (G, K), axis)
    factor = 2 * order(place & (G // 2 - 1)) + 1
    return factor, jnp.where(place < G // 2, 0, -(G // 2))


def spread(value, shape):
    for axis in range(2):
        times = shape[axis] // value.shape[axis]
        if times > 1:
            value = jnp.concatenate([value] * times, axis=axis)
    return value


def signed(index, length):
    return jnp.where(index < length // 2, index, index - length)


def forward_table(shape, frequency, order, axis):
    factor, offset = (spread(value, shape) for value in folded(order, axis))
    return cosine_step(frequency(iota(shape, 1 - axis)) * factor + offset, 2 * G)


def fresnel(shape, frequency_u, frequency_v):
    u, v = frequency_u(iota(shape, 0)), frequency_v(iota(shape, 1))
    square = u * u + v * v
    angle = jnp.minimum(square, LIMIT).astype(F32) * FRESNEL_RATE
    keep = jnp.where(square <= LIMIT, 1.0 / (G * G), 0.0)
    return cosine_of(angle) * keep, -sine_of(angle) * keep


def copies_kernel(potential_ref, out_ref):
    values = potential_ref[0]
    pick = iota((K, K), 0) + iota((K, K), 1) == K - 1
    mirror = jnp.where(pick, 1.0, 0.0)
    quarters = [values[:, K * i : K * (i + 1)] for i in range(4)]
    for i in (1, 3):
        quarters[i] = jnp.dot(
            quarters[i], mirror, precision=lax.Precision.HIGHEST, preferred_element_type=F32
        )
    pieces = [
        jnp.concatenate([quarter[layer : layer + 1] for quarter in quarters], axis=0)[None]
        for layer in range(SLICES)
    ]
    out_ref[...] = jnp.concatenate(pieces * (out_ref.shape[0] // SLICES), axis=0)


AHEAD_LEFT = (0, ROWS, G)
AHEAD_RIGHT = (AHEAD_LEFT[0] + AHEAD_LEFT[1], G, G)
BACK_RIGHT = (AHEAD_RIGHT[0] + G, G, G)
BACK_LEFT = (BACK_RIGHT[0] + G, G, G)
CROP_LEFT = (BACK_LEFT[0] + G, K, G)
IMAGE_RIGHT = (CROP_LEFT[0] + K, K, 2 * K)
IMAGE_LEFT = (IMAGE_RIGHT[0] + K, 2 * K, 2 * K)
TABLE_ROWS = IMAGE_LEFT[0] + IMAGE_LEFT[1]

def terms(ref, where):
    row, rows, columns = where
    return ref[row : row + rows, :columns], ref[row : row + rows, G : G + columns]


def near(index):
    return index - ROWS // 2


def whole(index):
    return signed(index, G)


def centred(index):
    return index - K // 2


def prepare_kernel(
    own_ref, slab_ref, tilt_ref, tilts_ref, aperture_ref, positions_ref, coef_ref, table_ref, factor_ref, across_ref
):
    own = own_ref[0]
    across_ref[0], across_ref[1] = circle(tilt_ref[0, own] * position(iota((G, K), 0), mixed), G)
    factor_ref[0], factor_ref[1] = fresnel((ROWS, G), near, whole)

    tilts = tilts_ref[...]
    beams = tilts.shape[1]
    square = jnp.sum((tilts * tilts).astype(F32), axis=0, keepdims=True)
    angle = -DEFOCUS_RATE * jnp.broadcast_to(square, (8, beams))
    turns = jnp.floor(angle * (0.5 / math.pi) + 0.5)
    half = 0.5 * ((angle - turns * 6.28125) - turns * (2.0 * math.pi - 6.28125))
    sine, cosine = sine_of(half), cosine_of(half)
    amount = jnp.broadcast_to(aperture_ref[...].astype(F32) * (1.0 / math.sqrt(beams)), (8, beams))
    weight_re = spread(amount * (1.0 - 2.0 * sine * sine), (K, beams))
    weight_im = spread(amount * (2.0 * sine * cosine), (K, beams))
    none = jnp.zeros((6, K), F32)
    steep = jnp.concatenate([tilts.astype(F32), none], axis=0).astype(BF16)
    for core in range(2):
        at = pl.multiple_of((slab_ref[0] ^ core) * K, K)
        places = jnp.concatenate([positions_ref[:, pl.ds(at, K)].astype(F32), none], axis=0)
        steps = jnp.dot(places.T.astype(BF16), steep, preferred_element_type=F32)
        sine, cosine = circle(-steps.astype(jnp.int32), K)
        coef_ref[0, K * core : K * (core + 1), :] = cosine * weight_re - sine * weight_im
        coef_ref[1, K * core : K * (core + 1), :] = cosine * weight_im + sine * weight_re

    m, other = iota((2 * K, 2 * K), 0), iota((2 * K, 2 * K), 1)
    turn = (4 * (m >> 1) + 1) * centred(other & (K - 1)) + K * ((other >> 7) - (m & 1))
    left, right = iota((K, 2 * K), 0), iota((K, 2 * K), 1)
    for (row, rows, columns), table in (
        (AHEAD_LEFT, forward_table((ROWS, G), near, mixed, 1)),
        (AHEAD_RIGHT, forward_table((G, G), whole, natural, 0)),
        (BACK_RIGHT, forward_table((G, G), whole, natural, 1)),
        (BACK_LEFT, forward_table((G, G), near, mixed, 0)),
        (CROP_LEFT, forward_table((K, G), centred, mixed, 1)),
        (IMAGE_RIGHT, cosine_step(signed(left, K) * (4 * (right & (K - 1)) + 1) - K * (right >> 7), 2 * G)),
        (IMAGE_LEFT, cosine_step(turn, 2 * G)),
    ):
        high, low = split(table)
        table_ref[row : row + rows, :columns] = high
        table_ref[row : row + rows, G : G + columns] = low


def from_left(table, field):
    high, low = split(field)
    short = table[0].shape[1] - field.shape[0]
    if short:
        none = jnp.zeros((short, field.shape[1]), BF16)
        high, low = jnp.concatenate([high, none], axis=0), jnp.concatenate([low, none], axis=0)
    return jnp.dot(
        jnp.concatenate([table[0], table[0], table[1]], axis=1),
        jnp.concatenate([high, low, high], axis=0),
        preferred_element_type=F32,
    )


def from_right(field, table):
    high, low = split(field)
    return jnp.dot(
        jnp.concatenate([high, low, high], axis=1),
        jnp.concatenate([table[0], table[0], table[1]], axis=0),
        preferred_element_type=F32,
    )


def halves(value, axis):
    half = value.shape[axis] // 2
    return lax.slice_in_dim(value, 0, half, axis=axis), lax.slice_in_dim(value, half, 2 * half, axis=axis)


def fold(real, imag, axis):
    real_ahead, real_back = halves(real, axis)
    imag_ahead, imag_back = halves(imag, axis)
    return (
        jnp.concatenate([real_ahead + real_back, imag_ahead - imag_back], axis=axis),
        jnp.concatenate([imag_ahead + imag_back, real_back - real_ahead], axis=axis),
    )


def unfold(real, imag, axis):
    real_even, real_odd = halves(real, axis)
    imag_even, imag_odd = halves(imag, axis)
    return (
        jnp.concatenate([real_even - imag_odd, real_even + imag_odd], axis=axis),
        jnp.concatenate([imag_even + real_odd, imag_even - real_odd], axis=axis),
    )


def spectrum(real, imag, left, right, factor):
    field = from_left(left, jnp.concatenate(fold(real, imag, 0), axis=1))
    field = jnp.concatenate(fold(*halves(field, 1), 1), axis=0)
    real, imag = halves(from_right(field, right), 0)
    return (
        real * factor[0] - imag * factor[1],
        real * factor[1] + imag * factor[0],
    )


def screened(real, imag, potential_ref, layer):
    def rows(half, parity, side):
        places = [
            (CUBE - 1 - k if half else k) * REST + (REST // 2 if half else 0) for k in range(CUBE)
        ]
        own = 4 * layer + 2 * (1 - parity if half else parity) + side
        return jnp.concatenate(
            [potential_ref[pl.ds(PIECE * place + own, REST // 2, PIECE), :] for place in places], axis=0
        )

    potential = jnp.concatenate(
        [
            jnp.concatenate([rows(half, parity, side) for side in range(2)], axis=1)
            for half in range(2)
            for parity in range(2)
        ],
        axis=0,
    )
    turned = potential - math.pi / 2
    sine, cosine = cosine_of(turned), sine_of(turned)
    return -(real * cosine + imag * sine), real * sine - imag * cosine


def plane_wave(across_ref, tilt_y):
    sine_x, cosine_x = (jnp.concatenate([across_ref[i]] * (G // K), axis=1) for i in range(2))
    sine_y, cosine_y = circle(tilt_y * position(iota((8, G), 1), natural), G)
    sine_y, cosine_y = (jnp.concatenate([value] * (G // 8), axis=0) for value in (sine_y, cosine_y))
    return cosine_x * cosine_y - sine_x * sine_y, sine_x * cosine_y + cosine_x * sine_y


def band_of(value):
    return jnp.where(iota((value.shape[0], K), 1) < K // 2, value[:, :K], value[:, K:])


def propagate_kernel(own_ref, tilt_ref, potential_ref, table_ref, factor_ref, across_ref, out_ref):
    table = functools.partial(terms, table_ref)
    real, imag = plane_wave(across_ref, tilt_ref[1, own_ref[0]])
    for layer in range(SLICES - 1):
        real, imag = screened(real, imag, potential_ref, layer)
        real, imag = spectrum(real, imag, table(AHEAD_LEFT), table(AHEAD_RIGHT), factor_ref)
        field = from_right(jnp.concatenate([real, imag], axis=0), table(BACK_RIGHT))
        field = jnp.concatenate(unfold(*halves(field, 0), 1), axis=1)
        real, imag = unfold(*halves(from_left(table(BACK_LEFT), field), 1), 0)
    crop_right = [band_of(term) for term in table(AHEAD_RIGHT)]
    first = (ROWS - K) // 2
    crop_factor = [band_of(factor_ref[i, first : first + K, :]) for i in range(2)]
    real, imag = screened(real, imag, potential_ref, SLICES - 1)
    real, imag = spectrum(real, imag, table(CROP_LEFT), crop_right, crop_factor)
    product = from_right(jnp.concatenate([real, imag], axis=0), table(IMAGE_RIGHT))
    real = product[:K, :K] - product[K:, K:]
    imag = product[:K, K:] + product[K:, :K]
    out_ref[...] = from_left(table(IMAGE_LEFT), jnp.concatenate([real, imag], axis=0))


def probe_kernel(configs, block_ref, coef_ref, mine_ref, other_ref):
    here = block_ref.shape[0] // (2 * K)
    field = jnp.concatenate(
        [
            jnp.concatenate(
                [block_ref[pl.ds(2 * K * config + part, K, 2), :] for part in range(2)], axis=0
            )
            for config in range(here)
        ],
        axis=1,
    )
    real, imag = coef_ref[0], coef_ref[1]
    table = jnp.concatenate(
        [jnp.concatenate([real, -imag], axis=1), jnp.concatenate([imag, real], axis=1)], axis=0
    )
    waves = from_left(split(table), field)
    probes = waves.shape[0] // 2
    real, imag = waves[:probes], waves[probes:]
    power = real * real + imag * imag
    total = sum(power[:, K * config : K * config + K] for config in range(here)) * (1.0 / configs)
    mine_ref[...] = total[: probes // 2]
    other_ref[...] = total[probes // 2 :]


VMEM = pl.BlockSpec(memory_space=pltpu.VMEM)
SMEM = pl.BlockSpec(memory_space=pltpu.SMEM)
PARAMS = pltpu.CompilerParams(vmem_limit_bytes=24 * 1024 * 1024)


def shape_of(dtype, *shape):
    return jax.ShapeDtypeStruct(shape, dtype)


def prepare(own, slab, tilts, aperture, positions):
    beams = tilts.shape[1]
    out = [
        shape_of(F32, 2, 2 * K, beams),
        shape_of(BF16, TABLE_ROWS, 2 * G),
        shape_of(F32, 2, ROWS, G),
        shape_of(F32, 2, G, K),
    ]
    return pl.pallas_call(
        prepare_kernel,
        out_shape=out,
        in_specs=[SMEM] * 3 + [VMEM] * 3,
        out_specs=[VMEM] * len(out),
        compiler_params=PARAMS,
        name="prepare",
    )(own, slab, tilts, tilts, aperture, positions)


def propagate(*operands):
    return pl.pallas_call(
        propagate_kernel,
        out_shape=shape_of(F32, 2 * K, K),
        in_specs=[SMEM] * 2 + [VMEM] * (len(operands) - 2),
        out_specs=VMEM,
        compiler_params=PARAMS,
        name="propagate",
    )(*operands)


def probe(block, coef, configs):
    quarter = coef.shape[1] // 2
    return pl.pallas_call(
        functools.partial(probe_kernel, configs),
        out_shape=[shape_of(F32, quarter, K)] * 2,
        in_specs=[VMEM] * 2,
        out_specs=[VMEM] * 2,
        compiler_params=PARAMS,
        name="probe",
    )(block, coef)


def copies_of(potential, count):
    return pl.pallas_call(
        copies_kernel,
        out_shape=shape_of(F32, count * SLICES, 4, K),
        in_specs=[VMEM],
        out_specs=VMEM,
        compiler_params=PARAMS,
        name="copies",
    )(potential)


def per_device(groups, potential, tilts, aperture, positions):
    far, near = groups
    devices = lax.axis_size("beam")
    pairs, cores = lax.axis_size("pair"), lax.axis_size("core")
    configs = pairs * cores
    beams = tilts.shape[0]

    part = lax.all_to_all(copies_of(potential, REST), "beam", 0, 0, axis_index_groups=far, tiled=True)

    own = lax.axis_index("beam").reshape(1)
    slab = lax.axis_index(("pair", "core")).reshape(1)
    tilts = tilts.T
    coef, *tables = prepare(own, slab, tilts, aperture.reshape(1, beams), positions.T)
    part, coef, *tables = lax.optimization_barrier((part, coef, *tables))
    part = part.reshape(REST * PIECE, K)
    whole = lax.all_to_all(
        jnp.broadcast_to(part[None], (CUBE, *part.shape)), "beam", 0, 0, axis_index_groups=near
    ).reshape(devices * PIECE, K)
    image = propagate(own, tilts, whole, *tables)

    rows = jnp.broadcast_to(image.reshape(1, K, 2, K), (pairs, K, 2, K)).reshape(pairs * K, 2, K)
    block = lax.all_to_all(rows, ("pair", "beam"), 0, 0, tiled=True).reshape(2 * pairs * beams, K)
    mine, other = probe(block, coef, configs)
    return mine + lax.ppermute(other, "core", [(0, 1), (1, 0)])


def spread_bits(value, targets):
    return sum(((value >> source) & 1) << target for source, target in enumerate(reversed(targets)))


def exchange_groups():
    low, high = (5, 2, 0), (4, 3, 1)
    half = range(REST // 2)
    far = [
        [spread_bits(k, low) + spread_bits(j, high) for j in half]
        + [64 + spread_bits(k, low) + spread_bits(j, high) for j in reversed(half)]
        for k in range(CUBE)
    ]
    near = [
        [top + spread_bits(k, low) + spread_bits(j, high) for k in range(CUBE)]
        for top in (0, 64)
        for j in half
    ]
    return far, near


def solution(mesh):
    fine = jax.sharding.Mesh(mesh.devices.reshape(-1, 2, 2), ("beam", "pair", "core"))
    return jax.shard_map(
        functools.partial(per_device, exchange_groups()),
        mesh=fine,
        in_specs=(P(("pair", "core"), None, "beam"), P(), P(), P()),
        out_specs=P(("pair", "core"), "beam"),
        check_vma=False,
    )
```

```python
import functools
import math

import jax
import jax.numpy as jnp
from jax import lax
from jax.experimental import pallas as pl
from jax.experimental.pallas import tpu as pltpu
from jax.sharding import PartitionSpec as P

G = 256
K = 128
SLICES = 3
LIMIT = (G // 3) ** 2
REACH = G // 3
ROWS = 176
NEAR, FAR = 32, 4
PIECE = SLICES * 4

FRESNEL_RATE = 0.00019
DEFOCUS_RATE = 0.01

F32 = jnp.float32
BF16 = jnp.bfloat16


def split(value):
    high = value.astype(BF16)
    return high, (value - high.astype(F32)).astype(BF16)


def sine_of(t):
    s = t * t
    sine = jnp.full_like(t, 2.60501958e-6)
    for term in (-1.9808983e-4, 8.33304978e-3, -1.66666579e-1, 0.999999996):
        sine = sine * s + term
    return sine * t


def cosine_of(t):
    s = t * t
    cosine = jnp.full_like(t, 2.31515759e-5)
    for term in (-1.38535979e-3, 4.16635698e-2, -0.499999047, 0.999999953):
        cosine = cosine * s + term
    return cosine


def half_angle(steps, length):
    near = ((steps + length // 2) & (length - 1)) - length // 2
    return near.astype(F32) * (math.pi / length)


def cosine_step(steps, length):
    sine = sine_of(half_angle(steps, length))
    return 1.0 - 2.0 * sine * sine


def circle(steps, length):
    half = half_angle(steps, length)
    sine = sine_of(half)
    return 2.0 * sine * cosine_of(half), 1.0 - 2.0 * sine * sine


def iota(shape, axis):
    return lax.broadcasted_iota(jnp.int32, shape, axis)


def natural(place):
    return place


def mixed(place):
    return 2 * (place & (G // 4 - 1)) + (place >> 6)


def position(place, order):
    n = order(place & (G // 2 - 1))
    return jnp.where(place < G // 2, n, G - 1 - n)


def folded(order, axis):
    place = iota((8, G) if axis else (G, K), axis)
    factor = 2 * order(place & (G // 2 - 1)) + 1
    return factor, jnp.where(place < G // 2, 0, -(G // 2))


def spread(value, shape):
    for axis in range(2):
        times = shape[axis] // value.shape[axis]
        if times > 1:
            value = jnp.concatenate([value] * times, axis=axis)
    return value


def signed(index, length):
    return jnp.where(index < length // 2, index, index - length)


def forward_table(shape, frequency, order, axis):
    factor, offset = (spread(value, shape) for value in folded(order, axis))
    return cosine_step(frequency(iota(shape, 1 - axis)) * factor + offset, 2 * G)


def fresnel(shape, frequency_u, frequency_v):
    u, v = frequency_u(iota(shape, 0)), frequency_v(iota(shape, 1))
    square = u * u + v * v
    angle = jnp.minimum(square, LIMIT).astype(F32) * FRESNEL_RATE
    keep = jnp.where(square <= LIMIT, 1.0 / (G * G), 0.0)
    return cosine_of(angle) * keep, -sine_of(angle) * keep


def copies_kernel(potential_ref, out_ref):
    values = potential_ref[0]
    pick = iota((K, K), 0) + iota((K, K), 1) == K - 1
    mirror = jnp.where(pick, 1.0, 0.0)
    quarters = [values[:, K * i : K * (i + 1)] for i in range(4)]
    for i in (1, 3):
        quarters[i] = jnp.dot(
            quarters[i], mirror, precision=lax.Precision.HIGHEST, preferred_element_type=F32
        )
    pieces = [
        jnp.concatenate([quarter[layer : layer + 1] for quarter in quarters], axis=0)[None]
        for layer in range(SLICES)
    ]
    out_ref[...] = jnp.concatenate(pieces * (out_ref.shape[0] // SLICES), axis=0)


AHEAD_LEFT = (0, ROWS, G)
AHEAD_RIGHT = (AHEAD_LEFT[0] + AHEAD_LEFT[1], G, G)
BACK_RIGHT = (AHEAD_RIGHT[0] + G, G, G)
BACK_LEFT = (BACK_RIGHT[0] + G, G, G)
CROP_LEFT = (BACK_LEFT[0] + G, K, G)
IMAGE_RIGHT = (CROP_LEFT[0] + K, K, 2 * K)
IMAGE_LEFT = (IMAGE_RIGHT[0] + K, 2 * K, 2 * K)
TABLE_ROWS = IMAGE_LEFT[0] + IMAGE_LEFT[1]

def terms(ref, where):
    row, rows, columns = where
    return ref[row : row + rows, :columns], ref[row : row + rows, G : G + columns]


def near(index):
    return index - ROWS // 2


def whole(index):
    return signed(index, G)


def centred(index):
    return index - K // 2


def prepare_kernel(
    own_ref, slab_ref, tilt_ref, tilts_ref, aperture_ref, positions_ref, coef_ref, table_ref, factor_ref, across_ref
):
    own = own_ref[0]
    across_ref[0], across_ref[1] = circle(tilt_ref[0, own] * position(iota((G, K), 0), mixed), G)
    factor_ref[0], factor_ref[1] = fresnel((ROWS, G), near, whole)

    tilts = tilts_ref[...]
    beams = tilts.shape[1]
    square = jnp.sum((tilts * tilts).astype(F32), axis=0, keepdims=True)
    angle = -DEFOCUS_RATE * jnp.broadcast_to(square, (8, beams))
    turns = jnp.floor(angle * (0.5 / math.pi) + 0.5)
    half = 0.5 * ((angle - turns * 6.28125) - turns * (2.0 * math.pi - 6.28125))
    sine, cosine = sine_of(half), cosine_of(half)
    amount = jnp.broadcast_to(aperture_ref[...].astype(F32) * (1.0 / math.sqrt(beams)), (8, beams))
    weight_re = spread(amount * (1.0 - 2.0 * sine * sine), (K, beams))
    weight_im = spread(amount * (2.0 * sine * cosine), (K, beams))
    none = jnp.zeros((6, K), F32)
    steep = jnp.concatenate([tilts.astype(F32), none], axis=0).astype(BF16)
    for core in range(2):
        at = pl.multiple_of((slab_ref[0] ^ core) * K, K)
        places = jnp.concatenate([positions_ref[:, pl.ds(at, K)].astype(F32), none], axis=0)
        steps = jnp.dot(places.T.astype(BF16), steep, preferred_element_type=F32)
        sine, cosine = circle(-steps.astype(jnp.int32), K)
        coef_ref[0, K * core : K * (core + 1), :] = cosine * weight_re - sine * weight_im
        coef_ref[1, K * core : K * (core + 1), :] = cosine * weight_im + sine * weight_re

    m, other = iota((2 * K, 2 * K), 0), iota((2 * K, 2 * K), 1)
    turn = (4 * (m >> 1) + 1) * centred(other & (K - 1)) + K * ((other >> 7) - (m & 1))
    left, right = iota((K, 2 * K), 0), iota((K, 2 * K), 1)
    for (row, rows, columns), table in (
        (AHEAD_LEFT, forward_table((ROWS, G), near, mixed, 1)),
        (AHEAD_RIGHT, forward_table((G, G), whole, natural, 0)),
        (BACK_RIGHT, forward_table((G, G), whole, natural, 1)),
        (BACK_LEFT, forward_table((G, G), near, mixed, 0)),
        (CROP_LEFT, forward_table((K, G), centred, mixed, 1)),
        (IMAGE_RIGHT, cosine_step(signed(left, K) * (4 * (right & (K - 1)) + 1) - K * (right >> 7), 2 * G)),
        (IMAGE_LEFT, cosine_step(turn, 2 * G)),
    ):
        high, low = split(table)
        table_ref[row : row + rows, :columns] = high
        table_ref[row : row + rows, G : G + columns] = low


def from_left(table, field):
    high, low = split(field)
    short = table[0].shape[1] - field.shape[0]
    if short:
        none = jnp.zeros((short, field.shape[1]), BF16)
        high, low = jnp.concatenate([high, none], axis=0), jnp.concatenate([low, none], axis=0)
    return jnp.dot(
        jnp.concatenate([table[0], table[0], table[1]], axis=1),
        jnp.concatenate([high, low, high], axis=0),
        preferred_element_type=F32,
    )


def from_right(field, table):
    table = jnp.concatenate([table[0], table[0], table[1]], axis=0)

    def product(rows):
        high, low = split(rows)
        return jnp.dot(jnp.concatenate([high, low, high], axis=1), table, preferred_element_type=F32)

    return jnp.concatenate([product(rows) for rows in halves(field, 0)], axis=0)


def halves(value, axis):
    half = value.shape[axis] // 2
    return lax.slice_in_dim(value, 0, half, axis=axis), lax.slice_in_dim(value, half, 2 * half, axis=axis)


def fold(real, imag, axis):
    real_ahead, real_back = halves(real, axis)
    imag_ahead, imag_back = halves(imag, axis)
    return (
        jnp.concatenate([real_ahead + real_back, imag_ahead - imag_back], axis=axis),
        jnp.concatenate([imag_ahead + imag_back, real_back - real_ahead], axis=axis),
    )


def unfold(real, imag, axis):
    real_even, real_odd = halves(real, axis)
    imag_even, imag_odd = halves(imag, axis)
    return (
        jnp.concatenate([real_even - imag_odd, real_even + imag_odd], axis=axis),
        jnp.concatenate([imag_even + real_odd, imag_even - real_odd], axis=axis),
    )


def spectrum(real, imag, left, right, factor):
    field = from_left(left, jnp.concatenate(fold(real, imag, 0), axis=1))
    field = jnp.concatenate(fold(*halves(field, 1), 1), axis=0)
    real, imag = halves(from_right(field, right), 0)
    return (
        real * factor[0] - imag * factor[1],
        real * factor[1] + imag * factor[0],
    )


def screened(real, imag, potential_ref, layer):
    count = G // 4

    def rows(half, parity, side):
        own = 4 * layer + 2 * (1 - parity if half else parity) + side
        return potential_ref[pl.ds(PIECE * count * half + own, count, PIECE), :]

    potential = jnp.concatenate(
        [
            jnp.concatenate([rows(half, parity, side) for side in range(2)], axis=1)
            for half in range(2)
            for parity in range(2)
        ],
        axis=0,
    )
    turned = potential - math.pi / 2
    sine, cosine = cosine_of(turned), sine_of(turned)
    return -(real * cosine + imag * sine), real * sine - imag * cosine


def plane_wave(across_ref, tilt_y):
    sine_x, cosine_x = (jnp.concatenate([across_ref[i]] * (G // K), axis=1) for i in range(2))
    sine_y, cosine_y = circle(tilt_y * position(iota((8, G), 1), natural), G)
    sine_y, cosine_y = (jnp.concatenate([value] * (G // 8), axis=0) for value in (sine_y, cosine_y))
    return cosine_x * cosine_y - sine_x * sine_y, sine_x * cosine_y + cosine_x * sine_y


def band_of(value):
    return jnp.where(iota((value.shape[0], K), 1) < K // 2, value[:, :K], value[:, K:])


def propagate_kernel(own_ref, tilt_ref, potential_ref, table_ref, factor_ref, across_ref, out_ref):
    table = functools.partial(terms, table_ref)
    real, imag = plane_wave(across_ref, tilt_ref[1, own_ref[0]])
    for layer in range(SLICES - 1):
        real, imag = screened(real, imag, potential_ref, layer)
        real, imag = spectrum(real, imag, table(AHEAD_LEFT), table(AHEAD_RIGHT), factor_ref)
        field = from_right(jnp.concatenate([real, imag], axis=0), table(BACK_RIGHT))
        field = jnp.concatenate(unfold(*halves(field, 0), 1), axis=1)
        real, imag = unfold(*halves(from_left(table(BACK_LEFT), field), 1), 0)
    crop_right = [band_of(term) for term in table(AHEAD_RIGHT)]
    first = (ROWS - K) // 2
    crop_factor = [band_of(factor_ref[i, first : first + K, :]) for i in range(2)]
    real, imag = screened(real, imag, potential_ref, SLICES - 1)
    real, imag = spectrum(real, imag, table(CROP_LEFT), crop_right, crop_factor)
    product = from_right(jnp.concatenate([real, imag], axis=0), table(IMAGE_RIGHT))
    real = product[:K, :K] - product[K:, K:]
    imag = product[:K, K:] + product[K:, :K]
    out_ref[...] = from_left(table(IMAGE_LEFT), jnp.concatenate([real, imag], axis=0))


def probe_kernel(configs, block_ref, coef_ref, mine_ref, other_ref):
    here = block_ref.shape[0] // (2 * K)
    field = jnp.concatenate(
        [
            jnp.concatenate(
                [block_ref[pl.ds(2 * K * config + part, K, 2), :] for part in range(2)], axis=0
            )
            for config in range(here)
        ],
        axis=1,
    )
    real, imag = coef_ref[0], coef_ref[1]
    table = jnp.concatenate(
        [jnp.concatenate([real, -imag], axis=1), jnp.concatenate([imag, real], axis=1)], axis=0
    )
    waves = from_left(split(table), field)
    probes = waves.shape[0] // 2
    real, imag = waves[:probes], waves[probes:]
    power = real * real + imag * imag
    total = sum(power[:, K * config : K * config + K] for config in range(here)) * (1.0 / configs)
    mine_ref[...] = total[: probes // 2]
    other_ref[...] = total[probes // 2 :]


VMEM = pl.BlockSpec(memory_space=pltpu.VMEM)
SMEM = pl.BlockSpec(memory_space=pltpu.SMEM)
PARAMS = pltpu.CompilerParams(vmem_limit_bytes=24 * 1024 * 1024)


def shape_of(dtype, *shape):
    return jax.ShapeDtypeStruct(shape, dtype)


def prepare(own, slab, tilts, aperture, positions):
    beams = tilts.shape[1]
    out = [
        shape_of(F32, 2, 2 * K, beams),
        shape_of(BF16, TABLE_ROWS, 2 * G),
        shape_of(F32, 2, ROWS, G),
        shape_of(F32, 2, G, K),
    ]
    return pl.pallas_call(
        prepare_kernel,
        out_shape=out,
        in_specs=[SMEM] * 3 + [VMEM] * 3,
        out_specs=[VMEM] * len(out),
        compiler_params=PARAMS,
        name="prepare",
    )(own, slab, tilts, tilts, aperture, positions)


def propagate(*operands):
    return pl.pallas_call(
        propagate_kernel,
        out_shape=shape_of(F32, 2 * K, K),
        in_specs=[SMEM] * 2 + [VMEM] * (len(operands) - 2),
        out_specs=VMEM,
        compiler_params=PARAMS,
        name="propagate",
    )(*operands)


def probe(block, coef, configs):
    quarter = coef.shape[1] // 2
    return pl.pallas_call(
        functools.partial(probe_kernel, configs),
        out_shape=[shape_of(F32, quarter, K)] * 2,
        in_specs=[VMEM] * 2,
        out_specs=[VMEM] * 2,
        compiler_params=PARAMS,
        name="probe",
    )(block, coef)


def copies_of(potential, count):
    return pl.pallas_call(
        copies_kernel,
        out_shape=shape_of(F32, count * SLICES, 4, K),
        in_specs=[VMEM],
        out_specs=VMEM,
        compiler_params=PARAMS,
        name="copies",
    )(potential)


def per_device(groups, potential, tilts, aperture, positions):
    near, far = groups
    devices = lax.axis_size("beam")
    pairs, cores = lax.axis_size("pair"), lax.axis_size("core")
    configs = pairs * cores
    beams = tilts.shape[0]

    part = lax.all_to_all(copies_of(potential, NEAR), "beam", 0, 0, axis_index_groups=near, tiled=True)

    own = lax.axis_index("beam").reshape(1)
    slab = lax.axis_index(("pair", "core")).reshape(1)
    tilts = tilts.T
    coef, *tables = prepare(own, slab, tilts, aperture.reshape(1, beams), positions.T)
    part, coef, *tables = lax.optimization_barrier((part, coef, *tables))
    part = part.reshape(NEAR * PIECE, K)
    whole = lax.all_to_all(
        jnp.broadcast_to(part[None], (FAR, *part.shape)), "beam", 0, 0, axis_index_groups=far
    ).reshape(devices * PIECE, K)
    image = propagate(own, tilts, whole, *tables)

    rows = jnp.broadcast_to(image.reshape(1, K, 2, K), (pairs, K, 2, K)).reshape(pairs * K, 2, K)
    block = lax.all_to_all(rows, ("pair", "beam"), 0, 0, tiled=True).reshape(2 * pairs * beams, K)
    mine, other = probe(block, coef, configs)
    return mine + lax.ppermute(other, "core", [(0, 1), (1, 0)])


def exchange_groups():
    run, turned = range(NEAR), range(NEAR - 1, -1, -1)
    near = [[NEAR * x + i for i in (run if 2 * x < FAR else turned)] for x in range(FAR)]
    order = [*range(FAR // 2), *range(FAR - 1, FAR // 2 - 1, -1)]
    far = [[NEAR * x + i for x in order] for i in run]
    return near, far


def solution(mesh):
    fine = jax.sharding.Mesh(mesh.devices.reshape(-1, 2, 2), ("beam", "pair", "core"))
    return jax.shard_map(
        functools.partial(per_device, exchange_groups()),
        mesh=fine,
        in_specs=(P(("pair", "core"), None, "beam"), P(), P(), P()),
        out_specs=P(("pair", "core"), "beam"),
        check_vma=False,
    )
```

```python
import functools
import math

import jax
import jax.numpy as jnp
from jax import lax
from jax.experimental import pallas as pl
from jax.experimental.pallas import tpu as pltpu
from jax.sharding import PartitionSpec as P

G = 256
K = 128
SLICES = 3
LIMIT = (G // 3) ** 2
REACH = G // 3
ROWS = 176
NEAR, FAR = 32, 4
PIECE = SLICES * 4

FRESNEL_RATE = 0.00019
DEFOCUS_RATE = 0.01

F32 = jnp.float32
BF16 = jnp.bfloat16


def split(value):
    high = value.astype(BF16)
    return high, (value - high.astype(F32)).astype(BF16)


def sine_of(t):
    s = t * t
    sine = jnp.full_like(t, 2.60501958e-6)
    for term in (-1.9808983e-4, 8.33304978e-3, -1.66666579e-1, 0.999999996):
        sine = sine * s + term
    return sine * t


def cosine_of(t):
    s = t * t
    cosine = jnp.full_like(t, 2.31515759e-5)
    for term in (-1.38535979e-3, 4.16635698e-2, -0.499999047, 0.999999953):
        cosine = cosine * s + term
    return cosine


def half_angle(steps, length):
    near = ((steps + length // 2) & (length - 1)) - length // 2
    return near.astype(F32) * (math.pi / length)


def cosine_step(steps, length):
    sine = sine_of(half_angle(steps, length))
    return 1.0 - 2.0 * sine * sine


def circle(steps, length):
    half = half_angle(steps, length)
    sine = sine_of(half)
    return 2.0 * sine * cosine_of(half), 1.0 - 2.0 * sine * sine


def iota(shape, axis):
    return lax.broadcasted_iota(jnp.int32, shape, axis)


def natural(place):
    return place


def mixed(place):
    return 2 * (place & (G // 4 - 1)) + (place >> 6)


def position(place, order):
    n = order(place & (G // 2 - 1))
    return jnp.where(place < G // 2, n, G - 1 - n)


def folded(order, axis):
    place = iota((8, G) if axis else (G, K), axis)
    factor = 2 * order(place & (G // 2 - 1)) + 1
    return factor, jnp.where(place < G // 2, 0, -(G // 2))


def spread(value, shape):
    for axis in range(2):
        times = shape[axis] // value.shape[axis]
        if times > 1:
            value = jnp.concatenate([value] * times, axis=axis)
    return value


def signed(index, length):
    return jnp.where(index < length // 2, index, index - length)


def forward_table(shape, frequency, order, axis):
    factor, offset = (spread(value, shape) for value in folded(order, axis))
    return cosine_step(frequency(iota(shape, 1 - axis)) * factor + offset, 2 * G)


def fresnel(shape, frequency_u, frequency_v):
    u, v = frequency_u(iota(shape, 0)), frequency_v(iota(shape, 1))
    square = u * u + v * v
    angle = jnp.minimum(square, LIMIT).astype(F32) * FRESNEL_RATE
    keep = jnp.where(square <= LIMIT, 1.0 / (G * G), 0.0)
    return cosine_of(angle) * keep, -sine_of(angle) * keep


def copies_kernel(potential_ref, out_ref):
    values = potential_ref[0]
    pick = iota((K, K), 0) + iota((K, K), 1) == K - 1
    mirror = jnp.where(pick, 1.0, 0.0)
    quarters = [values[:, K * i : K * (i + 1)] for i in range(4)]
    for i in (1, 3):
        quarters[i] = jnp.dot(
            quarters[i], mirror, precision=lax.Precision.HIGHEST, preferred_element_type=F32
        )
    pieces = [
        jnp.concatenate([quarter[layer : layer + 1] for quarter in quarters], axis=0)[None]
        for layer in range(SLICES)
    ]
    out_ref[...] = jnp.concatenate(pieces * (out_ref.shape[0] // SLICES), axis=0)


AHEAD_LEFT = (0, ROWS, G)
AHEAD_RIGHT = (AHEAD_LEFT[0] + AHEAD_LEFT[1], G, G)
BACK_RIGHT = (AHEAD_RIGHT[0] + G, G, G)
BACK_LEFT = (BACK_RIGHT[0] + G, G, G)
CROP_LEFT = (BACK_LEFT[0] + G, K, G)
IMAGE_RIGHT = (CROP_LEFT[0] + K, K, 2 * K)
IMAGE_LEFT = (IMAGE_RIGHT[0] + K, 2 * K, 2 * K)
TABLE_ROWS = IMAGE_LEFT[0] + IMAGE_LEFT[1]

def terms(ref, where):
    row, rows, columns = where
    return ref[row : row + rows, :columns], ref[row : row + rows, G : G + columns]


def near(index):
    return index - ROWS // 2


def whole(index):
    return signed(index, G)


def centred(index):
    return index - K // 2


def prepare_kernel(
    own_ref, slab_ref, tilt_ref, tilts_ref, aperture_ref, positions_ref, coef_ref, table_ref, factor_ref, across_ref
):
    own = own_ref[0]
    across_ref[0], across_ref[1] = circle(tilt_ref[0, own] * position(iota((G, K), 0), mixed), G)
    factor_ref[0], factor_ref[1] = fresnel((ROWS, G), near, whole)

    tilts = tilts_ref[...]
    beams = tilts.shape[1]
    square = jnp.sum((tilts * tilts).astype(F32), axis=0, keepdims=True)
    angle = -DEFOCUS_RATE * jnp.broadcast_to(square, (8, beams))
    turns = jnp.floor(angle * (0.5 / math.pi) + 0.5)
    half = 0.5 * ((angle - turns * 6.28125) - turns * (2.0 * math.pi - 6.28125))
    sine, cosine = sine_of(half), cosine_of(half)
    amount = jnp.broadcast_to(aperture_ref[...].astype(F32) * (1.0 / math.sqrt(beams)), (8, beams))
    weight_re = spread(amount * (1.0 - 2.0 * sine * sine), (K, beams))
    weight_im = spread(amount * (2.0 * sine * cosine), (K, beams))
    none = jnp.zeros((6, K), F32)
    steep = jnp.concatenate([tilts.astype(F32), none], axis=0).astype(BF16)
    for core in range(2):
        at = pl.multiple_of((slab_ref[0] ^ core) * K, K)
        places = jnp.concatenate([positions_ref[:, pl.ds(at, K)].astype(F32), none], axis=0)
        steps = jnp.dot(places.T.astype(BF16), steep, preferred_element_type=F32)
        sine, cosine = circle(-steps.astype(jnp.int32), K)
        coef_ref[0, K * core : K * (core + 1), :] = cosine * weight_re - sine * weight_im
        coef_ref[1, K * core : K * (core + 1), :] = cosine * weight_im + sine * weight_re

    m, other = iota((2 * K, 2 * K), 0), iota((2 * K, 2 * K), 1)
    turn = (4 * (m >> 1) + 1) * centred(other & (K - 1)) + K * ((other >> 7) - (m & 1))
    left, right = iota((K, 2 * K), 0), iota((K, 2 * K), 1)
    for (row, rows, columns), table in (
        (AHEAD_LEFT, forward_table((ROWS, G), near, mixed, 1)),
        (AHEAD_RIGHT, forward_table((G, G), whole, natural, 0)),
        (BACK_RIGHT, forward_table((G, G), whole, natural, 1)),
        (BACK_LEFT, forward_table((G, G), near, mixed, 0)),
        (CROP_LEFT, forward_table((K, G), centred, mixed, 1)),
        (IMAGE_RIGHT, cosine_step(signed(left, K) * (4 * (right & (K - 1)) + 1) - K * (right >> 7), 2 * G)),
        (IMAGE_LEFT, cosine_step(turn, 2 * G)),
    ):
        high, low = split(table)
        table_ref[row : row + rows, :columns] = high
        table_ref[row : row + rows, G : G + columns] = low


def from_left(table, field):
    high, low = split(field)
    short = table[0].shape[1] - field.shape[0]
    if short:
        none = jnp.zeros((short, field.shape[1]), BF16)
        high, low = jnp.concatenate([high, none], axis=0), jnp.concatenate([low, none], axis=0)
    return jnp.dot(
        jnp.concatenate([table[0], table[0], table[1]], axis=1),
        jnp.concatenate([high, low, high], axis=0),
        preferred_element_type=F32,
    )


def from_right(field, table):
    table = jnp.concatenate([table[0], table[0], table[1]], axis=0)

    def product(rows):
        high, low = split(rows)
        return jnp.dot(jnp.concatenate([high, low, high], axis=1), table, preferred_element_type=F32)

    return jnp.concatenate([product(rows) for rows in halves(field, 0)], axis=0)


def halves(value, axis):
    half = value.shape[axis] // 2
    return lax.slice_in_dim(value, 0, half, axis=axis), lax.slice_in_dim(value, half, 2 * half, axis=axis)


def fold(real, imag, axis):
    real_ahead, real_back = halves(real, axis)
    imag_ahead, imag_back = halves(imag, axis)
    return (
        jnp.concatenate([real_ahead + real_back, imag_ahead - imag_back], axis=axis),
        jnp.concatenate([imag_ahead + imag_back, real_back - real_ahead], axis=axis),
    )


def unfold(real, imag, axis):
    real_even, real_odd = halves(real, axis)
    imag_even, imag_odd = halves(imag, axis)
    return (
        jnp.concatenate([real_even - imag_odd, real_even + imag_odd], axis=axis),
        jnp.concatenate([imag_even + real_odd, imag_even - real_odd], axis=axis),
    )


def spectrum(real, imag, left, right, factor):
    field = from_left(left, jnp.concatenate(fold(real, imag, 0), axis=1))
    field = jnp.concatenate(fold(*halves(field, 1), 1), axis=0)
    real, imag = halves(from_right(field, right), 0)
    return (
        real * factor[0] - imag * factor[1],
        real * factor[1] + imag * factor[0],
    )


def screened(real, imag, potential_ref, layer):
    count = G // 4

    def rows(half, parity, side):
        own = 4 * layer + 2 * (1 - parity if half else parity) + side
        return potential_ref[pl.ds(PIECE * count * half + own, count, PIECE), :]

    potential = jnp.concatenate(
        [
            jnp.concatenate([rows(half, parity, side) for side in range(2)], axis=1)
            for half in range(2)
            for parity in range(2)
        ],
        axis=0,
    )
    turned = potential - math.pi / 2
    sine, cosine = cosine_of(turned), sine_of(turned)
    return -(real * cosine + imag * sine), real * sine - imag * cosine


def plane_wave(across_ref, tilt_y):
    sine_x, cosine_x = (jnp.concatenate([across_ref[i]] * (G // K), axis=1) for i in range(2))
    sine_y, cosine_y = circle(tilt_y * position(iota((8, G), 1), natural), G)
    sine_y, cosine_y = (jnp.concatenate([value] * (G // 8), axis=0) for value in (sine_y, cosine_y))
    return cosine_x * cosine_y - sine_x * sine_y, sine_x * cosine_y + cosine_x * sine_y


def band_of(value):
    return jnp.where(iota((value.shape[0], K), 1) < K // 2, value[:, :K], value[:, K:])


def propagate_kernel(own_ref, tilt_ref, potential_ref, table_ref, factor_ref, across_ref, out_ref):
    table = functools.partial(terms, table_ref)
    real, imag = plane_wave(across_ref, tilt_ref[1, own_ref[0]])
    for layer in range(SLICES - 1):
        real, imag = screened(real, imag, potential_ref, layer)
        real, imag = spectrum(real, imag, table(AHEAD_LEFT), table(AHEAD_RIGHT), factor_ref)
        field = from_right(jnp.concatenate([real, imag], axis=0), table(BACK_RIGHT))
        field = jnp.concatenate(unfold(*halves(field, 0), 1), axis=1)
        real, imag = unfold(*halves(from_left(table(BACK_LEFT), field), 1), 0)
    crop_right = [band_of(term) for term in table(AHEAD_RIGHT)]
    first = (ROWS - K) // 2
    crop_factor = [band_of(factor_ref[i, first : first + K, :]) for i in range(2)]
    real, imag = screened(real, imag, potential_ref, SLICES - 1)
    real, imag = spectrum(real, imag, table(CROP_LEFT), crop_right, crop_factor)
    product = from_right(jnp.concatenate([real, imag], axis=0), table(IMAGE_RIGHT))
    real = product[:K, :K] - product[K:, K:]
    imag = product[:K, K:] + product[K:, :K]
    out_ref[...] = from_left(table(IMAGE_LEFT), jnp.concatenate([real, imag], axis=0))


def probe_kernel(configs, block_ref, coef_ref, mine_ref, other_ref):
    here = block_ref.shape[0] // (2 * K)
    field = jnp.concatenate(
        [
            jnp.concatenate(
                [block_ref[pl.ds(2 * config + part, K, 2 * here), :] for part in range(2)], axis=0
            )
            for config in range(here)
        ],
        axis=1,
    )
    real, imag = coef_ref[0], coef_ref[1]
    table = jnp.concatenate(
        [jnp.concatenate([real, -imag], axis=1), jnp.concatenate([imag, real], axis=1)], axis=0
    )
    waves = from_left(split(table), field)
    probes = waves.shape[0] // 2
    real, imag = waves[:probes], waves[probes:]
    power = real * real + imag * imag
    total = sum(power[:, K * config : K * config + K] for config in range(here)) * (1.0 / configs)
    mine_ref[...] = total[: probes // 2]
    other_ref[...] = total[probes // 2 :]


VMEM = pl.BlockSpec(memory_space=pltpu.VMEM)
SMEM = pl.BlockSpec(memory_space=pltpu.SMEM)
PARAMS = pltpu.CompilerParams(vmem_limit_bytes=24 * 1024 * 1024)


def shape_of(dtype, *shape):
    return jax.ShapeDtypeStruct(shape, dtype)


def prepare(own, slab, tilts, aperture, positions):
    beams = tilts.shape[1]
    out = [
        shape_of(F32, 2, 2 * K, beams),
        shape_of(BF16, TABLE_ROWS, 2 * G),
        shape_of(F32, 2, ROWS, G),
        shape_of(F32, 2, G, K),
    ]
    return pl.pallas_call(
        prepare_kernel,
        out_shape=out,
        in_specs=[SMEM] * 3 + [VMEM] * 3,
        out_specs=[VMEM] * len(out),
        compiler_params=PARAMS,
        name="prepare",
    )(own, slab, tilts, tilts, aperture, positions)


def propagate(*operands):
    return pl.pallas_call(
        propagate_kernel,
        out_shape=shape_of(F32, 2 * K, K),
        in_specs=[SMEM] * 2 + [VMEM] * (len(operands) - 2),
        out_specs=VMEM,
        compiler_params=PARAMS,
        name="propagate",
    )(*operands)


def probe(block, coef, configs):
    quarter = coef.shape[1] // 2
    return pl.pallas_call(
        functools.partial(probe_kernel, configs),
        out_shape=[shape_of(F32, quarter, K)] * 2,
        in_specs=[VMEM] * 2,
        out_specs=[VMEM] * 2,
        compiler_params=PARAMS,
        name="probe",
    )(block, coef)


def copies_of(potential, count):
    return pl.pallas_call(
        copies_kernel,
        out_shape=shape_of(F32, count * SLICES, 4, K),
        in_specs=[VMEM],
        out_specs=VMEM,
        compiler_params=PARAMS,
        name="copies",
    )(potential)


def per_device(groups, potential, tilts, aperture, positions):
    near, far = groups
    devices = lax.axis_size("beam")
    pairs, cores = lax.axis_size("pair"), lax.axis_size("core")
    configs = pairs * cores
    beams = tilts.shape[0]

    part = lax.all_to_all(copies_of(potential, NEAR), "beam", 0, 0, axis_index_groups=near, tiled=True)

    own = lax.axis_index("beam").reshape(1)
    slab = lax.axis_index(("pair", "core")).reshape(1)
    tilts = tilts.T
    coef, *tables = prepare(own, slab, tilts, aperture.reshape(1, beams), positions.T)
    part, coef, *tables = lax.optimization_barrier((part, coef, *tables))
    part = part.reshape(NEAR * PIECE, K)
    whole = lax.all_to_all(
        jnp.broadcast_to(part[None], (FAR, *part.shape)), "beam", 0, 0, axis_index_groups=far
    ).reshape(devices * PIECE, K)
    image = propagate(own, tilts, whole, *tables)

    rows = jnp.broadcast_to(image.reshape(K, 1, 2, K), (K, pairs, 2, K)).reshape(pairs * K, 2, K)
    block = lax.all_to_all(rows, ("beam", "pair"), 0, 0, tiled=True).reshape(2 * pairs * beams, K)
    mine, other = probe(block, coef, configs)
    return mine + lax.ppermute(other, "core", [(0, 1), (1, 0)])


def exchange_groups():
    run, turned = range(NEAR), range(NEAR - 1, -1, -1)
    near = [[NEAR * x + i for i in (run if 2 * x < FAR else turned)] for x in range(FAR)]
    order = [*range(FAR // 2), *range(FAR - 1, FAR // 2 - 1, -1)]
    far = [[NEAR * x + i for x in order] for i in run]
    return near, far


def solution(mesh):
    fine = jax.sharding.Mesh(mesh.devices.reshape(-1, 2, 2), ("beam", "pair", "core"))
    return jax.shard_map(
        functools.partial(per_device, exchange_groups()),
        mesh=fine,
        in_specs=(P(("pair", "core"), None, "beam"), P(), P(), P()),
        out_specs=P(("pair", "core"), "beam"),
        check_vma=False,
    )
```

```python
import functools
import math

import jax
import jax.numpy as jnp
from jax import lax
from jax.experimental import pallas as pl
from jax.experimental.pallas import tpu as pltpu
from jax.sharding import PartitionSpec as P

G = 256
K = 128
SLICES = 3
LIMIT = (G // 3) ** 2
REACH = G // 3
ROWS = 176
NEAR, FAR = 32, 4
PIECE = SLICES * 4

FRESNEL_RATE = 0.00019
DEFOCUS_RATE = 0.01

F32 = jnp.float32
BF16 = jnp.bfloat16


def split(value):
    high = value.astype(BF16)
    return high, (value - high.astype(F32)).astype(BF16)


def sine_of(t):
    s = t * t
    sine = jnp.full_like(t, 2.60501958e-6)
    for term in (-1.9808983e-4, 8.33304978e-3, -1.66666579e-1, 0.999999996):
        sine = sine * s + term
    return sine * t


def cosine_of(t):
    s = t * t
    cosine = jnp.full_like(t, 2.31515759e-5)
    for term in (-1.38535979e-3, 4.16635698e-2, -0.499999047, 0.999999953):
        cosine = cosine * s + term
    return cosine


def half_angle(steps, length):
    near = ((steps + length // 2) & (length - 1)) - length // 2
    return near.astype(F32) * (math.pi / length)


def cosine_step(steps, length):
    sine = sine_of(half_angle(steps, length))
    return 1.0 - 2.0 * sine * sine


def circle(steps, length):
    half = half_angle(steps, length)
    sine = sine_of(half)
    return 2.0 * sine * cosine_of(half), 1.0 - 2.0 * sine * sine


def iota(shape, axis):
    return lax.broadcasted_iota(jnp.int32, shape, axis)


def natural(place):
    return place


def mixed(place):
    return 2 * (place & (G // 4 - 1)) + (place >> 6)


def position(place, order):
    n = order(place & (G // 2 - 1))
    return jnp.where(place < G // 2, n, G - 1 - n)


def folded(order, axis):
    place = iota((8, G) if axis else (G, K), axis)
    factor = 2 * order(place & (G // 2 - 1)) + 1
    return factor, jnp.where(place < G // 2, 0, -(G // 2))


def spread(value, shape):
    for axis in range(2):
        times = shape[axis] // value.shape[axis]
        if times > 1:
            value = jnp.concatenate([value] * times, axis=axis)
    return value


def signed(index, length):
    return jnp.where(index < length // 2, index, index - length)


def forward_table(shape, frequency, order, axis):
    factor, offset = (spread(value, shape) for value in folded(order, axis))
    return cosine_step(frequency(iota(shape, 1 - axis)) * factor + offset, 2 * G)


def fresnel(shape, frequency_u, frequency_v):
    u, v = frequency_u(iota(shape, 0)), frequency_v(iota(shape, 1))
    square = u * u + v * v
    angle = jnp.minimum(square, LIMIT).astype(F32) * FRESNEL_RATE
    keep = jnp.where(square <= LIMIT, 1.0 / (G * G), 0.0)
    return cosine_of(angle) * keep, -sine_of(angle) * keep


def copies_kernel(potential_ref, out_ref):
    values = potential_ref[0]
    pick = iota((K, K), 0) + iota((K, K), 1) == K - 1
    mirror = jnp.where(pick, 1.0, 0.0)
    quarters = [values[:, K * i : K * (i + 1)] for i in range(4)]
    for i in (1, 3):
        quarters[i] = jnp.dot(
            quarters[i], mirror, precision=lax.Precision.HIGHEST, preferred_element_type=F32
        )
    pieces = [
        jnp.concatenate([quarter[layer : layer + 1] for quarter in quarters], axis=0)[None]
        for layer in range(SLICES)
    ]
    out_ref[...] = jnp.concatenate(pieces * (out_ref.shape[0] // SLICES), axis=0)


AHEAD_LEFT = (0, ROWS, G)
AHEAD_RIGHT = (AHEAD_LEFT[0] + AHEAD_LEFT[1], G, G)
BACK_RIGHT = (AHEAD_RIGHT[0] + G, G, G)
BACK_LEFT = (BACK_RIGHT[0] + G, G, G)
CROP_LEFT = (BACK_LEFT[0] + G, K, G)
IMAGE_RIGHT = (CROP_LEFT[0] + K, K, 2 * K)
IMAGE_LEFT = (IMAGE_RIGHT[0] + K, 2 * K, 2 * K)
TABLE_ROWS = IMAGE_LEFT[0] + IMAGE_LEFT[1]

def terms(ref, where):
    row, rows, columns = where
    return ref[row : row + rows, :columns], ref[row : row + rows, G : G + columns]


def near(index):
    return index - ROWS // 2


def whole(index):
    return signed(index, G)


def centred(index):
    return index - K // 2


def prepare_kernel(
    own_ref, slab_ref, tilt_ref, tilts_ref, aperture_ref, positions_ref, coef_ref, table_ref, factor_ref, across_ref
):
    own = own_ref[0]
    across_ref[0], across_ref[1] = circle(tilt_ref[0, own] * position(iota((G, K), 0), mixed), G)
    factor_ref[0], factor_ref[1] = fresnel((ROWS, G), near, whole)

    tilts = tilts_ref[...]
    beams = tilts.shape[1]
    square = jnp.sum((tilts * tilts).astype(F32), axis=0, keepdims=True)
    angle = -DEFOCUS_RATE * jnp.broadcast_to(square, (8, beams))
    turns = jnp.floor(angle * (0.5 / math.pi) + 0.5)
    half = 0.5 * ((angle - turns * 6.28125) - turns * (2.0 * math.pi - 6.28125))
    sine, cosine = sine_of(half), cosine_of(half)
    amount = jnp.broadcast_to(aperture_ref[...].astype(F32) * (1.0 / math.sqrt(beams)), (8, beams))
    weight_re = spread(amount * (1.0 - 2.0 * sine * sine), (K, beams))
    weight_im = spread(amount * (2.0 * sine * cosine), (K, beams))
    none = jnp.zeros((6, K), F32)
    steep = jnp.concatenate([tilts.astype(F32), none], axis=0).astype(BF16)
    for core in range(2):
        at = pl.multiple_of((slab_ref[0] ^ core) * K, K)
        places = jnp.concatenate([positions_ref[:, pl.ds(at, K)].astype(F32), none], axis=0)
        steps = jnp.dot(places.T.astype(BF16), steep, preferred_element_type=F32)
        sine, cosine = circle(-steps.astype(jnp.int32), K)
        coef_ref[0, K * core : K * (core + 1), :] = cosine * weight_re - sine * weight_im
        coef_ref[1, K * core : K * (core + 1), :] = cosine * weight_im + sine * weight_re

    m, other = iota((2 * K, 2 * K), 0), iota((2 * K, 2 * K), 1)
    turn = (4 * (m >> 1) + 1) * centred(other & (K - 1)) + K * ((other >> 7) - (m & 1))
    left, right = iota((K, 2 * K), 0), iota((K, 2 * K), 1)
    for (row, rows, columns), table in (
        (AHEAD_LEFT, forward_table((ROWS, G), near, mixed, 1)),
        (AHEAD_RIGHT, forward_table((G, G), whole, natural, 0)),
        (BACK_RIGHT, forward_table((G, G), whole, natural, 1)),
        (BACK_LEFT, forward_table((G, G), near, mixed, 0)),
        (CROP_LEFT, forward_table((K, G), centred, mixed, 1)),
        (IMAGE_RIGHT, cosine_step(signed(left, K) * (4 * (right & (K - 1)) + 1) - K * (right >> 7), 2 * G)),
        (IMAGE_LEFT, cosine_step(turn, 2 * G)),
    ):
        high, low = split(table)
        table_ref[row : row + rows, :columns] = high
        table_ref[row : row + rows, G : G + columns] = low


def from_left(table, field):
    high, low = split(field)
    short = table[0].shape[1] - field.shape[0]
    if short:
        none = jnp.zeros((short, field.shape[1]), BF16)
        high, low = jnp.concatenate([high, none], axis=0), jnp.concatenate([low, none], axis=0)
    return jnp.dot(
        jnp.concatenate([table[0], table[0], table[1]], axis=1),
        jnp.concatenate([high, low, high], axis=0),
        preferred_element_type=F32,
    )


def from_right(field, table):
    table = jnp.concatenate([table[0], table[0], table[1]], axis=0)

    def product(rows):
        high, low = split(rows)
        return jnp.dot(jnp.concatenate([high, low, high], axis=1), table, preferred_element_type=F32)

    return jnp.concatenate([product(rows) for rows in halves(field, 0)], axis=0)


def halves(value, axis):
    half = value.shape[axis] // 2
    return lax.slice_in_dim(value, 0, half, axis=axis), lax.slice_in_dim(value, half, 2 * half, axis=axis)


def fold(real, imag, axis):
    real_ahead, real_back = halves(real, axis)
    imag_ahead, imag_back = halves(imag, axis)
    return (
        jnp.concatenate([real_ahead + real_back, imag_ahead - imag_back], axis=axis),
        jnp.concatenate([imag_ahead + imag_back, real_back - real_ahead], axis=axis),
    )


def unfold(real, imag, axis):
    real_even, real_odd = halves(real, axis)
    imag_even, imag_odd = halves(imag, axis)
    return (
        jnp.concatenate([real_even - imag_odd, real_even + imag_odd], axis=axis),
        jnp.concatenate([imag_even + real_odd, imag_even - real_odd], axis=axis),
    )


def spectrum(real, imag, left, right, factor):
    field = from_left(left, jnp.concatenate(fold(real, imag, 0), axis=1))
    field = jnp.concatenate(fold(*halves(field, 1), 1), axis=0)
    real, imag = halves(from_right(field, right), 0)
    return (
        real * factor[0] - imag * factor[1],
        real * factor[1] + imag * factor[0],
    )


def screened(real, imag, potential_ref, layer):
    count = G // 4

    def rows(half, parity, side):
        own = 4 * layer + 2 * (1 - parity if half else parity) + side
        return potential_ref[pl.ds(PIECE * count * half + own, count, PIECE), :]

    potential = jnp.concatenate(
        [
            jnp.concatenate([rows(half, parity, side) for side in range(2)], axis=1)
            for half in range(2)
            for parity in range(2)
        ],
        axis=0,
    )
    turned = potential - math.pi / 2
    sine, cosine = cosine_of(turned), sine_of(turned)
    return -(real * cosine + imag * sine), real * sine - imag * cosine


def plane_wave(across_ref, tilt_y):
    sine_x, cosine_x = (jnp.concatenate([across_ref[i]] * (G // K), axis=1) for i in range(2))
    sine_y, cosine_y = circle(tilt_y * position(iota((8, G), 1), natural), G)
    sine_y, cosine_y = (jnp.concatenate([value] * (G // 8), axis=0) for value in (sine_y, cosine_y))
    return cosine_x * cosine_y - sine_x * sine_y, sine_x * cosine_y + cosine_x * sine_y


def band_of(value):
    return jnp.where(iota((value.shape[0], K), 1) < K // 2, value[:, :K], value[:, K:])


def propagate_kernel(own_ref, tilt_ref, potential_ref, table_ref, factor_ref, across_ref, out_ref):
    table = functools.partial(terms, table_ref)
    real, imag = plane_wave(across_ref, tilt_ref[1, own_ref[0]])
    for layer in range(SLICES - 1):
        real, imag = screened(real, imag, potential_ref, layer)
        real, imag = spectrum(real, imag, table(AHEAD_LEFT), table(AHEAD_RIGHT), factor_ref)
        field = from_right(jnp.concatenate([real, imag], axis=0), table(BACK_RIGHT))
        field = jnp.concatenate(unfold(*halves(field, 0), 1), axis=1)
        real, imag = unfold(*halves(from_left(table(BACK_LEFT), field), 1), 0)
    crop_right = [band_of(term) for term in table(AHEAD_RIGHT)]
    first = (ROWS - K) // 2
    crop_factor = [band_of(factor_ref[i, first : first + K, :]) for i in range(2)]
    real, imag = screened(real, imag, potential_ref, SLICES - 1)
    real, imag = spectrum(real, imag, table(CROP_LEFT), crop_right, crop_factor)
    product = from_right(jnp.concatenate([real, imag], axis=0), table(IMAGE_RIGHT))
    real = product[:K, :K] - product[K:, K:]
    imag = product[:K, K:] + product[K:, :K]
    out_ref[...] = from_left(table(IMAGE_LEFT), jnp.concatenate([real, imag], axis=0))


def sort_kernel(pairs, in_ref, out_ref):
    for x in range(FAR):
        for part in range(2):
            rows = in_ref[pl.ds(2 * NEAR * x + part, NEAR, 2), :]
            for pair in range(pairs):
                out_ref[pl.ds(2 * (FAR * pair + x) + part, NEAR, 2 * FAR * pairs), :] = rows


def probe_kernel(configs, block_ref, coef_ref, mine_ref, other_ref):
    here = block_ref.shape[0] // (2 * K)
    stride = 2 * FAR * here
    field = jnp.concatenate(
        [
            jnp.concatenate(
                [
                    block_ref[pl.ds(2 * (FAR * config + x) + part, NEAR, stride), :]
                    for part in range(2)
                    for x in range(FAR)
                ],
                axis=0,
            )
            for config in range(here)
        ],
        axis=1,
    )
    real, imag = coef_ref[0], coef_ref[1]
    table = jnp.concatenate(
        [jnp.concatenate([real, -imag], axis=1), jnp.concatenate([imag, real], axis=1)], axis=0
    )
    waves = from_left(split(table), field)
    probes = waves.shape[0] // 2
    real, imag = waves[:probes], waves[probes:]
    power = real * real + imag * imag
    total = sum(power[:, K * config : K * config + K] for config in range(here)) * (1.0 / configs)
    mine_ref[...] = total[: probes // 2]
    other_ref[...] = total[probes // 2 :]


BEAM = ("x", "place")
VMEM = pl.BlockSpec(memory_space=pltpu.VMEM)
SMEM = pl.BlockSpec(memory_space=pltpu.SMEM)
PARAMS = pltpu.CompilerParams(vmem_limit_bytes=24 * 1024 * 1024)


def shape_of(dtype, *shape):
    return jax.ShapeDtypeStruct(shape, dtype)


def prepare(own, slab, tilts, aperture, positions):
    beams = tilts.shape[1]
    out = [
        shape_of(F32, 2, 2 * K, beams),
        shape_of(BF16, TABLE_ROWS, 2 * G),
        shape_of(F32, 2, ROWS, G),
        shape_of(F32, 2, G, K),
    ]
    return pl.pallas_call(
        prepare_kernel,
        out_shape=out,
        in_specs=[SMEM] * 3 + [VMEM] * 3,
        out_specs=[VMEM] * len(out),
        compiler_params=PARAMS,
        name="prepare",
    )(own, slab, tilts, tilts, aperture, positions)


def propagate(*operands):
    return pl.pallas_call(
        propagate_kernel,
        out_shape=shape_of(F32, 2 * K, K),
        in_specs=[SMEM] * 2 + [VMEM] * (len(operands) - 2),
        out_specs=VMEM,
        compiler_params=PARAMS,
        name="propagate",
    )(*operands)


def probe(block, coef, configs):
    quarter = coef.shape[1] // 2
    return pl.pallas_call(
        functools.partial(probe_kernel, configs),
        out_shape=[shape_of(F32, quarter, K)] * 2,
        in_specs=[VMEM] * 2,
        out_specs=[VMEM] * 2,
        compiler_params=PARAMS,
        name="probe",
    )(block, coef)


def sorted_rows(rows, pairs):
    return pl.pallas_call(
        functools.partial(sort_kernel, pairs),
        out_shape=shape_of(F32, pairs * rows.shape[0], K),
        in_specs=[VMEM],
        out_specs=VMEM,
        compiler_params=PARAMS,
        name="sort",
    )(rows)


def copies_of(potential, count):
    return pl.pallas_call(
        copies_kernel,
        out_shape=shape_of(F32, count * SLICES, 4, K),
        in_specs=[VMEM],
        out_specs=VMEM,
        compiler_params=PARAMS,
        name="copies",
    )(potential)


def per_device(groups, potential, tilts, aperture, positions):
    near, far = groups
    devices = lax.axis_size(BEAM)
    pairs, cores = lax.axis_size("pair"), lax.axis_size("core")
    configs = pairs * cores
    beams = tilts.shape[0]

    part = lax.all_to_all(copies_of(potential, NEAR), BEAM, 0, 0, axis_index_groups=near, tiled=True)

    own = lax.axis_index(BEAM).reshape(1)
    slab = lax.axis_index(("pair", "core")).reshape(1)
    tilts = tilts.T
    coef, *tables = prepare(own, slab, tilts, aperture.reshape(1, beams), positions.T)
    part, coef, *tables = lax.optimization_barrier((part, coef, *tables))
    part = part.reshape(NEAR * PIECE, K)
    whole = lax.all_to_all(
        jnp.broadcast_to(part[None], (FAR, *part.shape)), BEAM, 0, 0, axis_index_groups=far
    ).reshape(devices * PIECE, K)
    image = propagate(own, tilts, whole, *tables)

    rows = lax.all_to_all(image.reshape(FAR, NEAR * 2, K), "x", 0, 0)
    rows = sorted_rows(rows.reshape(2 * K, K), pairs).reshape(NEAR * pairs, 2 * FAR, K)
    block = lax.all_to_all(rows, ("place", "pair"), 0, 0, tiled=True).reshape(2 * pairs * beams, K)
    mine, other = probe(block, coef, configs)
    return mine + lax.ppermute(other, "core", [(0, 1), (1, 0)])


def exchange_groups():
    run, turned = range(NEAR), range(NEAR - 1, -1, -1)
    near = [[NEAR * x + i for i in (run if 2 * x < FAR else turned)] for x in range(FAR)]
    order = [*range(FAR // 2), *range(FAR - 1, FAR // 2 - 1, -1)]
    far = [[NEAR * x + i for x in order] for i in run]
    return near, far


def solution(mesh):
    fine = jax.sharding.Mesh(mesh.devices.reshape(FAR, NEAR, 2, 2), (*BEAM, "pair", "core"))
    return jax.shard_map(
        functools.partial(per_device, exchange_groups()),
        mesh=fine,
        in_specs=(P(("pair", "core"), None, BEAM), P(), P(), P()),
        out_specs=P(("pair", "core"), BEAM),
        check_vma=False,
    )
```

```python
import functools
import math

import jax
import jax.numpy as jnp
from jax import lax
from jax.experimental import pallas as pl
from jax.experimental.pallas import tpu as pltpu
from jax.sharding import PartitionSpec as P

G = 256
K = 128
SLICES = 3
LIMIT = (G // 3) ** 2
REACH = G // 3
ROWS = 176
NEAR, FAR = 32, 4
PIECE = SLICES * 4

FRESNEL_RATE = 0.00019
DEFOCUS_RATE = 0.01

F32 = jnp.float32
BF16 = jnp.bfloat16


def split(value):
    high = value.astype(BF16)
    return high, (value - high.astype(F32)).astype(BF16)


def sine_of(t):
    s = t * t
    sine = jnp.full_like(t, 2.60501958e-6)
    for term in (-1.9808983e-4, 8.33304978e-3, -1.66666579e-1, 0.999999996):
        sine = sine * s + term
    return sine * t


def cosine_of(t):
    s = t * t
    cosine = jnp.full_like(t, 2.31515759e-5)
    for term in (-1.38535979e-3, 4.16635698e-2, -0.499999047, 0.999999953):
        cosine = cosine * s + term
    return cosine


def half_angle(steps, length):
    near = ((steps + length // 2) & (length - 1)) - length // 2
    return near.astype(F32) * (math.pi / length)


def cosine_step(steps, length):
    sine = sine_of(half_angle(steps, length))
    return 1.0 - 2.0 * sine * sine


def circle(steps, length):
    half = half_angle(steps, length)
    sine = sine_of(half)
    return 2.0 * sine * cosine_of(half), 1.0 - 2.0 * sine * sine


def iota(shape, axis):
    return lax.broadcasted_iota(jnp.int32, shape, axis)


def natural(place):
    return place


def mixed(place):
    return 2 * (place & (G // 4 - 1)) + (place >> 6)


def position(place, order):
    n = order(place & (G // 2 - 1))
    return jnp.where(place < G // 2, n, G - 1 - n)


def folded(order, axis):
    place = iota((8, G) if axis else (G, K), axis)
    factor = 2 * order(place & (G // 2 - 1)) + 1
    return factor, jnp.where(place < G // 2, 0, -(G // 2))


def spread(value, shape):
    for axis in range(2):
        times = shape[axis] // value.shape[axis]
        if times > 1:
            value = jnp.concatenate([value] * times, axis=axis)
    return value


def signed(index, length):
    return jnp.where(index < length // 2, index, index - length)


def forward_table(shape, frequency, order, axis):
    factor, offset = (spread(value, shape) for value in folded(order, axis))
    return cosine_step(frequency(iota(shape, 1 - axis)) * factor + offset, 2 * G)


def fresnel(shape, frequency_u, frequency_v):
    u, v = frequency_u(iota(shape, 0)), frequency_v(iota(shape, 1))
    square = u * u + v * v
    angle = jnp.minimum(square, LIMIT).astype(F32) * FRESNEL_RATE
    keep = jnp.where(square <= LIMIT, 1.0 / (G * G), 0.0)
    return cosine_of(angle) * keep, -sine_of(angle) * keep


def copies_kernel(potential_ref, out_ref):
    mirror = jnp.where(iota((K, K), 0) + iota((K, K), 1) == K - 1, 1.0, 0.0)
    pieces = []
    for layer in range(SLICES):
        rows = potential_ref[layer]
        turned = jnp.dot(rows, mirror, precision=lax.Precision.HIGHEST, preferred_element_type=F32)
        pieces.append(jnp.where((iota(rows.shape, 0) & 1) == 1, turned, rows)[None])
    out_ref[...] = jnp.concatenate(pieces * (out_ref.shape[0] // SLICES), axis=0)


AHEAD_LEFT = (0, ROWS, G)
AHEAD_RIGHT = (AHEAD_LEFT[0] + AHEAD_LEFT[1], G, G)
BACK_RIGHT = (AHEAD_RIGHT[0] + G, G, G)
BACK_LEFT = (BACK_RIGHT[0] + G, G, G)
CROP_LEFT = (BACK_LEFT[0] + G, K, G)
IMAGE_RIGHT = (CROP_LEFT[0] + K, K, 2 * K)
IMAGE_LEFT = (IMAGE_RIGHT[0] + K, 2 * K, 2 * K)
TABLE_ROWS = IMAGE_LEFT[0] + IMAGE_LEFT[1]

def terms(ref, where):
    row, rows, columns = where
    return ref[row : row + rows, :columns], ref[row : row + rows, G : G + columns]


def near(index):
    return index - ROWS // 2


def whole(index):
    return signed(index, G)


def centred(index):
    return index - K // 2


def prepare_kernel(
    own_ref, slab_ref, tilt_ref, tilts_ref, aperture_ref, positions_ref, coef_ref, table_ref, factor_ref, across_ref
):
    own = own_ref[0]
    across_ref[0], across_ref[1] = circle(tilt_ref[0, own] * position(iota((G, K), 0), mixed), G)
    factor_ref[0], factor_ref[1] = fresnel((ROWS, G), near, whole)

    tilts = tilts_ref[...]
    beams = tilts.shape[1]
    square = jnp.sum((tilts * tilts).astype(F32), axis=0, keepdims=True)
    angle = -DEFOCUS_RATE * jnp.broadcast_to(square, (8, beams))
    turns = jnp.floor(angle * (0.5 / math.pi) + 0.5)
    half = 0.5 * ((angle - turns * 6.28125) - turns * (2.0 * math.pi - 6.28125))
    sine, cosine = sine_of(half), cosine_of(half)
    amount = jnp.broadcast_to(aperture_ref[...].astype(F32) * (1.0 / math.sqrt(beams)), (8, beams))
    weight_re = spread(amount * (1.0 - 2.0 * sine * sine), (K, beams))
    weight_im = spread(amount * (2.0 * sine * cosine), (K, beams))
    none = jnp.zeros((6, K), F32)
    steep = jnp.concatenate([tilts.astype(F32), none], axis=0).astype(BF16)
    for core in range(2):
        at = pl.multiple_of((slab_ref[0] ^ core) * K, K)
        places = jnp.concatenate([positions_ref[:, pl.ds(at, K)].astype(F32), none], axis=0)
        steps = jnp.dot(places.T.astype(BF16), steep, preferred_element_type=F32)
        sine, cosine = circle(-steps.astype(jnp.int32), K)
        coef_ref[0, K * core : K * (core + 1), :] = cosine * weight_re - sine * weight_im
        coef_ref[1, K * core : K * (core + 1), :] = cosine * weight_im + sine * weight_re

    m, other = iota((2 * K, 2 * K), 0), iota((2 * K, 2 * K), 1)
    row = NEAR * ((m >> 1) & (FAR - 1)) + (m >> 3)
    turn = (4 * row + 1) * centred(other & (K - 1)) + K * ((other >> 7) - (m & 1))
    left, right = iota((K, 2 * K), 0), iota((K, 2 * K), 1)
    for (row, rows, columns), table in (
        (AHEAD_LEFT, forward_table((ROWS, G), near, mixed, 1)),
        (AHEAD_RIGHT, forward_table((G, G), whole, natural, 0)),
        (BACK_RIGHT, forward_table((G, G), whole, natural, 1)),
        (BACK_LEFT, forward_table((G, G), near, mixed, 0)),
        (CROP_LEFT, forward_table((K, G), centred, mixed, 1)),
        (IMAGE_RIGHT, cosine_step(signed(left, K) * (4 * (right & (K - 1)) + 1) - K * (right >> 7), 2 * G)),
        (IMAGE_LEFT, cosine_step(turn, 2 * G)),
    ):
        high, low = split(table)
        table_ref[row : row + rows, :columns] = high
        table_ref[row : row + rows, G : G + columns] = low


def from_left(table, field):
    high, low = split(field)
    short = table[0].shape[1] - field.shape[0]
    if short:
        none = jnp.zeros((short, field.shape[1]), BF16)
        high, low = jnp.concatenate([high, none], axis=0), jnp.concatenate([low, none], axis=0)
    return jnp.dot(
        jnp.concatenate([table[0], table[0], table[1]], axis=1),
        jnp.concatenate([high, low, high], axis=0),
        preferred_element_type=F32,
    )


def from_right(field, table):
    table = jnp.concatenate([table[0], table[0], table[1]], axis=0)

    def product(rows):
        high, low = split(rows)
        return jnp.dot(jnp.concatenate([high, low, high], axis=1), table, preferred_element_type=F32)

    return jnp.concatenate([product(rows) for rows in halves(field, 0)], axis=0)


def halves(value, axis):
    half = value.shape[axis] // 2
    return lax.slice_in_dim(value, 0, half, axis=axis), lax.slice_in_dim(value, half, 2 * half, axis=axis)


def fold(real, imag, axis):
    real_ahead, real_back = halves(real, axis)
    imag_ahead, imag_back = halves(imag, axis)
    return (
        jnp.concatenate([real_ahead + real_back, imag_ahead - imag_back], axis=axis),
        jnp.concatenate([imag_ahead + imag_back, real_back - real_ahead], axis=axis),
    )


def unfold(real, imag, axis):
    real_even, real_odd = halves(real, axis)
    imag_even, imag_odd = halves(imag, axis)
    return (
        jnp.concatenate([real_even - imag_odd, real_even + imag_odd], axis=axis),
        jnp.concatenate([imag_even + real_odd, imag_even - real_odd], axis=axis),
    )


def spectrum(real, imag, left, right, factor):
    field = from_left(left, jnp.concatenate(fold(real, imag, 0), axis=1))
    field = jnp.concatenate(fold(*halves(field, 1), 1), axis=0)
    real, imag = halves(from_right(field, right), 0)
    return (
        real * factor[0] - imag * factor[1],
        real * factor[1] + imag * factor[0],
    )


def screened(real, imag, potential_ref, layer):
    count = G // 4

    def rows(half, parity, side):
        own = 4 * layer + 2 * (1 - parity if half else parity) + side
        return potential_ref[pl.ds(PIECE * count * half + own, count, PIECE), :]

    potential = jnp.concatenate(
        [
            jnp.concatenate([rows(half, parity, side) for side in range(2)], axis=1)
            for half in range(2)
            for parity in range(2)
        ],
        axis=0,
    )
    turned = potential - math.pi / 2
    sine, cosine = cosine_of(turned), sine_of(turned)
    return -(real * cosine + imag * sine), real * sine - imag * cosine


def plane_wave(across_ref, tilt_y):
    sine_x, cosine_x = (jnp.concatenate([across_ref[i]] * (G // K), axis=1) for i in range(2))
    sine_y, cosine_y = circle(tilt_y * position(iota((8, G), 1), natural), G)
    sine_y, cosine_y = (jnp.concatenate([value] * (G // 8), axis=0) for value in (sine_y, cosine_y))
    return cosine_x * cosine_y - sine_x * sine_y, sine_x * cosine_y + cosine_x * sine_y


def band_of(value):
    return jnp.where(iota((value.shape[0], K), 1) < K // 2, value[:, :K], value[:, K:])


def propagate_kernel(own_ref, tilt_ref, potential_ref, table_ref, factor_ref, across_ref, out_ref):
    table = functools.partial(terms, table_ref)
    real, imag = plane_wave(across_ref, tilt_ref[1, own_ref[0]])
    for layer in range(SLICES - 1):
        real, imag = screened(real, imag, potential_ref, layer)
        real, imag = spectrum(real, imag, table(AHEAD_LEFT), table(AHEAD_RIGHT), factor_ref)
        field = from_right(jnp.concatenate([real, imag], axis=0), table(BACK_RIGHT))
        field = jnp.concatenate(unfold(*halves(field, 0), 1), axis=1)
        real, imag = unfold(*halves(from_left(table(BACK_LEFT), field), 1), 0)
    crop_right = [band_of(term) for term in table(AHEAD_RIGHT)]
    first = (ROWS - K) // 2
    crop_factor = [band_of(factor_ref[i, first : first + K, :]) for i in range(2)]
    real, imag = screened(real, imag, potential_ref, SLICES - 1)
    real, imag = spectrum(real, imag, table(CROP_LEFT), crop_right, crop_factor)
    product = from_right(jnp.concatenate([real, imag], axis=0), table(IMAGE_RIGHT))
    real = product[:K, :K] - product[K:, K:]
    imag = product[:K, K:] + product[K:, :K]
    out_ref[...] = from_left(table(IMAGE_LEFT), jnp.concatenate([real, imag], axis=0))


def probe_kernel(configs, block_ref, coef_ref, mine_ref, other_ref):
    here = block_ref.shape[0] // (2 * K)
    stride = 2 * FAR * here
    field = jnp.concatenate(
        [
            jnp.concatenate(
                [
                    block_ref[pl.ds(2 * (here * x + config) + part, NEAR, stride), :]
                    for part in range(2)
                    for x in range(FAR)
                ],
                axis=0,
            )
            for config in range(here)
        ],
        axis=1,
    )
    real, imag = coef_ref[0], coef_ref[1]
    table = jnp.concatenate(
        [jnp.concatenate([real, -imag], axis=1), jnp.concatenate([imag, real], axis=1)], axis=0
    )
    waves = from_left(split(table), field)
    probes = waves.shape[0] // 2
    real, imag = waves[:probes], waves[probes:]
    power = real * real + imag * imag
    total = sum(power[:, K * config : K * config + K] for config in range(here)) * (1.0 / configs)
    mine_ref[...] = total[: probes // 2]
    other_ref[...] = total[probes // 2 :]


BEAM = ("x", "place")
VMEM = pl.BlockSpec(memory_space=pltpu.VMEM)
SMEM = pl.BlockSpec(memory_space=pltpu.SMEM)
PARAMS = pltpu.CompilerParams(vmem_limit_bytes=24 * 1024 * 1024)


def shape_of(dtype, *shape):
    return jax.ShapeDtypeStruct(shape, dtype)


def prepare(own, slab, tilts, aperture, positions):
    beams = tilts.shape[1]
    out = [
        shape_of(F32, 2, 2 * K, beams),
        shape_of(BF16, TABLE_ROWS, 2 * G),
        shape_of(F32, 2, ROWS, G),
        shape_of(F32, 2, G, K),
    ]
    return pl.pallas_call(
        prepare_kernel,
        out_shape=out,
        in_specs=[SMEM] * 3 + [VMEM] * 3,
        out_specs=[VMEM] * len(out),
        compiler_params=PARAMS,
        name="prepare",
    )(own, slab, tilts, tilts, aperture, positions)


def propagate(*operands):
    return pl.pallas_call(
        propagate_kernel,
        out_shape=shape_of(F32, 2 * K, K),
        in_specs=[SMEM] * 2 + [VMEM] * (len(operands) - 2),
        out_specs=VMEM,
        compiler_params=PARAMS,
        name="propagate",
    )(*operands)


def probe(block, coef, configs):
    quarter = coef.shape[1] // 2
    return pl.pallas_call(
        functools.partial(probe_kernel, configs),
        out_shape=[shape_of(F32, quarter, K)] * 2,
        in_specs=[VMEM] * 2,
        out_specs=[VMEM] * 2,
        compiler_params=PARAMS,
        name="probe",
    )(block, coef)


def copies_of(potential, count):
    return pl.pallas_call(
        copies_kernel,
        out_shape=shape_of(F32, count * SLICES, 4, K),
        in_specs=[VMEM],
        out_specs=VMEM,
        compiler_params=pltpu.CompilerParams(vmem_limit_bytes=60 * 1024 * 1024),
        name="copies",
    )(potential.transpose(1, 0, 2).reshape(SLICES, 4, K))


def per_device(groups, potential, tilts, aperture, positions):
    near, far = groups
    devices = lax.axis_size(BEAM)
    pairs, cores = lax.axis_size("pair"), lax.axis_size("core")
    configs = pairs * cores
    beams = tilts.shape[0]

    part = lax.all_to_all(copies_of(potential, NEAR), BEAM, 0, 0, axis_index_groups=near, tiled=True)

    own = lax.axis_index(BEAM).reshape(1)
    slab = lax.axis_index(("pair", "core")).reshape(1)
    tilts = tilts.T
    coef, *tables = prepare(own, slab, tilts, aperture.reshape(1, beams), positions.T)
    part, coef, *tables = lax.optimization_barrier((part, coef, *tables))
    part = part.reshape(NEAR * PIECE, K)
    whole = lax.all_to_all(
        jnp.broadcast_to(part[None], (FAR, *part.shape)), BEAM, 0, 0, axis_index_groups=far
    ).reshape(devices * PIECE, K)
    image = propagate(own, tilts, whole, *tables)

    rows = jnp.broadcast_to(image.reshape(K, 1, 2, K), (K, pairs, 2, K)).reshape(pairs * K, 2, K)
    block = lax.all_to_all(rows, ("place", "x", "pair"), 0, 0, tiled=True).reshape(2 * pairs * beams, K)
    mine, other = probe(block, coef, configs)
    return mine + lax.ppermute(other, "core", [(0, 1), (1, 0)])


def exchange_groups():
    run, turned = range(NEAR), range(NEAR - 1, -1, -1)
    near = [[NEAR * x + i for i in (run if 2 * x < FAR else turned)] for x in range(FAR)]
    order = [*range(FAR // 2), *range(FAR - 1, FAR // 2 - 1, -1)]
    far = [[NEAR * x + i for x in order] for i in run]
    return near, far


def solution(mesh):
    fine = jax.sharding.Mesh(mesh.devices.reshape(FAR, NEAR, 2, 2), (*BEAM, "pair", "core"))
    return jax.shard_map(
        functools.partial(per_device, exchange_groups()),
        mesh=fine,
        in_specs=(P(("pair", "core"), None, BEAM), P(), P(), P()),
        out_specs=P(("pair", "core"), BEAM),
        check_vma=False,
    )
```

```python
import functools
import math

import jax
import jax.numpy as jnp
from jax import lax
from jax.experimental import pallas as pl
from jax.experimental.pallas import tpu as pltpu
from jax.sharding import PartitionSpec as P

G = 256
K = 128
SLICES = 3
LIMIT = (G // 3) ** 2
REACH = G // 3
ROWS = 176
NEAR, FAR = 32, 4
PIECE = SLICES * 4

FRESNEL_RATE = 0.00019
DEFOCUS_RATE = 0.01

F32 = jnp.float32
BF16 = jnp.bfloat16


def split(value):
    high = value.astype(BF16)
    return high, (value - high.astype(F32)).astype(BF16)


def sine_of(t):
    s = t * t
    sine = jnp.full_like(t, 2.60501958e-6)
    for term in (-1.9808983e-4, 8.33304978e-3, -1.66666579e-1, 0.999999996):
        sine = sine * s + term
    return sine * t


def cosine_of(t):
    s = t * t
    cosine = jnp.full_like(t, 2.31515759e-5)
    for term in (-1.38535979e-3, 4.16635698e-2, -0.499999047, 0.999999953):
        cosine = cosine * s + term
    return cosine


def half_angle(steps, length):
    near = ((steps + length // 2) & (length - 1)) - length // 2
    return near.astype(F32) * (math.pi / length)


def cosine_step(steps, length):
    sine = sine_of(half_angle(steps, length))
    return 1.0 - 2.0 * sine * sine


def circle(steps, length):
    half = half_angle(steps, length)
    sine = sine_of(half)
    return 2.0 * sine * cosine_of(half), 1.0 - 2.0 * sine * sine


def iota(shape, axis):
    return lax.broadcasted_iota(jnp.int32, shape, axis)


def natural(place):
    return place


def mixed(place):
    return 2 * (place & (G // 4 - 1)) + (place >> 6)


def position(place, order):
    n = order(place & (G // 2 - 1))
    return jnp.where(place < G // 2, n, G - 1 - n)


def folded(order, axis):
    place = iota((8, G) if axis else (G, K), axis)
    factor = 2 * order(place & (G // 2 - 1)) + 1
    return factor, jnp.where(place < G // 2, 0, -(G // 2))


def spread(value, shape):
    for axis in range(2):
        times = shape[axis] // value.shape[axis]
        if times > 1:
            value = jnp.concatenate([value] * times, axis=axis)
    return value


def signed(index, length):
    return jnp.where(index < length // 2, index, index - length)


def forward_table(shape, frequency, order, axis):
    factor, offset = (spread(value, shape) for value in folded(order, axis))
    return cosine_step(frequency(iota(shape, 1 - axis)) * factor + offset, 2 * G)


def fresnel(shape, frequency_u, frequency_v):
    u, v = frequency_u(iota(shape, 0)), frequency_v(iota(shape, 1))
    square = u * u + v * v
    angle = jnp.minimum(square, LIMIT).astype(F32) * FRESNEL_RATE
    keep = jnp.where(square <= LIMIT, 1.0 / (G * G), 0.0)
    return cosine_of(angle) * keep, -sine_of(angle) * keep


def copies_kernel(potential_ref, out_ref):
    mirror = jnp.where(iota((K, K), 0) + iota((K, K), 1) == K - 1, 1.0, 0.0)
    rows = jnp.concatenate([potential_ref[layer] for layer in range(SLICES)], axis=0)
    turned = jnp.dot(rows, mirror, precision=lax.Precision.HIGHEST, preferred_element_type=F32)
    rows = jnp.where((iota(rows.shape, 0) & 1) == 1, turned, rows)
    pieces = [rows[4 * layer : 4 * (layer + 1)][None] for layer in range(SLICES)]
    out_ref[...] = jnp.concatenate(pieces * (out_ref.shape[0] // SLICES), axis=0)


AHEAD_LEFT = (0, ROWS, G)
AHEAD_RIGHT = (AHEAD_LEFT[0] + AHEAD_LEFT[1], G, G)
BACK_RIGHT = (AHEAD_RIGHT[0] + G, G, G)
BACK_LEFT = (BACK_RIGHT[0] + G, G, G)
CROP_LEFT = (BACK_LEFT[0] + G, K, G)
IMAGE_RIGHT = (CROP_LEFT[0] + K, K, 2 * K)
IMAGE_LEFT = (IMAGE_RIGHT[0] + K, 2 * K, 2 * K)
TABLE_ROWS = IMAGE_LEFT[0] + IMAGE_LEFT[1]

def terms(ref, where):
    row, rows, columns = where
    return ref[row : row + rows, :columns], ref[row : row + rows, G : G + columns]


def near(index):
    return index - ROWS // 2


def whole(index):
    return signed(index, G)


def centred(index):
    return index - K // 2


def prepare_kernel(
    own_ref, slab_ref, tilt_ref, tilts_ref, aperture_ref, positions_ref, coef_ref, table_ref, factor_ref, across_ref
):
    own = own_ref[0]
    across_ref[0], across_ref[1] = circle(tilt_ref[0, own] * position(iota((G, K), 0), mixed), G)
    factor_ref[0], factor_ref[1] = fresnel((ROWS, G), near, whole)

    tilts = tilts_ref[...]
    beams = tilts.shape[1]
    square = jnp.sum((tilts * tilts).astype(F32), axis=0, keepdims=True)
    angle = -DEFOCUS_RATE * jnp.broadcast_to(square, (8, beams))
    turns = jnp.floor(angle * (0.5 / math.pi) + 0.5)
    half = 0.5 * ((angle - turns * 6.28125) - turns * (2.0 * math.pi - 6.28125))
    sine, cosine = sine_of(half), cosine_of(half)
    amount = jnp.broadcast_to(aperture_ref[...].astype(F32) * (1.0 / math.sqrt(beams)), (8, beams))
    weight_re = spread(amount * (1.0 - 2.0 * sine * sine), (K, beams))
    weight_im = spread(amount * (2.0 * sine * cosine), (K, beams))
    none = jnp.zeros((6, K), F32)
    steep = jnp.concatenate([tilts.astype(F32), none], axis=0).astype(BF16)
    for core in range(2):
        at = pl.multiple_of((slab_ref[0] ^ core) * K, K)
        places = jnp.concatenate([positions_ref[:, pl.ds(at, K)].astype(F32), none], axis=0)
        steps = jnp.dot(places.T.astype(BF16), steep, preferred_element_type=F32)
        sine, cosine = circle(-steps.astype(jnp.int32), K)
        coef_ref[0, K * core : K * (core + 1), :] = cosine * weight_re - sine * weight_im
        coef_ref[1, K * core : K * (core + 1), :] = cosine * weight_im + sine * weight_re

    m, other = iota((2 * K, 2 * K), 0), iota((2 * K, 2 * K), 1)
    row = NEAR * ((m >> 1) & (FAR - 1)) + (m >> 3)
    turn = (4 * row + 1) * centred(other & (K - 1)) + K * ((other >> 7) - (m & 1))
    left, right = iota((K, 2 * K), 0), iota((K, 2 * K), 1)
    for (row, rows, columns), table in (
        (AHEAD_LEFT, forward_table((ROWS, G), near, mixed, 1)),
        (AHEAD_RIGHT, forward_table((G, G), whole, natural, 0)),
        (BACK_RIGHT, forward_table((G, G), whole, natural, 1)),
        (BACK_LEFT, forward_table((G, G), near, mixed, 0)),
        (CROP_LEFT, forward_table((K, G), centred, mixed, 1)),
        (IMAGE_RIGHT, cosine_step(signed(left, K) * (4 * (right & (K - 1)) + 1) - K * (right >> 7), 2 * G)),
        (IMAGE_LEFT, cosine_step(turn, 2 * G)),
    ):
        high, low = split(table)
        table_ref[row : row + rows, :columns] = high
        table_ref[row : row + rows, G : G + columns] = low


def from_left(table, field):
    high, low = split(field)
    short = table[0].shape[1] - field.shape[0]
    if short:
        none = jnp.zeros((short, field.shape[1]), BF16)
        high, low = jnp.concatenate([high, none], axis=0), jnp.concatenate([low, none], axis=0)
    return jnp.dot(
        jnp.concatenate([table[0], table[0], table[1]], axis=1),
        jnp.concatenate([high, low, high], axis=0),
        preferred_element_type=F32,
    )


def from_right(field, table):
    table = jnp.concatenate([table[0], table[0], table[1]], axis=0)

    def product(rows):
        high, low = split(rows)
        return jnp.dot(jnp.concatenate([high, low, high], axis=1), table, preferred_element_type=F32)

    return jnp.concatenate([product(rows) for rows in halves(field, 0)], axis=0)


def halves(value, axis):
    half = value.shape[axis] // 2
    return lax.slice_in_dim(value, 0, half, axis=axis), lax.slice_in_dim(value, half, 2 * half, axis=axis)


def fold(real, imag, axis):
    real_ahead, real_back = halves(real, axis)
    imag_ahead, imag_back = halves(imag, axis)
    return (
        jnp.concatenate([real_ahead + real_back, imag_ahead - imag_back], axis=axis),
        jnp.concatenate([imag_ahead + imag_back, real_back - real_ahead], axis=axis),
    )


def unfold(real, imag, axis):
    real_even, real_odd = halves(real, axis)
    imag_even, imag_odd = halves(imag, axis)
    return (
        jnp.concatenate([real_even - imag_odd, real_even + imag_odd], axis=axis),
        jnp.concatenate([imag_even + real_odd, imag_even - real_odd], axis=axis),
    )


def spectrum(real, imag, left, right, factor):
    field = from_left(left, jnp.concatenate(fold(real, imag, 0), axis=1))
    field = jnp.concatenate(fold(*halves(field, 1), 1), axis=0)
    real, imag = halves(from_right(field, right), 0)
    return (
        real * factor[0] - imag * factor[1],
        real * factor[1] + imag * factor[0],
    )


def screened(real, imag, potential_ref, layer):
    count = G // 4

    def rows(half, parity, side):
        own = 4 * layer + 2 * (1 - parity if half else parity) + side
        return potential_ref[pl.ds(PIECE * count * half + own, count, PIECE), :]

    potential = jnp.concatenate(
        [
            jnp.concatenate([rows(half, parity, side) for side in range(2)], axis=1)
            for half in range(2)
            for parity in range(2)
        ],
        axis=0,
    )
    turned = potential - math.pi / 2
    sine, cosine = cosine_of(turned), sine_of(turned)
    return -(real * cosine + imag * sine), real * sine - imag * cosine


def plane_wave(across_ref, tilt_y):
    sine_x, cosine_x = (jnp.concatenate([across_ref[i]] * (G // K), axis=1) for i in range(2))
    sine_y, cosine_y = circle(tilt_y * position(iota((8, G), 1), natural), G)
    sine_y, cosine_y = (jnp.concatenate([value] * (G // 8), axis=0) for value in (sine_y, cosine_y))
    return cosine_x * cosine_y - sine_x * sine_y, sine_x * cosine_y + cosine_x * sine_y


def band_of(value):
    return jnp.where(iota((value.shape[0], K), 1) < K // 2, value[:, :K], value[:, K:])


def propagate_kernel(own_ref, tilt_ref, potential_ref, table_ref, factor_ref, across_ref, out_ref):
    table = functools.partial(terms, table_ref)
    real, imag = plane_wave(across_ref, tilt_ref[1, own_ref[0]])
    for layer in range(SLICES - 1):
        real, imag = screened(real, imag, potential_ref, layer)
        real, imag = spectrum(real, imag, table(AHEAD_LEFT), table(AHEAD_RIGHT), factor_ref)
        field = from_right(jnp.concatenate([real, imag], axis=0), table(BACK_RIGHT))
        field = jnp.concatenate(unfold(*halves(field, 0), 1), axis=1)
        real, imag = unfold(*halves(from_left(table(BACK_LEFT), field), 1), 0)
    crop_right = [band_of(term) for term in table(AHEAD_RIGHT)]
    first = (ROWS - K) // 2
    crop_factor = [band_of(factor_ref[i, first : first + K, :]) for i in range(2)]
    real, imag = screened(real, imag, potential_ref, SLICES - 1)
    real, imag = spectrum(real, imag, table(CROP_LEFT), crop_right, crop_factor)
    product = from_right(jnp.concatenate([real, imag], axis=0), table(IMAGE_RIGHT))
    real = product[:K, :K] - product[K:, K:]
    imag = product[:K, K:] + product[K:, :K]
    out_ref[...] = from_left(table(IMAGE_LEFT), jnp.concatenate([real, imag], axis=0))


def probe_kernel(configs, block_ref, coef_ref, mine_ref, other_ref):
    here = block_ref.shape[0] // (2 * K)
    stride = 2 * FAR * here
    field = jnp.concatenate(
        [
            jnp.concatenate(
                [
                    block_ref[pl.ds(2 * (here * x + config) + part, NEAR, stride), :]
                    for part in range(2)
                    for x in range(FAR)
                ],
                axis=0,
            )
            for config in range(here)
        ],
        axis=1,
    )
    real, imag = coef_ref[0], coef_ref[1]
    table = jnp.concatenate(
        [jnp.concatenate([real, -imag], axis=1), jnp.concatenate([imag, real], axis=1)], axis=0
    )
    waves = from_left(split(table), field)
    probes = waves.shape[0] // 2
    real, imag = waves[:probes], waves[probes:]
    power = real * real + imag * imag
    total = sum(power[:, K * config : K * config + K] for config in range(here)) * (1.0 / configs)
    mine_ref[...] = total[: probes // 2]
    other_ref[...] = total[probes // 2 :]


BEAM = ("x", "place")
VMEM = pl.BlockSpec(memory_space=pltpu.VMEM)
SMEM = pl.BlockSpec(memory_space=pltpu.SMEM)
PARAMS = pltpu.CompilerParams(vmem_limit_bytes=24 * 1024 * 1024)


def shape_of(dtype, *shape):
    return jax.ShapeDtypeStruct(shape, dtype)


def prepare(own, slab, tilts, aperture, positions):
    beams = tilts.shape[1]
    out = [
        shape_of(F32, 2, 2 * K, beams),
        shape_of(BF16, TABLE_ROWS, 2 * G),
        shape_of(F32, 2, ROWS, G),
        shape_of(F32, 2, G, K),
    ]
    return pl.pallas_call(
        prepare_kernel,
        out_shape=out,
        in_specs=[SMEM] * 3 + [VMEM] * 3,
        out_specs=[VMEM] * len(out),
        compiler_params=PARAMS,
        name="prepare",
    )(own, slab, tilts, tilts, aperture, positions)


def propagate(*operands):
    return pl.pallas_call(
        propagate_kernel,
        out_shape=shape_of(F32, 2 * K, K),
        in_specs=[SMEM] * 2 + [VMEM] * (len(operands) - 2),
        out_specs=VMEM,
        compiler_params=PARAMS,
        name="propagate",
    )(*operands)


def probe(block, coef, configs):
    quarter = coef.shape[1] // 2
    return pl.pallas_call(
        functools.partial(probe_kernel, configs),
        out_shape=[shape_of(F32, quarter, K)] * 2,
        in_specs=[VMEM] * 2,
        out_specs=[VMEM] * 2,
        compiler_params=PARAMS,
        name="probe",
    )(block, coef)


def copies_of(potential, count):
    return pl.pallas_call(
        copies_kernel,
        out_shape=shape_of(F32, count * SLICES, 4, K),
        in_specs=[VMEM],
        out_specs=VMEM,
        compiler_params=pltpu.CompilerParams(vmem_limit_bytes=60 * 1024 * 1024),
        name="copies",
    )(potential.transpose(1, 0, 2).reshape(SLICES, 4, K))


def per_device(groups, potential, tilts, aperture, positions):
    near, far = groups
    devices = lax.axis_size(BEAM)
    pairs, cores = lax.axis_size("pair"), lax.axis_size("core")
    configs = pairs * cores
    beams = tilts.shape[0]

    part = lax.all_to_all(copies_of(potential, NEAR), BEAM, 0, 0, axis_index_groups=near, tiled=True)

    own = lax.axis_index(BEAM).reshape(1)
    slab = lax.axis_index(("pair", "core")).reshape(1)
    tilts = tilts.T
    coef, *tables = prepare(own, slab, tilts, aperture.reshape(1, beams), positions.T)
    part, coef, *tables = lax.optimization_barrier((part, coef, *tables))
    part = part.reshape(NEAR * PIECE, K)
    whole = lax.all_to_all(
        jnp.broadcast_to(part[None], (FAR, *part.shape)), BEAM, 0, 0, axis_index_groups=far
    ).reshape(devices * PIECE, K)
    image = propagate(own, tilts, whole, *tables)

    rows = jnp.broadcast_to(image.reshape(K, 1, 2, K), (K, pairs, 2, K)).reshape(pairs * K, 2, K)
    block = lax.all_to_all(rows, ("place", "x", "pair"), 0, 0, tiled=True).reshape(2 * pairs * beams, K)
    mine, other = probe(block, coef, configs)
    return mine + lax.ppermute(other, "core", [(0, 1), (1, 0)])


def exchange_groups():
    run, turned = range(NEAR), range(NEAR - 1, -1, -1)
    near = [[NEAR * x + i for i in (run if 2 * x < FAR else turned)] for x in range(FAR)]
    order = [*range(FAR // 2), *range(FAR - 1, FAR // 2 - 1, -1)]
    far = [[NEAR * x + i for x in order] for i in run]
    return near, far


def solution(mesh):
    fine = jax.sharding.Mesh(mesh.devices.reshape(FAR, NEAR, 2, 2), (*BEAM, "pair", "core"))
    return jax.shard_map(
        functools.partial(per_device, exchange_groups()),
        mesh=fine,
        in_specs=(P(("pair", "core"), None, BEAM), P(), P(), P()),
        out_specs=P(("pair", "core"), BEAM),
        check_vma=False,
    )
```

```python
import functools
import math

import jax
import jax.numpy as jnp
from jax import lax
from jax.experimental import pallas as pl
from jax.experimental.pallas import tpu as pltpu
from jax.sharding import PartitionSpec as P

G = 256
K = 128
SLICES = 3
LIMIT = (G // 3) ** 2
REACH = G // 3
ROWS = 176
NEAR, FAR = 32, 4
PIECE = SLICES * 4

FRESNEL_RATE = 0.00019
DEFOCUS_RATE = 0.01

F32 = jnp.float32
BF16 = jnp.bfloat16


def split(value):
    high = value.astype(BF16)
    return high, (value - high.astype(F32)).astype(BF16)


def sine_of(t):
    s = t * t
    sine = jnp.full_like(t, 2.60501958e-6)
    for term in (-1.9808983e-4, 8.33304978e-3, -1.66666579e-1, 0.999999996):
        sine = sine * s + term
    return sine * t


def cosine_of(t):
    s = t * t
    cosine = jnp.full_like(t, 2.31515759e-5)
    for term in (-1.38535979e-3, 4.16635698e-2, -0.499999047, 0.999999953):
        cosine = cosine * s + term
    return cosine


def half_angle(steps, length):
    near = ((steps + length // 2) & (length - 1)) - length // 2
    return near.astype(F32) * (math.pi / length)


def cosine_step(steps, length):
    sine = sine_of(half_angle(steps, length))
    return 1.0 - 2.0 * sine * sine


def circle(steps, length):
    half = half_angle(steps, length)
    sine = sine_of(half)
    return 2.0 * sine * cosine_of(half), 1.0 - 2.0 * sine * sine


def iota(shape, axis):
    return lax.broadcasted_iota(jnp.int32, shape, axis)


def natural(place):
    return place


def mixed(place):
    return 2 * (place & (G // 4 - 1)) + (place >> 6)


def position(place, order):
    n = order(place & (G // 2 - 1))
    return jnp.where(place < G // 2, n, G - 1 - n)


def folded(order, axis):
    place = iota((8, G) if axis else (G, K), axis)
    factor = 2 * order(place & (G // 2 - 1)) + 1
    return factor, jnp.where(place < G // 2, 0, -(G // 2))


def spread(value, shape):
    for axis in range(2):
        times = shape[axis] // value.shape[axis]
        if times > 1:
            value = jnp.concatenate([value] * times, axis=axis)
    return value


def signed(index, length):
    return jnp.where(index < length // 2, index, index - length)


def forward_table(shape, frequency, order, axis):
    factor, offset = (spread(value, shape) for value in folded(order, axis))
    return cosine_step(frequency(iota(shape, 1 - axis)) * factor + offset, 2 * G)


def fresnel(shape, frequency_u, frequency_v):
    u, v = frequency_u(iota(shape, 0)), frequency_v(iota(shape, 1))
    square = u * u + v * v
    angle = jnp.minimum(square, LIMIT).astype(F32) * FRESNEL_RATE
    keep = jnp.where(square <= LIMIT, 1.0 / (G * G), 0.0)
    return cosine_of(angle) * keep, -sine_of(angle) * keep


def copies_kernel(potential_ref, out_ref):
    mirror = jnp.where(iota((K, K), 0) + iota((K, K), 1) == K - 1, 1.0, 0.0)
    rows = jnp.concatenate([potential_ref[layer] for layer in range(SLICES)], axis=0)
    turned = jnp.dot(rows, mirror, precision=lax.Precision.HIGHEST, preferred_element_type=F32)
    rows = jnp.where((iota(rows.shape, 0) & 1) == 1, turned, rows)
    pieces = [rows[4 * layer : 4 * (layer + 1)][None] for layer in range(SLICES)]
    out_ref[...] = jnp.concatenate(pieces * (out_ref.shape[0] // SLICES), axis=0)


AHEAD_LEFT = (0, ROWS, G)
AHEAD_RIGHT = (AHEAD_LEFT[0] + AHEAD_LEFT[1], G, G)
BACK_RIGHT = (AHEAD_RIGHT[0] + G, G, G)
BACK_LEFT = (BACK_RIGHT[0] + G, G, G)
CROP_LEFT = (BACK_LEFT[0] + G, K, G)
IMAGE_RIGHT = (CROP_LEFT[0] + K, K, 2 * K)
IMAGE_LEFT = (IMAGE_RIGHT[0] + K, 2 * K, 2 * K)
TABLE_ROWS = IMAGE_LEFT[0] + IMAGE_LEFT[1]

def terms(ref, where):
    row, rows, columns = where
    return ref[row : row + rows, :columns], ref[row : row + rows, G : G + columns]


def near(index):
    return index - ROWS // 2


def whole(index):
    return signed(index, G)


def centred(index):
    return index - K // 2


def prepare_kernel(
    own_ref, slab_ref, tilt_ref, tilts_ref, aperture_ref, positions_ref, coef_ref, table_ref, factor_ref, across_ref
):
    own = own_ref[0]
    across_ref[0], across_ref[1] = circle(tilt_ref[0, own] * position(iota((G, K), 0), mixed), G)
    factor_ref[0], factor_ref[1] = fresnel((ROWS, G), near, whole)

    tilts = tilts_ref[...]
    beams = tilts.shape[1]
    square = jnp.sum((tilts * tilts).astype(F32), axis=0, keepdims=True)
    angle = -DEFOCUS_RATE * jnp.broadcast_to(square, (8, beams))
    turns = jnp.floor(angle * (0.5 / math.pi) + 0.5)
    half = 0.5 * ((angle - turns * 6.28125) - turns * (2.0 * math.pi - 6.28125))
    sine, cosine = sine_of(half), cosine_of(half)
    amount = jnp.broadcast_to(aperture_ref[...].astype(F32) * (1.0 / math.sqrt(beams)), (8, beams))
    weight_re = spread(amount * (1.0 - 2.0 * sine * sine), (K, beams))
    weight_im = spread(amount * (2.0 * sine * cosine), (K, beams))
    none = jnp.zeros((6, K), F32)
    steep = jnp.concatenate([tilts.astype(F32), none], axis=0).astype(BF16)
    for core in range(2):
        at = pl.multiple_of((slab_ref[0] ^ core) * K, K)
        places = jnp.concatenate([positions_ref[:, pl.ds(at, K)].astype(F32), none], axis=0)
        steps = jnp.dot(places.T.astype(BF16), steep, preferred_element_type=F32)
        sine, cosine = circle(-steps.astype(jnp.int32), K)
        coef_ref[0, K * core : K * (core + 1), :] = cosine * weight_re - sine * weight_im
        coef_ref[1, K * core : K * (core + 1), :] = cosine * weight_im + sine * weight_re

    m, other = iota((2 * K, 2 * K), 0), iota((2 * K, 2 * K), 1)
    turn = (4 * (m >> 1) + 1) * centred(other & (K - 1)) + K * ((other >> 7) - (m & 1))
    left, right = iota((K, 2 * K), 0), iota((K, 2 * K), 1)
    for (row, rows, columns), table in (
        (AHEAD_LEFT, forward_table((ROWS, G), near, mixed, 1)),
        (AHEAD_RIGHT, forward_table((G, G), whole, natural, 0)),
        (BACK_RIGHT, forward_table((G, G), whole, natural, 1)),
        (BACK_LEFT, forward_table((G, G), near, mixed, 0)),
        (CROP_LEFT, forward_table((K, G), centred, mixed, 1)),
        (IMAGE_RIGHT, cosine_step(signed(left, K) * (4 * (right & (K - 1)) + 1) - K * (right >> 7), 2 * G)),
        (IMAGE_LEFT, cosine_step(turn, 2 * G)),
    ):
        high, low = split(table)
        table_ref[row : row + rows, :columns] = high
        table_ref[row : row + rows, G : G + columns] = low


def from_left(table, field):
    high, low = split(field)
    short = table[0].shape[1] - field.shape[0]
    if short:
        none = jnp.zeros((short, field.shape[1]), BF16)
        high, low = jnp.concatenate([high, none], axis=0), jnp.concatenate([low, none], axis=0)
    return jnp.dot(
        jnp.concatenate([table[0], table[0], table[1]], axis=1),
        jnp.concatenate([high, low, high], axis=0),
        preferred_element_type=F32,
    )


def from_right(field, table):
    table = jnp.concatenate([table[0], table[0], table[1]], axis=0)

    def product(rows):
        high, low = split(rows)
        return jnp.dot(jnp.concatenate([high, low, high], axis=1), table, preferred_element_type=F32)

    return jnp.concatenate([product(rows) for rows in halves(field, 0)], axis=0)


def halves(value, axis):
    half = value.shape[axis] // 2
    return lax.slice_in_dim(value, 0, half, axis=axis), lax.slice_in_dim(value, half, 2 * half, axis=axis)


def fold(real, imag, axis):
    real_ahead, real_back = halves(real, axis)
    imag_ahead, imag_back = halves(imag, axis)
    return (
        jnp.concatenate([real_ahead + real_back, imag_ahead - imag_back], axis=axis),
        jnp.concatenate([imag_ahead + imag_back, real_back - real_ahead], axis=axis),
    )


def unfold(real, imag, axis):
    real_even, real_odd = halves(real, axis)
    imag_even, imag_odd = halves(imag, axis)
    return (
        jnp.concatenate([real_even - imag_odd, real_even + imag_odd], axis=axis),
        jnp.concatenate([imag_even + real_odd, imag_even - real_odd], axis=axis),
    )


def spectrum(real, imag, left, right, factor):
    field = from_left(left, jnp.concatenate(fold(real, imag, 0), axis=1))
    field = jnp.concatenate(fold(*halves(field, 1), 1), axis=0)
    real, imag = halves(from_right(field, right), 0)
    return (
        real * factor[0] - imag * factor[1],
        real * factor[1] + imag * factor[0],
    )


def screened(real, imag, potential_ref, layer):
    count = G // 4

    def rows(half, parity, side):
        own = 4 * layer + 2 * (1 - parity if half else parity) + side
        return potential_ref[pl.ds(PIECE * count * half + own, count, PIECE), :]

    potential = jnp.concatenate(
        [
            jnp.concatenate([rows(half, parity, side) for side in range(2)], axis=1)
            for half in range(2)
            for parity in range(2)
        ],
        axis=0,
    )
    turned = potential - math.pi / 2
    sine, cosine = cosine_of(turned), sine_of(turned)
    return -(real * cosine + imag * sine), real * sine - imag * cosine


def plane_wave(across_ref, tilt_y):
    sine_x, cosine_x = (jnp.concatenate([across_ref[i]] * (G // K), axis=1) for i in range(2))
    sine_y, cosine_y = circle(tilt_y * position(iota((8, G), 1), natural), G)
    sine_y, cosine_y = (jnp.concatenate([value] * (G // 8), axis=0) for value in (sine_y, cosine_y))
    return cosine_x * cosine_y - sine_x * sine_y, sine_x * cosine_y + cosine_x * sine_y


def band_of(value):
    return jnp.where(iota((value.shape[0], K), 1) < K // 2, value[:, :K], value[:, K:])


def propagate_kernel(own_ref, tilt_ref, potential_ref, table_ref, factor_ref, across_ref, out_ref):
    table = functools.partial(terms, table_ref)
    real, imag = plane_wave(across_ref, tilt_ref[1, own_ref[0]])
    for layer in range(SLICES - 1):
        real, imag = screened(real, imag, potential_ref, layer)
        real, imag = spectrum(real, imag, table(AHEAD_LEFT), table(AHEAD_RIGHT), factor_ref)
        field = from_right(jnp.concatenate([real, imag], axis=0), table(BACK_RIGHT))
        field = jnp.concatenate(unfold(*halves(field, 0), 1), axis=1)
        real, imag = unfold(*halves(from_left(table(BACK_LEFT), field), 1), 0)
    crop_right = [band_of(term) for term in table(AHEAD_RIGHT)]
    first = (ROWS - K) // 2
    crop_factor = [band_of(factor_ref[i, first : first + K, :]) for i in range(2)]
    real, imag = screened(real, imag, potential_ref, SLICES - 1)
    real, imag = spectrum(real, imag, table(CROP_LEFT), crop_right, crop_factor)
    product = from_right(jnp.concatenate([real, imag], axis=0), table(IMAGE_RIGHT))
    real = product[:K, :K] - product[K:, K:]
    imag = product[:K, K:] + product[K:, :K]
    out_ref[...] = from_left(table(IMAGE_LEFT), jnp.concatenate([real, imag], axis=0))


def probe_kernel(configs, block_ref, coef_ref, mine_ref, other_ref):
    here = block_ref.shape[0] // (2 * K)
    field = jnp.concatenate(
        [
            jnp.concatenate(
                [block_ref[pl.ds(2 * config + part, K, 2 * here), :] for part in range(2)], axis=0
            )
            for config in range(here)
        ],
        axis=1,
    )
    real, imag = coef_ref[0], coef_ref[1]
    table = jnp.concatenate(
        [jnp.concatenate([real, -imag], axis=1), jnp.concatenate([imag, real], axis=1)], axis=0
    )
    waves = from_left(split(table), field)
    probes = waves.shape[0] // 2
    real, imag = waves[:probes], waves[probes:]
    power = real * real + imag * imag
    total = sum(power[:, K * config : K * config + K] for config in range(here)) * (1.0 / configs)
    mine_ref[...] = total[: probes // 2]
    other_ref[...] = total[probes // 2 :]


VMEM = pl.BlockSpec(memory_space=pltpu.VMEM)
SMEM = pl.BlockSpec(memory_space=pltpu.SMEM)
PARAMS = pltpu.CompilerParams(vmem_limit_bytes=24 * 1024 * 1024)


def shape_of(dtype, *shape):
    return jax.ShapeDtypeStruct(shape, dtype)


def prepare(own, slab, tilts, aperture, positions):
    beams = tilts.shape[1]
    out = [
        shape_of(F32, 2, 2 * K, beams),
        shape_of(BF16, TABLE_ROWS, 2 * G),
        shape_of(F32, 2, ROWS, G),
        shape_of(F32, 2, G, K),
    ]
    return pl.pallas_call(
        prepare_kernel,
        out_shape=out,
        in_specs=[SMEM] * 3 + [VMEM] * 3,
        out_specs=[VMEM] * len(out),
        compiler_params=PARAMS,
        name="prepare",
    )(own, slab, tilts, tilts, aperture, positions)


def propagate(*operands):
    return pl.pallas_call(
        propagate_kernel,
        out_shape=shape_of(F32, 2 * K, K),
        in_specs=[SMEM] * 2 + [VMEM] * (len(operands) - 2),
        out_specs=VMEM,
        compiler_params=PARAMS,
        name="propagate",
    )(*operands)


def probe(block, coef, configs):
    quarter = coef.shape[1] // 2
    return pl.pallas_call(
        functools.partial(probe_kernel, configs),
        out_shape=[shape_of(F32, quarter, K)] * 2,
        in_specs=[VMEM] * 2,
        out_specs=[VMEM] * 2,
        compiler_params=PARAMS,
        name="probe",
    )(block, coef)


def copies_of(potential, count):
    return pl.pallas_call(
        copies_kernel,
        out_shape=shape_of(F32, count * SLICES, 4, K),
        in_specs=[VMEM],
        out_specs=VMEM,
        compiler_params=pltpu.CompilerParams(vmem_limit_bytes=60 * 1024 * 1024),
        name="copies",
    )(potential.transpose(1, 0, 2).reshape(SLICES, 4, K))


def per_device(groups, potential, tilts, aperture, positions):
    near, far = groups
    devices = lax.axis_size("beam")
    pairs, cores = lax.axis_size("pair"), lax.axis_size("core")
    configs = pairs * cores
    beams = tilts.shape[0]

    part = lax.all_to_all(copies_of(potential, NEAR), "beam", 0, 0, axis_index_groups=near, tiled=True)

    own = lax.axis_index("beam").reshape(1)
    slab = lax.axis_index(("pair", "core")).reshape(1)
    tilts = tilts.T
    coef, *tables = prepare(own, slab, tilts, aperture.reshape(1, beams), positions.T)
    part, coef, *tables = lax.optimization_barrier((part, coef, *tables))
    part = part.reshape(NEAR * PIECE, K)
    whole = lax.all_to_all(
        jnp.broadcast_to(part[None], (FAR, *part.shape)), "beam", 0, 0, axis_index_groups=far
    ).reshape(devices * PIECE, K)
    image = propagate(own, tilts, whole, *tables)

    rows = jnp.broadcast_to(image.reshape(K, 1, 2, K), (K, pairs, 2, K)).reshape(pairs * K, 2, K)
    block = lax.all_to_all(rows, ("beam", "pair"), 0, 0, tiled=True).reshape(2 * pairs * beams, K)
    mine, other = probe(block, coef, configs)
    return mine + lax.ppermute(other, "core", [(0, 1), (1, 0)])


def exchange_groups():
    run, turned = range(NEAR), range(NEAR - 1, -1, -1)
    near = [[NEAR * x + i for i in (run if 2 * x < FAR else turned)] for x in range(FAR)]
    order = [*range(FAR // 2), *range(FAR - 1, FAR // 2 - 1, -1)]
    far = [[NEAR * x + i for x in order] for i in run]
    return near, far


def solution(mesh):
    fine = jax.sharding.Mesh(mesh.devices.reshape(-1, 2, 2), ("beam", "pair", "core"))
    return jax.shard_map(
        functools.partial(per_device, exchange_groups()),
        mesh=fine,
        in_specs=(P(("pair", "core"), None, "beam"), P(), P(), P()),
        out_specs=P(("pair", "core"), "beam"),
        check_vma=False,
    )
```
